128 devices in a mesh: learner: 32 (over z_hi, y, x), tensor: 4 (over z_lo, core).
Axes of the slice: x: 4, y: 4, z: 4 (z_hi: 2, z_lo: 2; z = z_hi * 2 + z_lo), core: 2. Of those that a mesh axis runs over, the one named last changes fastest.
Arguments:
- inputs: bfloat16 [2, 256, 8192], P(None, 'learner', 'tensor'), may hold values from -6 to 6
- frozen_gate_weight: bfloat16 [28672, 8192], P(('learner', 'tensor')), may hold values from -0.0625 to 0.0625
- frozen_up_weight: bfloat16 [28672, 8192], P(('learner', 'tensor')), may hold values from -0.0625 to 0.0625
- frozen_down_weight: bfloat16 [28672, 8192], P(('learner', 'tensor')), may hold values from -0.125 to 0.125
- adapter_first_gate: bfloat16 [64, 8192], P(None, 'learner'), may hold values from -0.0625 to 0.0625
- adapter_second_gate: bfloat16 [28672, 64], P(('learner', 'tensor')), may hold values from -0.75 to 0.75
- adapter_first_up: bfloat16 [64, 8192], P(None, 'learner'), may hold values from -0.0625 to 0.0625
- adapter_second_up: bfloat16 [28672, 64], P(('learner', 'tensor')), may hold values from -0.75 to 0.75
- adapter_first_down: bfloat16 [28672, 64], P(('learner', 'tensor')), may hold values from -0.03125 to 0.03125
- adapter_second_down: bfloat16 [64, 8192], P(None, 'learner'), may hold values from -0.75 to 0.75
Outputs:
- outputs: bfloat16 [2, 256, 8192], P(None, 'learner', 'tensor')
The draws below stay inside these ranges and needn't reach their ends.
All inputs are finite; a program needn't handle non-finite values.
Results may differ from the reference program's by a relative error of at most 0.0071.
Values may be sent and summed in bfloat16 or wider, within the bound.
No kernel may reach another device: no remote copies, remote signals or barrier semaphores. Data moves between devices by JAX's collectives and lax.ppermute only.
A program may use at most 128 MiB of HBM per device.

```python
import jax
import jax.numpy as jnp
from jax import lax

MODEL_WIDTH = 8192
HIDDEN_UNITS = 28672
ADAPTER_RANK = 64
STEPS = 2
ROWS_ALL = 256
N_LEARNER = 32
N_TENSOR = 4


def raised(result, own_key, source, target, shards_of, factor):
    owner, partner = [(jnp.arange(result.shape[dim]) // (result.shape[dim] // shards_of)).reshape([-1 if axis == dim else 1 for axis in range(result.ndim)]) for dim in (source, target)]
    chosen = jax.random.permutation(own_key, shards_of)[partner]
    strong = (owner == chosen) | (owner == (partner + shards_of // 2) % shards_of)
    return jnp.where(strong, factor * result, result)


def levels(stream_key, shape, cuts, low, top_value):
    gain, own = 1.0, jax.random.fold_in(stream_key, 6)
    for dim, blocks in cuts:
        heights = jnp.exp(jax.random.uniform(jax.random.fold_in(own, dim), (blocks,), jnp.float32, low / len(cuts), top_value / len(cuts)))
        gain = gain * jnp.repeat(heights, shape[dim] // blocks).reshape([-1 if axis == dim else 1 for axis in range(len(shape))])
    return gain


def bell_draw(own_key, extent, spread, most, shards=(), kind=jnp.bfloat16):
    result = spread * jax.random.normal(own_key, extent, jnp.float32)
    if shards:
        result = result * levels(own_key, extent, shards, -0.22, 0.18)
    return jnp.clip(result, -most, most).astype(kind)


def gaussian_with(stream_key, shape, width, limit, cuts, heavy, dtype=jnp.bfloat16):
    array = width * jax.random.normal(stream_key, shape, jnp.float32)
    if cuts:
        array = array * levels(stream_key, shape, cuts, -0.22, 0.18)
    return jnp.clip(raised(array, jax.random.fold_in(stream_key, 3), *heavy), -limit, limit).astype(dtype)


def setup_inputs(seed: int = 0) -> dict:
    keys = jax.random.split(jax.random.key(seed), 11)
    return {
        "inputs": bell_draw(keys[0], (STEPS, ROWS_ALL, MODEL_WIDTH), 1.0, 6.0, ((1, 32), (2, 4))),
        "frozen_gate_weight": bell_draw(keys[1], (HIDDEN_UNITS, MODEL_WIDTH), MODEL_WIDTH ** -0.5, 0.0625, ((0, 128),)),
        "frozen_up_weight": bell_draw(keys[2], (HIDDEN_UNITS, MODEL_WIDTH), MODEL_WIDTH ** -0.5, 0.0625, ((0, 128),)),
        "frozen_down_weight": gaussian_with(keys[3], (HIDDEN_UNITS, MODEL_WIDTH), HIDDEN_UNITS ** -0.5, 0.125, ((0, 128),), (0, 1, 128, 5.5)),
        "adapter_first_gate": bell_draw(keys[4], (ADAPTER_RANK, MODEL_WIDTH), MODEL_WIDTH ** -0.5, 0.0625, ((1, 32),)),
        "adapter_second_gate": bell_draw(keys[5], (HIDDEN_UNITS, ADAPTER_RANK), ADAPTER_RANK ** -0.5, 0.75, ((0, 128),)),
        "adapter_first_up": bell_draw(keys[6], (ADAPTER_RANK, MODEL_WIDTH), MODEL_WIDTH ** -0.5, 0.0625, ((1, 32),)),
        "adapter_second_up": bell_draw(keys[7], (HIDDEN_UNITS, ADAPTER_RANK), ADAPTER_RANK ** -0.5, 0.75, ((0, 128),)),
        "adapter_first_down": bell_draw(keys[8], (HIDDEN_UNITS, ADAPTER_RANK), HIDDEN_UNITS ** -0.5, 0.03125, ((0, 128),)),
        "adapter_second_down": bell_draw(keys[9], (ADAPTER_RANK, MODEL_WIDTH), ADAPTER_RANK ** -0.5, 0.75, ((1, 32),)),
    }


adapter_scale = 0.5


def merge_adapter_weight(frozen_matrix, left, right):
    low_rank_update = jnp.dot(left, right, preferred_element_type=jnp.float32)
    return (frozen_matrix.astype(jnp.float32) + adapter_scale * low_rank_update).astype(jnp.bfloat16)


def project_rows(rows, weight):
    return lax.dot_general(rows, weight, (((1,), (1,)), ((), ())), preferred_element_type=jnp.float32)


def reference(inputs, frozen_gate_weight, frozen_up_weight, frozen_down_weight, adapter_first_gate, adapter_second_gate, adapter_first_up, adapter_second_up, adapter_first_down, adapter_second_down):
    weight_blocks = N_LEARNER * N_TENSOR
    feature_width = HIDDEN_UNITS // weight_blocks
    flat_rows = inputs.reshape(STEPS * ROWS_ALL, MODEL_WIDTH)
    gate_blocks = frozen_gate_weight.reshape(weight_blocks, feature_width, MODEL_WIDTH)
    up_blocks = frozen_up_weight.reshape(weight_blocks, feature_width, MODEL_WIDTH)
    gate_adapter_factor = adapter_second_gate.reshape(weight_blocks, feature_width, ADAPTER_RANK)
    up_adapter_factor = adapter_second_up.reshape(weight_blocks, feature_width, ADAPTER_RANK)
    down_blocks = frozen_down_weight.reshape(weight_blocks, feature_width, MODEL_WIDTH)
    down_adapter_factor = adapter_first_down.reshape(weight_blocks, feature_width, ADAPTER_RANK)

    def one_block(total, pieces):
        gate_frozen_part, gate_left_factor, up_frozen_part, up_left_factor, down_frozen_part, down_left_factor = pieces
        combined_gate_weight = merge_adapter_weight(gate_frozen_part, gate_left_factor, adapter_first_gate)
        combined_up_weight = merge_adapter_weight(up_frozen_part, up_left_factor, adapter_first_up)
        combined_down_weight = merge_adapter_weight(down_frozen_part, down_left_factor, adapter_second_down)
        gate = project_rows(flat_rows, combined_gate_weight)
        upper = project_rows(flat_rows, combined_up_weight)
        hidden = (jax.nn.silu(gate) * upper).astype(jnp.bfloat16)
        return total + jnp.dot(hidden, combined_down_weight, preferred_element_type=jnp.float32), None

    start_total = jnp.zeros((STEPS * ROWS_ALL, MODEL_WIDTH), jnp.float32)
    total, _ = lax.scan(one_block, start_total, (gate_blocks, gate_adapter_factor, up_blocks, up_adapter_factor, down_blocks, down_adapter_factor))
    return total.astype(jnp.bfloat16).reshape(STEPS, ROWS_ALL, MODEL_WIDTH)
```

```python
import itertools

import jax
import jax.numpy as jnp
from jax import lax
from jax.experimental import pallas as pl
from jax.experimental.pallas import tpu as pltpu
from jax.sharding import Mesh, PartitionSpec as P

AXES = ("zh", "y", "x", "zl", "c")
SIZES = (2, 4, 4, 2, 2)
adapter_scale = 0.5
WIDTH = 8192
UNITS = 224
TILE = 1024
STEPS = WIDTH // TILE
PARTS = TILE // 256
f32, bf16 = jnp.float32, jnp.bfloat16


def index(zh, y, x, zl, c):
    return (((zh * 4 + y) * 4 + x) * 2 + zl) * 2 + c


def pairs(partner):
    out = []
    for zh, y, x, zl, c in itertools.product(*map(range, SIZES)):
        z, y2, x2, c2 = partner(zh * 2 + zl, y, x, c)
        out.append((index(zh, y, x, zl, c), index(z >> 1, y2, x2, z & 1, c2)))
    return out


CORE = pairs(lambda z, y, x, c: (z, y, x, 1 - c))
ALONG_Z = {k: pairs(lambda z, y, x, c: (z ^ k, y, x, c)) for k in (1, 2, 3)}
FIRST = {
    k: pairs(lambda z, y, x, c: (z, y ^ k, x, c) if c else (z, y, x ^ k, c))
    for k in (1, 2, 3)
}
SECOND = {
    k: pairs(lambda z, y, x, c: (z, y, x ^ k, c) if c else (z, y ^ k, x, c))
    for k in (1, 2, 3)
}


def send(value, route):
    return lax.ppermute(value, AXES, route)


def nt(a, b):
    return lax.dot_general(a, b, (((1,), (1,)), ((), ())), preferred_element_type=f32)


def nn(a, b):
    return jnp.dot(a, b, preferred_element_type=f32)


def ffn_kernel(n, sends, place, *refs):
    rows = refs[:n]
    gate_w, gate_w2, up_w, up_w2, down_w, down_w2 = refs[n : n + 6]
    factors = refs[n + 6 : n + 6 + 2 * PARTS]
    second_gate, second_up, first_down = refs[n + 6 + 2 * PARTS : n + 9 + 2 * PARTS]
    outs = refs[n + 9 + 2 * PARTS : 2 * n + 9 + 2 * PARTS]
    gate, up, low, hidden, low_down, first, second = refs[2 * n + 9 + 2 * PARTS :]
    step = pl.program_id(0)
    mine, theirs = slice(0, UNITS), slice(UNITS, 2 * UNITS)

    @pl.when(step == 0)
    def _():
        gate[...] = jnp.zeros_like(gate)
        up[...] = jnp.zeros_like(up)
        low[...] = jnp.zeros_like(low)

    @pl.when(step < STEPS)
    def _():
        for j in range(PARTS):
            cols = slice(j * 256, (j + 1) * 256)
            first[0:64, cols] = factors[j][0:64, :]
            first[64:128, cols] = factors[PARTS + j][0:64, :]
        x = jnp.concatenate([r[...] for r in rows], axis=0)
        gate[0] += nt(x, gate_w[...])
        gate[1] += nt(x, gate_w2[...])
        up[0] += nt(x, up_w[...])
        up[1] += nt(x, up_w2[...])
        low[...] += nt(x, first[...])

    @pl.when(step == STEPS - 1)
    def _():
        u = (adapter_scale * low[...]).astype(bf16)
        total = None
        for half, part in ((0, mine), (1, theirs)):
            g = gate[half] + nt(u, second_gate[part, :])
            v = up[half] + nt(u, second_up[part, :])
            h = (g / (1.0 + jnp.exp(-g)) * v).astype(bf16)
            hidden[half] = h
            term = nn(h, first_down[part, :])
            total = term if total is None else total + term
        low_down[...] = (adapter_scale * total).astype(bf16)

    @pl.when(step >= STEPS)
    def _():
        for j in range(PARTS):
            cols = slice(j * 256, (j + 1) * 256)
            second[0:32, cols] = factors[j][64:96, :]
            second[32:64, cols] = factors[PARTS + j][64:96, :]
        result = nn(hidden[0], down_w[...])
        result += nn(hidden[1], down_w2[...])
        result += nn(low_down[...], second[...])
        for i, out in enumerate(outs):
            out[...] = result[i * 64 : (i + 1) * 64].astype(out.dtype)


def ffn(place, rows, weights, factor, factor2, seconds, kinds):
    n = len(rows)
    m = 64 * n

    def early(i, place):
        return (0, jnp.minimum(i, STEPS - 1))

    def late(i, place):
        return (0, jnp.maximum(i - STEPS, 0))

    def shard(other, j):
        def block(i, place):
            learner = lax.rem(i, STEPS) * PARTS + j
            zh, y, x = learner // 16, (learner // 4) % 4, learner % 4
            dz, dy, dx = zh ^ place[0], y ^ place[1], x ^ place[2]
            along_x = (place[3] ^ other) == 0
            near = jnp.where(along_x, dx, dy)
            far = jnp.where(along_x, dy, dx)
            return (far * 4 + near, dz)

        return pl.BlockSpec((96, 256), block)

    whole = lambda a: pl.BlockSpec(a.shape, lambda i, place: (0, 0))
    in_specs = (
        [pl.BlockSpec((64, TILE), early)] * n
        + [pl.BlockSpec((UNITS, TILE), early)] * 4
        + [pl.BlockSpec((UNITS, TILE), late)] * 2
        + [shard(0, j) for j in range(PARTS)]
        + [shard(1, j) for j in range(PARTS)]
        + [whole(a) for a in seconds]
    )
    flops = 2 * m * WIDTH * (6 * UNITS + 192)
    traffic = 2 * WIDTH * (6 * UNITS + 192 + 2 * m)
    return pl.pallas_call(
        lambda *refs: ffn_kernel(n, kinds, *refs),
        grid_spec=pltpu.PrefetchScalarGridSpec(
            num_scalar_prefetch=1,
            grid=(2 * STEPS,),
            in_specs=in_specs,
            out_specs=[pl.BlockSpec((64, TILE), late)] * n,
            scratch_shapes=[
                pltpu.VMEM((2, m, UNITS), f32),
                pltpu.VMEM((2, m, UNITS), f32),
                pltpu.VMEM((m, 128), f32),
                pltpu.VMEM((2, m, UNITS), bf16),
                pltpu.VMEM((m, 64), bf16),
                pltpu.VMEM((128, TILE), bf16),
                pltpu.VMEM((64, TILE), bf16),
            ],
        ),
        out_shape=[jax.ShapeDtypeStruct((64, WIDTH), kind) for kind in kinds],
        compiler_params=pltpu.CompilerParams(vmem_limit_bytes=40 * 1024 * 1024),
        cost_estimate=pl.CostEstimate(
            flops=flops, bytes_accessed=traffic, transcendentals=m * 2 * UNITS
        ),
    )(place, *rows, *weights, *([factor] * PARTS), *([factor2] * PARTS), *seconds)


def shards(
    inputs,
    frozen_gate_weight,
    frozen_up_weight,
    frozen_down_weight,
    adapter_first_gate,
    adapter_second_gate,
    adapter_first_up,
    adapter_second_up,
    adapter_first_down,
    adapter_second_down,
):
    zh, y, x, zl, c = (lax.axis_index(a) for a in AXES)
    place = jnp.stack([zh, y, x, c]).astype(jnp.int32)

    def ordered(flag, a, b, axis):
        return jnp.where(
            flag == 0, jnp.concatenate([a, b], axis), jnp.concatenate([b, a], axis)
        )

    own = jnp.where(c == 0, inputs[0], inputs[1])
    other = jnp.where(c == 0, inputs[1], inputs[0])
    wide = ordered(c, own, send(other, CORE), 1)
    from_z = {k: send(wide, ALONG_Z[k]) for k in (1, 2, 3)}
    block = jnp.concatenate(
        [ordered(zl, wide, from_z[1], 1), ordered(zl, from_z[2], from_z[3], 1)], 0
    )
    block = jnp.concatenate([block] + [send(block, FIRST[k]) for k in (1, 2, 3)], 0)
    rows = [block] + [send(block, SECOND[k]) for k in (1, 2, 3)]

    ranks = jnp.stack([adapter_first_gate, adapter_first_up, adapter_second_down])
    half = jnp.where(c == 0, ranks[:, :32], ranks[:, 32:]).reshape(96, 256)
    factor = jnp.concatenate([half, send(half, ALONG_Z[3])], 1)
    factor = jnp.concatenate([factor] + [send(factor, FIRST[k]) for k in (1, 2, 3)], 0)
    factor = jnp.concatenate([factor] + [send(factor, SECOND[k]) for k in (1, 2, 3)], 0)
    factor2 = send(factor, CORE)

    weights = []
    for w in (frozen_gate_weight, frozen_up_weight, frozen_down_weight):
        weights += [w, send(w, CORE)]
    seconds = jnp.concatenate(
        [adapter_second_gate, adapter_second_up, adapter_first_down], 1
    )
    seconds = jnp.concatenate([seconds, send(seconds, CORE)], 0)
    gate_b, up_b, down_b = (
        ordered(c, s[:, :32], s[:, 32:], 1)
        for s in (seconds[:, :64], seconds[:, 64:128], seconds[:, 128:])
    )
    blank = jnp.zeros((2 * UNITS, 32), bf16)
    gate_b = jnp.concatenate([gate_b[:, :32], blank, gate_b[:, 32:], blank], 1)
    up_b = jnp.concatenate([blank, up_b[:, :32], blank, up_b[:, 32:]], 1)

    parts = ffn(
        place, rows, weights, factor, factor2, (gate_b, up_b, down_b),
        (f32, bf16, bf16, bf16),
    )

    def widen(a):
        return a.astype(f32)

    total = parts[0]
    for k in (1, 2, 3):
        total = total + widen(send(parts[k], SECOND[k]))
    mine = total[:16]
    for k in (1, 2, 3):
        back = send(total[16 * k : 16 * (k + 1)].astype(bf16), FIRST[k])
        mine = mine + widen(back)
    lower, upper = mine[:, : WIDTH // 2], mine[:, WIDTH // 2 :]
    near = jnp.where(zl == 0, lower, upper)
    away = jnp.where(zl == 0, upper, lower)
    done = near[:8]
    for k, piece in ((1, away[:8]), (2, near[8:]), (3, away[8:])):
        done = done + widen(send(piece.astype(bf16), ALONG_Z[k]))
    done = done.astype(bf16)
    keep = jnp.where(c == 0, done[:, :2048], done[:, 2048:])
    give = jnp.where(c == 0, done[:, 2048:], done[:, :2048])
    got = send(give, CORE)
    return ordered(c, keep[None], got[None], 0)


def solution(mesh):
    fine = Mesh(mesh.devices.reshape(SIZES), AXES)
    learner, tensor = ("zh", "y", "x"), ("zl", "c")
    in_specs = (
        P(None, learner, tensor),
        P(AXES, None),
        P(AXES, None),
        P(AXES, None),
        P(None, learner),
        P(AXES, None),
        P(None, learner),
        P(AXES, None),
        P(AXES, None),
        P(None, learner),
    )
    return jax.shard_map(
        shards,
        mesh=fine,
        in_specs=in_specs,
        out_specs=P(None, learner, tensor),
        check_vma=False,
    )
```

```python
import itertools

import jax
import jax.numpy as jnp
from jax import lax
from jax.experimental import pallas as pl
from jax.experimental.pallas import tpu as pltpu
from jax.sharding import Mesh, PartitionSpec as P

AXES = ("zh", "y", "x", "zl", "c")
SIZES = (2, 4, 4, 2, 2)
adapter_scale = 0.5
WIDTH = 8192
HALF = WIDTH // 2
UNITS = 224
TILE = 2048
STEPS = WIDTH // TILE
PARTS = TILE // 256
f32, bf16 = jnp.float32, jnp.bfloat16


def index(zh, y, x, zl, c):
    return (((zh * 4 + y) * 4 + x) * 2 + zl) * 2 + c


def pairs(partner):
    out = []
    for zh, y, x, zl, c in itertools.product(*map(range, SIZES)):
        z, y2, x2, c2 = partner(zh * 2 + zl, y, x, c)
        out.append((index(zh, y, x, zl, c), index(z >> 1, y2, x2, z & 1, c2)))
    return out


CORE = pairs(lambda z, y, x, c: (z, y, x, 1 - c))
ALONG_Z = {k: pairs(lambda z, y, x, c: (z ^ k, y, x, c)) for k in (1, 2, 3)}
FIRST = {
    k: pairs(lambda z, y, x, c: (z, y ^ k, x, c) if c else (z, y, x ^ k, c))
    for k in (1, 2, 3)
}
SECOND = {
    k: pairs(lambda z, y, x, c: (z, y, x ^ k, c) if c else (z, y ^ k, x, c))
    for k in (1, 2, 3)
}


def send(value, route):
    return lax.ppermute(value, AXES, route)


def nt(a, b):
    return lax.dot_general(a, b, (((1,), (1,)), ((), ())), preferred_element_type=f32)


def nn(a, b):
    return jnp.dot(a, b, preferred_element_type=f32)


def widen(a):
    return a.astype(f32)


def after(value, others):
    return lax.optimization_barrier((value, others))[0]


def ffn_kernel(n, place, *refs):
    rows = refs[:n]
    gate_w, gate_w2, up_w, up_w2, down_w, down_w2 = refs[n : n + 6]
    factor, factor2, second_gate, second_up, first_down = refs[n + 6 : n + 11]
    outs = refs[n + 11 : 2 * n + 11]
    gate, up, low, first, second = refs[2 * n + 11 :]
    mine, theirs = slice(0, UNITS), slice(UNITS, 2 * UNITS)
    gate[...] = jnp.zeros_like(gate)
    up[...] = jnp.zeros_like(up)
    low[...] = jnp.zeros_like(low)

    def block(i, j, other):
        learner = i * PARTS + j
        zh, y, x = learner // 16, (learner // 4) % 4, learner % 4
        dz, dy, dx = zh ^ place[0], y ^ place[1], x ^ place[2]
        along_x = (place[3] ^ other) == 0
        near = jnp.where(along_x, dx, dy)
        far = jnp.where(along_x, dy, dx)
        return pl.ds(pl.multiple_of((far * 4 + near) * 16, 16), 16), dz * 256

    @pl.loop(0, STEPS)
    def _(i):
        tile = pl.ds(pl.multiple_of(i * TILE, TILE), TILE)
        for j in range(PARTS):
            cols = slice(j * 256, (j + 1) * 256)
            for o, src in ((0, factor), (1, factor2)):
                r, q = block(i, j, o)
                for k in range(4):
                    piece = src[r, pl.ds(pl.multiple_of(k * 512 + q, 256), 256)]
                    first[o * 64 + k * 16 : o * 64 + k * 16 + 16, cols] = piece
        x = jnp.concatenate([r[:, tile] for r in rows], axis=0)
        gate[0] += nt(gate_w[:, tile], x)
        gate[1] += nt(gate_w2[:, tile], x)
        up[0] += nt(up_w[:, tile], x)
        up[1] += nt(up_w2[:, tile], x)
        low[...] += nt(first[...], x)

    u = (adapter_scale * low[...]).astype(bf16)
    hidden, total = [], None
    for half, part in ((0, mine), (1, theirs)):
        g = gate[half] + nn(second_gate[part, :], u)
        v = up[half] + nn(second_up[part, :], u)
        hidden.append((g / (1.0 + jnp.exp(-g)) * v).T.astype(bf16))
        term = nn(hidden[half], first_down[part, :])
        total = term if total is None else total + term
    low_down = (adapter_scale * total).astype(bf16)

    @pl.loop(0, STEPS)
    def _(i):
        tile = pl.ds(pl.multiple_of(i * TILE, TILE), TILE)
        for j in range(PARTS):
            cols = slice(j * 256, (j + 1) * 256)
            for o, src in ((0, factor), (1, factor2)):
                r, q = block(i, j, o)
                for k in range(2):
                    piece = src[r, pl.ds(pl.multiple_of(2048 + k * 512 + q, 256), 256)]
                    second[o * 32 + k * 16 : o * 32 + k * 16 + 16, cols] = piece
        result = nn(hidden[0], down_w[:, tile])
        result += nn(hidden[1], down_w2[:, tile])
        result += nn(low_down, second[...])
        for k, out in enumerate(outs):
            out[:, tile] = result[k * 64 : (k + 1) * 64].astype(out.dtype)


def ffn(place, rows, weights, factor, factor2, seconds, kinds):
    n = len(rows)
    m = 64 * n
    flops = 2 * m * WIDTH * (6 * UNITS + 192)
    traffic = 2 * WIDTH * (6 * UNITS + 192 + 2 * m)
    operands = [*rows, *weights, factor, factor2, *seconds]
    operands = [pltpu.with_memory_space_constraint(a, pltpu.VMEM) for a in operands]
    vmem = pl.BlockSpec(memory_space=pltpu.VMEM)
    return pl.pallas_call(
        lambda *refs: ffn_kernel(n, *refs),
        in_specs=[pl.BlockSpec(memory_space=pltpu.SMEM)] + [vmem] * len(operands),
        out_specs=[vmem] * n,
        out_shape=[jax.ShapeDtypeStruct((64, WIDTH), kind) for kind in kinds],
        scratch_shapes=[
            pltpu.VMEM((2, UNITS, m), f32),
            pltpu.VMEM((2, UNITS, m), f32),
            pltpu.VMEM((128, m), f32),
            pltpu.VMEM((128, TILE), bf16),
            pltpu.VMEM((64, TILE), bf16),
        ],
        compiler_params=pltpu.CompilerParams(vmem_limit_bytes=14 * 1024 * 1024),
        cost_estimate=pl.CostEstimate(
            flops=flops, bytes_accessed=traffic, transcendentals=m * 2 * UNITS
        ),
    )(place, *operands)


def local(body, shapes, operands, place=None):
    vmem = pl.BlockSpec(memory_space=pltpu.VMEM)
    lead = [] if place is None else [place]
    return pl.pallas_call(
        body,
        in_specs=[pl.BlockSpec(memory_space=pltpu.SMEM)] * len(lead)
        + [vmem] * len(operands),
        out_specs=[vmem] * len(shapes),
        out_shape=[jax.ShapeDtypeStruct(s, kind) for s, kind in shapes],
        compiler_params=pltpu.CompilerParams(vmem_limit_bytes=14 * 1024 * 1024),
    )(*lead, *operands)


def pack_kernel(place, wide, z1, z2, z3, half, far_half, out):
    zl = place[4]
    here = pl.ds(pl.multiple_of(zl * HALF, HALF), HALF)
    there = pl.ds(pl.multiple_of((1 - zl) * HALF, HALF), HALF)
    pair = lambda a, b: jnp.concatenate([widen(a[...]), widen(b[...])], 0).astype(bf16)
    out[:, here] = pair(wide, z2)
    out[:, there] = pair(z1, z3)
    for i in range(6):
        at = WIDTH + 512 * i
        out[:, at : at + 256] = half[16 * i : 16 * i + 16, :]
        out[:, at + 256 : at + 512] = far_half[16 * i : 16 * i + 16, :]


def unpack_kernel(*refs):
    got, (block, factor) = refs[:4], refs[4:]
    for k, g in enumerate(got):
        block[16 * k : 16 * k + 16, :] = g[:, :WIDTH]
        factor[16 * k : 16 * k + 16, :] = g[:, WIDTH:]


def stack_kernel(*refs):
    out = refs[-1]
    for k, r in enumerate(refs[:-1]):
        out[64 * k : 64 * k + 64, :] = r[...]


def sum_kernel(own, b1, b2, b3, keep, s1, s2, s3):
    for k, out in enumerate((keep, s1, s2, s3)):
        part = slice(16 * k, 16 * k + 16)
        total = own[part, :]
        for b in (b1, b3, b2):
            total += widen(b[part, :])
        out[...] = total.astype(out.dtype)


def split_kernel(place, own, b1, b2, b3, keep, s1, s2, s3):
    zl = place[4]
    here = pl.ds(pl.multiple_of(zl * HALF, HALF), HALF)
    there = pl.ds(pl.multiple_of((1 - zl) * HALF, HALF), HALF)
    for cols, near, far in ((here, keep, s2), (there, s1, s3)):
        total = own[:, cols]
        for b in (b1, b2, b3):
            total += widen(b[:, cols])
        near[...] = total[:8].astype(near.dtype)
        far[...] = total[8:].astype(far.dtype)


def shards(
    inputs,
    frozen_gate_weight,
    frozen_up_weight,
    frozen_down_weight,
    adapter_first_gate,
    adapter_second_gate,
    adapter_first_up,
    adapter_second_up,
    adapter_first_down,
    adapter_second_down,
):
    zh, y, x, zl, c = (lax.axis_index(a) for a in AXES)
    place = jnp.stack([zh, y, x, c, zl]).astype(jnp.int32)

    def ordered(flag, a, b, axis):
        return jnp.where(
            flag == 0, jnp.concatenate([a, b], axis), jnp.concatenate([b, a], axis)
        )

    own = jnp.where(c == 0, inputs[0], inputs[1])
    other = jnp.where(c == 0, inputs[1], inputs[0])
    wide = ordered(c, own, send(other, CORE), 1)
    ranks = jnp.stack([adapter_first_gate, adapter_first_up, adapter_second_down])
    half = jnp.where(c == 0, ranks[:, :32], ranks[:, 32:]).reshape(96, 256)
    far_half = send(half, ALONG_Z[3])
    gate2 = send(frozen_gate_weight, CORE)

    from_z = {k: send(wide, ALONG_Z[k]) for k in (1, 2, 3)}
    (packed,) = local(
        pack_kernel,
        [((16, WIDTH + 3072), bf16)],
        (wide, from_z[1], from_z[2], from_z[3], half, far_half),
        place,
    )
    packed = after(packed, gate2)

    got = [packed] + [send(packed, FIRST[k]) for k in (1, 2, 3)]
    up2 = send(after(frozen_up_weight, packed), CORE)
    own_b = after((adapter_second_gate, adapter_second_up, adapter_first_down), packed)
    own_b = jnp.concatenate(own_b, 1)
    far_b = send(own_b, CORE)
    block, factor = local(
        unpack_kernel, [((64, WIDTH), bf16), ((64, 3072), bf16)], got
    )
    block, factor = after((block, factor), (up2, far_b))

    (factor,) = local(
        stack_kernel,
        [((256, 3072), bf16)],
        [factor] + [send(factor, SECOND[k]) for k in (1, 2, 3)],
    )
    rows = [block] + [send(block, SECOND[k]) for k in (1, 3)]
    factor2 = send(factor, CORE)
    rows.append(send(after(block, factor), SECOND[2]))
    down2 = send(after(frozen_down_weight, factor), CORE)

    seconds = jnp.concatenate([own_b, far_b], 0)
    gate_b, up_b, down_b = (
        ordered(c, s[:, :32], s[:, 32:], 1)
        for s in (seconds[:, :64], seconds[:, 64:128], seconds[:, 128:])
    )
    blank = jnp.zeros((2 * UNITS, 32), bf16)
    gate_b = jnp.concatenate([gate_b[:, :32], blank, gate_b[:, 32:], blank], 1)
    up_b = jnp.concatenate([blank, up_b[:, :32], blank, up_b[:, 32:]], 1)

    weights = (
        frozen_gate_weight, gate2, frozen_up_weight, up2, frozen_down_weight, down2,
    )
    seconds = (gate_b, up_b, down_b)

    total, part1, part3 = ffn(
        place, rows[:3], weights, factor, factor2, seconds, (f32, bf16, bf16)
    )
    back = {1: send(part1, SECOND[1]), 3: send(part3, SECOND[3])}
    (part2,) = ffn(
        place, [after(rows[3], part1)], weights, factor, factor2, seconds, (bf16,)
    )
    back[2] = send(part2, SECOND[2])
    small = [((16, WIDTH), f32)] + [((16, WIDTH), bf16)] * 3
    mine, *parts = local(sum_kernel, small, (total, back[1], back[2], back[3]))
    backs = [send(p, FIRST[k]) for k, p in zip((1, 2, 3), parts, strict=True)]
    small = [((8, HALF), f32)] + [((8, HALF), bf16)] * 3
    done, *parts = local(split_kernel, small, (mine, *backs), place)
    for k, p in zip((1, 2, 3), parts, strict=True):
        done = done + widen(send(p, ALONG_Z[k]))
    done = done.astype(bf16)
    keep = jnp.where(c == 0, done[:, :2048], done[:, 2048:])
    give = jnp.where(c == 0, done[:, 2048:], done[:, :2048])
    got = send(give, CORE)
    return ordered(c, keep[None], got[None], 0)


def solution(mesh):
    fine = Mesh(mesh.devices.reshape(SIZES), AXES)
    learner, tensor = ("zh", "y", "x"), ("zl", "c")
    in_specs = (
        P(None, learner, tensor),
        P(AXES, None),
        P(AXES, None),
        P(AXES, None),
        P(None, learner),
        P(AXES, None),
        P(None, learner),
        P(AXES, None),
        P(AXES, None),
        P(None, learner),
    )
    return jax.shard_map(
        shards,
        mesh=fine,
        in_specs=in_specs,
        out_specs=P(None, learner, tensor),
        check_vma=False,
    )
```

```python
import itertools

import jax
import jax.numpy as jnp
from jax import lax
from jax.experimental import pallas as pl
from jax.experimental.pallas import tpu as pltpu
from jax.sharding import Mesh, PartitionSpec as P

AXES = ("zh", "y", "x", "zl", "c")
SIZES = (2, 4, 4, 2, 2)
adapter_scale = 0.5
WIDTH = 8192
HALF = WIDTH // 2
UNITS = 224
TILE = 2048
STEPS = WIDTH // TILE
PARTS = TILE // 256
f32, bf16 = jnp.float32, jnp.bfloat16
SMALL = pl.CostEstimate(flops=1, bytes_accessed=1, transcendentals=0)


def index(zh, y, x, zl, c):
    return (((zh * 4 + y) * 4 + x) * 2 + zl) * 2 + c


def pairs(partner):
    out = []
    for zh, y, x, zl, c in itertools.product(*map(range, SIZES)):
        z, y2, x2, c2 = partner(zh * 2 + zl, y, x, c)
        out.append((index(zh, y, x, zl, c), index(z >> 1, y2, x2, z & 1, c2)))
    return out


CORE = pairs(lambda z, y, x, c: (z, y, x, 1 - c))
ALONG_Z = {k: pairs(lambda z, y, x, c: (z ^ k, y, x, c)) for k in (1, 2, 3)}
FIRST = {
    k: pairs(lambda z, y, x, c: (z, y ^ k, x, c) if c else (z, y, x ^ k, c))
    for k in (1, 2, 3)
}
SECOND = {
    k: pairs(lambda z, y, x, c: (z, y, x ^ k, c) if c else (z, y ^ k, x, c))
    for k in (1, 2, 3)
}


def send(value, route):
    return lax.ppermute(value, AXES, route)


def nt(a, b):
    return lax.dot_general(a, b, (((1,), (1,)), ((), ())), preferred_element_type=f32)


def tn(a, b):
    return lax.dot_general(a, b, (((0,), (0,)), ((), ())), preferred_element_type=f32)


def nn(a, b):
    return jnp.dot(a, b, preferred_element_type=f32)


def widen(a):
    return a.astype(f32)


def after(value, others):
    return lax.optimization_barrier((value, others))[0]


def project_kernel(n, *refs):
    rows, weights, out = refs[:n], refs[n : n + 4], refs[n + 4]
    for i in range(WIDTH // TILE):
        tile = slice(i * TILE, (i + 1) * TILE)
        x = jnp.concatenate([r[:, tile] for r in rows], axis=0)
        w = jnp.concatenate([r[:, tile] for r in weights], axis=0)
        if i == 0:
            out[...] = nt(w, x)
        else:
            out[...] += nt(w, x)


def down_kernel(n, place, *refs):
    rows = refs[:n]
    acc, down_w, down_w2, factor, factor2 = refs[n : n + 5]
    seconds = refs[n + 5]
    outs = refs[n + 6 : 2 * n + 6]
    low, first, second, hidden = refs[2 * n + 6 :]

    def shards_of(i, to, groups, base):
        for j in range(PARTS):
            learner = i * PARTS + j
            zh, y, x = learner // 16, (learner // 4) % 4, learner % 4
            dz, dy, dx = zh ^ place[0], y ^ place[1], x ^ place[2]
            for other, src in ((0, factor), (1, factor2)):
                along_x = (place[3] ^ other) == 0
                near = jnp.where(along_x, dx, dy)
                far = jnp.where(along_x, dy, dx)
                r = pl.ds(pl.multiple_of((far * 4 + near) * 16, 16), 16)
                for k in range(groups):
                    at = pl.multiple_of((base + k) * 512 + dz * 256, 256)
                    row = (place[3] ^ other) * 32 + (k // 2) * 64 + (k % 2) * 16
                    row = pl.ds(pl.multiple_of(row, 16), 16)
                    to[row, j * 256 : j * 256 + 256] = src[r, pl.ds(at, 256)]

    low[...] = jnp.zeros_like(low)

    @pl.loop(0, STEPS)
    def _(i):
        tile = pl.ds(pl.multiple_of(i * TILE, TILE), TILE)
        shards_of(i, first, 4, 0)
        x = jnp.concatenate([r[:, tile] for r in rows], axis=0)
        low[...] += nt(first[...], x)

    u = (adapter_scale * low[...]).astype(bf16)
    hs, back = [], 0.0
    for half, (ref, c) in enumerate(((seconds, 0), (factor2, 3072))):
        b = [ref[64 * k : 64 * k + 64, c : c + UNITS] for k in range(3)]
        at = half * UNITS
        g = acc[at : at + UNITS] + tn(b[0], u[:64])
        at += 2 * UNITS
        v = acc[at : at + UNITS] + tn(b[1], u[64:])
        h = g / (1.0 + jnp.exp(-g)) * v
        back += nn(b[2], h.astype(bf16))
        hs.append(h)
    h, back = jnp.concatenate(hs, axis=0), adapter_scale * back
    hidden[...] = jnp.concatenate([h, back], axis=0).T.astype(bf16)

    @pl.loop(0, STEPS)
    def _(i):
        tile = pl.ds(pl.multiple_of(i * TILE, TILE), TILE)
        shards_of(i, second, 2, 4)
        w = jnp.concatenate([down_w[:, tile], down_w2[:, tile], second[...]], axis=0)
        result = nn(hidden[...], w)
        for k, out in enumerate(outs):
            out[:, tile] = result[k * 64 : (k + 1) * 64].astype(out.dtype)


VMEM = pl.BlockSpec(memory_space=pltpu.VMEM)
SMEM = pl.BlockSpec(memory_space=pltpu.SMEM)


def in_vmem(operands):
    return [pltpu.with_memory_space_constraint(a, pltpu.VMEM) for a in operands]


def cost(macs):
    return pl.CostEstimate(flops=2 * macs, bytes_accessed=2 * macs // 64, transcendentals=0)


def project(rows, weights):
    n = len(rows)
    return pl.pallas_call(
        lambda *refs: project_kernel(n, *refs),
        in_specs=[VMEM] * (n + 4),
        out_specs=VMEM,
        out_shape=jax.ShapeDtypeStruct((4 * UNITS, 64 * n), f32),
        compiler_params=pltpu.CompilerParams(vmem_limit_bytes=10 * 1024 * 1024),
        cost_estimate=cost(64 * n * WIDTH * 4 * UNITS),
    )(*in_vmem([*rows, *weights]))


def down(place, rows, acc, weights, factors, seconds, kinds):
    n = len(rows)
    m = 64 * n
    operands = in_vmem([*rows, acc, *weights, *factors, seconds])
    return pl.pallas_call(
        lambda *refs: down_kernel(n, *refs),
        in_specs=[SMEM] + [VMEM] * len(operands),
        out_specs=[VMEM] * n,
        out_shape=[jax.ShapeDtypeStruct((64, WIDTH), kind) for kind in kinds],
        scratch_shapes=[
            pltpu.VMEM((128, m), f32),
            pltpu.VMEM((128, TILE), bf16),
            pltpu.VMEM((64, TILE), bf16),
            pltpu.VMEM((m, 512), bf16),
        ],
        compiler_params=pltpu.CompilerParams(vmem_limit_bytes=10 * 1024 * 1024),
        cost_estimate=cost(m * WIDTH * (2 * UNITS + 192)),
    )(place, *operands)


def local(body, shapes, operands, place=None, price=SMALL):
    lead = [] if place is None else [place]
    return pl.pallas_call(
        body,
        in_specs=[SMEM] * len(lead) + [VMEM] * len(operands),
        out_specs=[VMEM] * len(shapes),
        out_shape=[jax.ShapeDtypeStruct(s, kind) for s, kind in shapes],
        compiler_params=pltpu.CompilerParams(vmem_limit_bytes=6 * 1024 * 1024),
        cost_estimate=price,
    )(*lead, *operands)


def pack_kernel(place, wide, z1, z2, z3, half, far_half, out):
    zl = place[4]
    here = pl.ds(pl.multiple_of(zl * HALF, HALF), HALF)
    there = pl.ds(pl.multiple_of((1 - zl) * HALF, HALF), HALF)
    pair = lambda a, b: jnp.concatenate([widen(a[...]), widen(b[...])], 0).astype(bf16)
    out[:, here] = pair(wide, z2)
    out[:, there] = pair(z1, z3)
    for i in range(6):
        at = WIDTH + 512 * i
        out[:, at : at + 256] = half[16 * i : 16 * i + 16, :]
        out[:, at + 256 : at + 512] = far_half[16 * i : 16 * i + 16, :]


def unpack_kernel(*refs):
    got, (block, factor, packed) = refs[:4], refs[4:]
    for k, g in enumerate(got):
        at = slice(16 * k, 16 * k + 16)
        block[at, :] = g[:, :WIDTH]
        factor[at, :] = g[:, WIDTH:]
        packed[at, :] = g[...]


def seconds_kernel(*refs):
    out = refs[-1]
    out[...] = jnp.zeros_like(out)
    for k, r in enumerate(refs[:-1]):
        out[64 * k : 64 * k + 64, :UNITS] = r[...]


def stack_kernel(own, f1, f3, packed2, seconds, out, rows2):
    for k, r in enumerate((own, f1, packed2, f3)):
        out[64 * k : 64 * k + 64, :3072] = r[:, -3072:]
    out[:, 3072:] = seconds[...]
    rows2[...] = packed2[:, :WIDTH]


def add_kernel(own, b, out):
    out[...] = own[...] + widen(b[...])


def sum_kernel(own, b1, b3, keep, s1, s2, s3):
    for k, out in enumerate((keep, s1, s2, s3)):
        part = slice(16 * k, 16 * k + 16)
        total = own[part, :]
        for b in (b1, b3):
            total += widen(b[part, :])
        out[...] = total.astype(out.dtype)


def split_kernel(place, own, b1, b2, b3, keep, s1, s2, s3):
    zl = place[4]
    here = pl.ds(pl.multiple_of(zl * HALF, HALF), HALF)
    there = pl.ds(pl.multiple_of((1 - zl) * HALF, HALF), HALF)
    for cols, near, far in ((here, keep, s2), (there, s1, s3)):
        total = own[:, cols]
        for b in (b1, b2, b3):
            total += widen(b[:, cols])
        near[...] = total[:8].astype(near.dtype)
        far[...] = total[8:].astype(far.dtype)


def shards(
    inputs,
    frozen_gate_weight,
    frozen_up_weight,
    frozen_down_weight,
    adapter_first_gate,
    adapter_second_gate,
    adapter_first_up,
    adapter_second_up,
    adapter_first_down,
    adapter_second_down,
):
    zh, y, x, zl, c = (lax.axis_index(a) for a in AXES)
    place = jnp.stack([zh, y, x, c, zl]).astype(jnp.int32)

    def ordered(flag, a, b, axis):
        return jnp.where(
            flag == 0, jnp.concatenate([a, b], axis), jnp.concatenate([b, a], axis)
        )

    own = jnp.where(c == 0, inputs[0], inputs[1])
    other = jnp.where(c == 0, inputs[1], inputs[0])
    wide = ordered(c, own, send(other, CORE), 1)
    ranks = jnp.stack([adapter_first_gate, adapter_first_up, adapter_second_down])
    half = jnp.where(c == 0, ranks[:, :32], ranks[:, 32:]).reshape(96, 256)
    far_half = send(half, ALONG_Z[3])

    from_z = {k: send(wide, ALONG_Z[k]) for k in (1, 2, 3)}
    gate2 = send(after(frozen_gate_weight, wide), CORE)
    (packed,) = local(
        pack_kernel,
        [((16, WIDTH + 3072), bf16)],
        (wide, from_z[1], from_z[2], from_z[3], half, far_half),
        place,
    )
    packed = after(packed, gate2)

    got = [packed] + [send(packed, FIRST[k]) for k in (1, 2, 3)]
    up2 = send(after(frozen_up_weight, packed), CORE)
    seconds = (adapter_second_gate, adapter_second_up, adapter_first_down)
    (seconds,) = local(
        seconds_kernel,
        [((256, 256), bf16)],
        [a.T for a in after(seconds, packed)],
    )
    block, factor, packed = local(
        unpack_kernel,
        [((64, WIDTH), bf16), ((64, 3072), bf16), ((64, WIDTH + 3072), bf16)],
        got,
    )
    block, factor, packed = after((block, factor, packed), up2)

    got = [send(factor, SECOND[1]), send(factor, SECOND[3]), send(packed, SECOND[2])]
    down2 = send(after(frozen_down_weight, packed), CORE)
    factor, rows2 = local(
        stack_kernel,
        [((256, 3072 + 256), bf16), ((64, WIDTH), bf16)],
        (factor, *got, seconds),
    )
    factor2 = send(factor, CORE)
    rows1, rows3 = (send(after(block, factor), SECOND[k]) for k in (1, 3))

    weights = (frozen_gate_weight, gate2, frozen_up_weight, up2)
    down_weights = (frozen_down_weight, down2)

    rows = (block, rows2)
    acc = project(rows, weights)
    total, part2 = down(
        place, rows, acc, down_weights, (factor, factor2), seconds, (f32, bf16)
    )
    back2 = send(part2, SECOND[2])
    rows = after((rows1, rows3), part2)
    acc = project(rows, weights)
    part1, part3 = down(
        place, rows, acc, down_weights, (factor, factor2), seconds, (bf16, bf16)
    )
    back1, back3 = send(part1, SECOND[1]), send(part3, SECOND[3])
    (total,) = local(
        add_kernel, [((64, WIDTH), f32)], (total, back2), price=cost(64 * WIDTH * 64 * 16)
    )
    small = [((16, WIDTH), f32)] + [((16, WIDTH), bf16)] * 3
    mine, *parts = local(sum_kernel, small, (total, back1, back3))
    backs = [send(p, FIRST[k]) for k, p in zip((1, 2, 3), parts, strict=True)]
    small = [((8, HALF), f32)] + [((8, HALF), bf16)] * 3
    done, *parts = local(split_kernel, small, (mine, *backs), place)
    for k, p in zip((1, 2, 3), parts, strict=True):
        done = done + widen(send(p, ALONG_Z[k]))
    done = done.astype(bf16)
    keep = jnp.where(c == 0, done[:, :2048], done[:, 2048:])
    give = jnp.where(c == 0, done[:, 2048:], done[:, :2048])
    got = send(give, CORE)
    return ordered(c, keep[None], got[None], 0)


def solution(mesh):
    fine = Mesh(mesh.devices.reshape(SIZES), AXES)
    learner, tensor = ("zh", "y", "x"), ("zl", "c")
    in_specs = (
        P(None, learner, tensor),
        P(AXES, None),
        P(AXES, None),
        P(AXES, None),
        P(None, learner),
        P(AXES, None),
        P(None, learner),
        P(AXES, None),
        P(AXES, None),
        P(None, learner),
    )
    return jax.shard_map(
        shards,
        mesh=fine,
        in_specs=in_specs,
        out_specs=P(None, learner, tensor),
        check_vma=False,
    )
```

```python
import itertools

import jax
import jax.numpy as jnp
from jax import lax
from jax.experimental import pallas as pl
from jax.experimental.pallas import tpu as pltpu
from jax.sharding import Mesh, PartitionSpec as P

AXES = ("zh", "y", "x", "zl", "c")
SIZES = (2, 4, 4, 2, 2)
adapter_scale = 0.5
WIDTH = 8192
HALF = WIDTH // 2
QUARTER = WIDTH // 4
UNITS = 224
TILE = 4096
STEPS = WIDTH // TILE
PARTS = TILE // 256
f32, bf16 = jnp.float32, jnp.bfloat16
SMALL = pl.CostEstimate(flops=1, bytes_accessed=1, transcendentals=0)


def index(zh, y, x, zl, c):
    return (((zh * 4 + y) * 4 + x) * 2 + zl) * 2 + c


def pairs(partner):
    out = []
    for zh, y, x, zl, c in itertools.product(*map(range, SIZES)):
        z, y2, x2, c2 = partner(zh * 2 + zl, y, x, c)
        out.append((index(zh, y, x, zl, c), index(z >> 1, y2, x2, z & 1, c2)))
    return out


CORE = pairs(lambda z, y, x, c: (z, y, x, 1 - c))
ALONG_Z = {k: pairs(lambda z, y, x, c: (z ^ k, y, x, c)) for k in (1, 2, 3)}
FIRST = {
    k: pairs(lambda z, y, x, c: (z, y ^ k, x, c) if c else (z, y, x ^ k, c))
    for k in (1, 2, 3)
}
SECOND = {
    k: pairs(lambda z, y, x, c: (z, y, x ^ k, c) if c else (z, y ^ k, x, c))
    for k in (1, 2, 3)
}


def send(value, route):
    return lax.ppermute(value, AXES, route)


def nt(a, b):
    return lax.dot_general(a, b, (((1,), (1,)), ((), ())), preferred_element_type=f32)


def tn(a, b):
    return lax.dot_general(a, b, (((0,), (0,)), ((), ())), preferred_element_type=f32)


def nn(a, b):
    return jnp.dot(a, b, preferred_element_type=f32)


def widen(a):
    return a.astype(f32)


def after(value, others):
    return lax.optimization_barrier((value, others))[0]


def project_kernel(n, *refs):
    rows, weights, out = refs[:n], refs[n : n + 4], refs[n + 4]
    for i in range(WIDTH // TILE):
        tile = slice(i * TILE, (i + 1) * TILE)
        x = jnp.concatenate([r[:, tile] for r in rows], axis=0)
        w = jnp.concatenate([r[:, tile] for r in weights], axis=0)
        if i == 0:
            out[...] = nt(w, x)
        else:
            out[...] += nt(w, x)


def down_kernel(n, place, *refs):
    rows = refs[:n]
    acc, down_w, down_w2, seconds, theirs = refs[n : n + 5]
    if place is None:
        first, second = refs[n + 5 : n + 7]
    else:
        sources = refs[n + 5 : n + 7]
        first, second = refs[2 * n + 7 : 2 * n + 9]
    outs = refs[n + 7 : 2 * n + 7]
    hidden = refs[-1]

    def shards_of(learner, to, groups, base):
        if place is None:
            return
        zh, y, x = learner // 16, (learner // 4) % 4, learner % 4
        dz, dy, dx = zh ^ place[0], y ^ place[1], x ^ place[2]
        for other, src in enumerate(sources):
            along_x = (place[3] ^ other) == 0
            near = jnp.where(along_x, dx, dy)
            far = jnp.where(along_x, dy, dx)
            r = pl.ds(pl.multiple_of((far * 4 + near) * 16, 16), 16)
            for k in range(groups):
                at = pl.multiple_of((base + k) * 512 + dz * 256, 256)
                row = (place[3] ^ other) * 32 + (k // 2) * 64 + (k % 2) * 16
                row = pl.ds(pl.multiple_of(row, 16), 16)
                to[row, learner * 256 : learner * 256 + 256] = src[r, pl.ds(at, 256)]

    low = 0.0
    for i in range(STEPS):
        tile = slice(i * TILE, (i + 1) * TILE)
        for j in range(PARTS):
            shards_of(i * PARTS + j, first, 4, 0)
        x = jnp.concatenate([r[:, tile] for r in rows], axis=0)
        low += nt(first[:, tile], x)

    u = (adapter_scale * low).astype(bf16)
    hs, back = [], 0.0
    for half, (ref, c) in enumerate(((seconds, 0), (theirs, 3072))):
        b = [ref[64 * k : 64 * k + 64, c : c + UNITS] for k in range(3)]
        at = half * UNITS
        g = acc[at : at + UNITS] + tn(b[0], u[:64])
        at += 2 * UNITS
        v = acc[at : at + UNITS] + tn(b[1], u[64:])
        h = g / (1.0 + jnp.exp(-g)) * v
        back += nn(b[2], h.astype(bf16))
        hs.append(h)
    h = jnp.concatenate([*hs, adapter_scale * back], axis=0)
    hidden[...] = h.T.astype(bf16)

    for i in range(STEPS):
        tile = slice(i * TILE, (i + 1) * TILE)
        for j in range(PARTS):
            shards_of(i * PARTS + j, second, 2, 4)
        w = jnp.concatenate([r[:, tile] for r in (down_w, down_w2, second)], axis=0)
        result = nn(hidden[...], w)
        for k, out in enumerate(outs):
            out[:, tile] = result[k * 64 : (k + 1) * 64].astype(out.dtype)


VMEM = pl.BlockSpec(memory_space=pltpu.VMEM)
SMEM = pl.BlockSpec(memory_space=pltpu.SMEM)


def in_vmem(operands):
    return [pltpu.with_memory_space_constraint(a, pltpu.VMEM) for a in operands]


def cost(macs):
    return pl.CostEstimate(flops=2 * macs, bytes_accessed=2 * macs // 64, transcendentals=0)


def project(rows, weights):
    n = len(rows)
    return pl.pallas_call(
        lambda *refs: project_kernel(n, *refs),
        in_specs=[VMEM] * (n + 4),
        out_specs=VMEM,
        out_shape=jax.ShapeDtypeStruct((4 * UNITS, 64 * n), f32),
        compiler_params=pltpu.CompilerParams(vmem_limit_bytes=10 * 1024 * 1024),
        cost_estimate=SMALL,
    )(*in_vmem([*rows, *weights]))


def down(place, rows, acc, weights, seconds, factors, kinds):
    n = len(rows)
    theirs = factors[1] if place is not None else seconds[1]
    operands = in_vmem([*rows, acc, *weights, seconds[0], theirs, *factors])
    shapes = [((64, WIDTH), kind) for kind in kinds]
    lead = []
    body = lambda *refs: down_kernel(n, None, *refs)
    if place is not None:
        lead = [place]
        body = lambda *refs: down_kernel(n, *refs)
        shapes += [((128, WIDTH), bf16), ((64, WIDTH), bf16)]
    return pl.pallas_call(
        body,
        in_specs=[SMEM] * len(lead) + [VMEM] * len(operands),
        out_specs=[VMEM] * len(shapes),
        out_shape=[jax.ShapeDtypeStruct(s, kind) for s, kind in shapes],
        scratch_shapes=[pltpu.VMEM((64 * n, 512), bf16)],
        compiler_params=pltpu.CompilerParams(vmem_limit_bytes=10 * 1024 * 1024),
        cost_estimate=SMALL,
    )(*lead, *operands)


def local(body, shapes, operands, place=None, price=SMALL, far=(), scratch=()):
    lead = [] if place is None else [place]
    return pl.pallas_call(
        body,
        in_specs=[SMEM] * len(lead)
        + [VMEM] * len(operands)
        + [pl.BlockSpec(memory_space=pltpu.HBM)] * len(far),
        out_specs=[VMEM] * len(shapes),
        out_shape=[jax.ShapeDtypeStruct(s, kind) for s, kind in shapes],
        scratch_shapes=list(scratch),
        compiler_params=pltpu.CompilerParams(vmem_limit_bytes=6 * 1024 * 1024),
        cost_estimate=price,
    )(*lead, *operands, *far)


def shape_kernel(place, own, other, gate, up, down, wide, message, ranks, sems):
    c = place[3]
    half = pl.ds(pl.multiple_of(c * 32, 32), 32)
    copies = [
        pltpu.make_async_copy(r.at[half, :], ranks.at[k], sems.at[k])
        for k, r in enumerate((gate, up, down))
    ]
    for copy in copies:
        copy.start()
    wide[:, pl.ds(pl.multiple_of(c * QUARTER, QUARTER), QUARTER)] = own[...]
    wide[:, pl.ds(pl.multiple_of((1 - c) * QUARTER, QUARTER), QUARTER)] = other[...]
    rows = widen(wide[...])
    rows = jnp.concatenate([rows[:, :QUARTER], rows[:, QUARTER:]], axis=0)
    message[:, :QUARTER] = rows.astype(bf16)
    for copy in copies:
        copy.wait()
    for i in range(6):
        col = QUARTER + 256 * i
        message[:, col : col + 256] = ranks[i // 2, (i % 2) * 16 : (i % 2) * 16 + 16, :]


def pack_kernel(place, wide, z1, z2, message, far_message, out):
    zl = place[4]
    here = pl.ds(pl.multiple_of(zl * HALF, HALF), HALF)
    there = pl.ds(pl.multiple_of((1 - zl) * HALF, HALF), HALF)
    z3 = widen(far_message[:, :QUARTER])
    z3 = jnp.concatenate([z3[:8], z3[8:]], axis=1)
    pair = lambda a, b: jnp.concatenate([widen(a), widen(b)], 0).astype(bf16)
    out[:, here] = pair(wide[...], z2[...])
    out[:, there] = pair(z1[...], z3)
    for i in range(6):
        at, col = WIDTH + 512 * i, QUARTER + 256 * i
        out[:, at : at + 256] = message[:, col : col + 256]
        out[:, at + 256 : at + 512] = far_message[:, col : col + 256]


def unpack_kernel(*refs):
    got, (block, factor, packed) = refs[:4], refs[4:]
    for k, g in enumerate(got):
        at = slice(16 * k, 16 * k + 16)
        block[at, :] = g[:, :WIDTH]
        factor[at, :] = g[:, WIDTH:]
        packed[at, :] = g[...]


def seconds_kernel(gate_w, up_w, down_w, gate, up, down, out):
    out[...] = jnp.zeros_like(out)
    for k, r in enumerate((gate, up, down)):
        out[64 * k : 64 * k + 64, :UNITS] = r[...]


def stack_kernel(own, packed1, f2, packed3, seconds, out):
    for k, r in enumerate((own, packed1, f2, packed3)):
        out[64 * k : 64 * k + 64, :3072] = r[:, -3072:]
    out[:, 3072:] = seconds[...]


def add_kernel(own, b1, b3, out):
    out[...] = own[...] + widen(b1[...]) + widen(b3[...])


def sum_kernel(own, b, keep, s1, s2, s3):
    for k, out in enumerate((keep, s1, s2, s3)):
        part = slice(16 * k, 16 * k + 16)
        out[...] = (own[part, :] + widen(b[part, :])).astype(out.dtype)


def split_kernel(place, own, b1, b2, b3, keep, s1, s2, s3):
    zl = place[4]
    here = pl.ds(pl.multiple_of(zl * HALF, HALF), HALF)
    there = pl.ds(pl.multiple_of((1 - zl) * HALF, HALF), HALF)
    for cols, near, far in ((here, keep, s2), (there, s1, s3)):
        total = own[:, cols]
        for b in (b1, b2, b3):
            total += widen(b[:, cols])
        near[...] = total[:8].astype(near.dtype)
        far[...] = total[8:].astype(far.dtype)


def shards(
    inputs,
    frozen_gate_weight,
    frozen_up_weight,
    frozen_down_weight,
    adapter_first_gate,
    adapter_second_gate,
    adapter_first_up,
    adapter_second_up,
    adapter_first_down,
    adapter_second_down,
):
    zh, y, x, zl, c = (lax.axis_index(a) for a in AXES)
    place = jnp.stack([zh, y, x, c, zl]).astype(jnp.int32)

    def ordered(flag, a, b, axis):
        return jnp.where(
            flag == 0, jnp.concatenate([a, b], axis), jnp.concatenate([b, a], axis)
        )

    own = jnp.where(c == 0, inputs[0], inputs[1])
    other = jnp.where(c == 0, inputs[1], inputs[0])
    wide, message = local(
        shape_kernel,
        [((8, HALF), bf16), ((16, QUARTER + 1536), bf16)],
        (own, send(other, CORE)),
        place,
        far=(adapter_first_gate, adapter_first_up, adapter_second_down),
        scratch=[pltpu.VMEM((3, 32, 256), bf16), pltpu.SemaphoreType.DMA((3,))],
    )

    z1, z2, z3 = (
        send(v, ALONG_Z[k]) for k, v in ((1, wide), (2, wide), (3, message))
    )
    gate2 = send(after(frozen_gate_weight, wide), CORE)
    up2 = send(after(frozen_up_weight, wide), CORE)
    (packed,) = local(
        pack_kernel,
        [((16, WIDTH + 3072), bf16)],
        (wide, z1, z2, message, z3),
        place,
    )

    packed = after(packed, gate2)
    got = [packed] + [send(packed, FIRST[k]) for k in (1, 2, 3)]
    down2 = send(after(frozen_down_weight, packed), CORE)
    block, factor, packed = local(
        unpack_kernel,
        [((64, WIDTH), bf16), ((64, 3072), bf16), ((64, WIDTH + 3072), bf16)],
        got,
    )
    block, factor, packed = after((block, factor, packed), (up2, down2))

    packed1, packed3 = send(packed, SECOND[1]), send(packed, SECOND[3])
    factor_2 = send(factor, SECOND[2])
    seconds = (adapter_second_gate, adapter_second_up, adapter_first_down)
    owned, seconds = after(
        ((frozen_gate_weight, frozen_up_weight, frozen_down_weight), seconds), packed
    )
    (seconds,) = local(
        seconds_kernel, [((256, 256), bf16)], [*in_vmem(owned), *(a.T for a in seconds)]
    )
    (factor,) = local(
        stack_kernel,
        [((256, 3072 + 256), bf16)],
        (factor, packed1, factor_2, packed3, seconds),
    )
    factor2 = send(factor, CORE)
    rows2 = send(after(block, factor), SECOND[2])

    weights = (owned[0], gate2, owned[1], up2)
    down_weights = (owned[2], down2)

    rows = (block, packed1, packed3)
    acc = project(rows, weights)
    total, part1, part3, first, second = down(
        place, rows, acc, down_weights, (seconds, factor2), (factor, factor2),
        (f32, bf16, bf16),
    )
    back1, back3 = send(part1, SECOND[1]), send(part3, SECOND[3])
    rows = (after(rows2, part1),)
    acc = project(rows, weights)
    (part2,) = down(
        None, rows, acc, down_weights, (seconds, factor2), (first, second), (bf16,)
    )
    back2 = send(part2, SECOND[2])
    (total,) = local(
        add_kernel,
        [((64, WIDTH), f32)],
        (total, back1, back3),
        price=cost(64 * WIDTH * 64 * 16),
    )
    small = [((16, WIDTH), f32)] + [((16, WIDTH), bf16)] * 3
    mine, *parts = local(sum_kernel, small, (total, back2))
    backs = [send(p, FIRST[k]) for k, p in zip((1, 2, 3), parts, strict=True)]
    small = [((8, HALF), f32)] + [((8, HALF), bf16)] * 3
    done, *parts = local(split_kernel, small, (mine, *backs), place)
    for k, p in zip((1, 2, 3), parts, strict=True):
        done = done + widen(send(p, ALONG_Z[k]))
    done = done.astype(bf16)
    keep = jnp.where(c == 0, done[:, :2048], done[:, 2048:])
    give = jnp.where(c == 0, done[:, 2048:], done[:, :2048])
    got = send(give, CORE)
    return ordered(c, keep[None], got[None], 0)


def solution(mesh):
    fine = Mesh(mesh.devices.reshape(SIZES), AXES)
    learner, tensor = ("zh", "y", "x"), ("zl", "c")
    in_specs = (
        P(None, learner, tensor),
        P(AXES, None),
        P(AXES, None),
        P(AXES, None),
        P(None, learner),
        P(AXES, None),
        P(None, learner),
        P(AXES, None),
        P(AXES, None),
        P(None, learner),
    )
    return jax.shard_map(
        shards,
        mesh=fine,
        in_specs=in_specs,
        out_specs=P(None, learner, tensor),
        check_vma=False,
    )
```

```python
import itertools

import jax
import jax.numpy as jnp
from jax import lax
from jax.experimental import pallas as pl
from jax.experimental.pallas import tpu as pltpu
from jax.sharding import Mesh, PartitionSpec as P

AXES = ("zh", "y", "x", "zl", "c")
SIZES = (2, 4, 4, 2, 2)
adapter_scale = 0.5
WIDTH = 8192
HALF = WIDTH // 2
QUARTER = WIDTH // 4
UNITS = 224
TILE = 4096
STEPS = WIDTH // TILE
PARTS = TILE // 256
f32, bf16 = jnp.float32, jnp.bfloat16
C1, C2, CK = 3.6, 3.8, 8
SMALL = pl.CostEstimate(flops=1, bytes_accessed=1, transcendentals=0)


def index(zh, y, x, zl, c):
    return (((zh * 4 + y) * 4 + x) * 2 + zl) * 2 + c


def pairs(partner):
    out = []
    for zh, y, x, zl, c in itertools.product(*map(range, SIZES)):
        z, y2, x2, c2 = partner(zh * 2 + zl, y, x, c)
        out.append((index(zh, y, x, zl, c), index(z >> 1, y2, x2, z & 1, c2)))
    return out


CORE = pairs(lambda z, y, x, c: (z, y, x, 1 - c))
ALONG_Z = {k: pairs(lambda z, y, x, c: (z ^ k, y, x, c)) for k in (1, 2, 3)}
FIRST = {
    k: pairs(lambda z, y, x, c: (z, y ^ k, x, c) if c else (z, y, x ^ k, c))
    for k in (1, 2, 3)
}
SECOND = {
    k: pairs(lambda z, y, x, c: (z, y, x ^ k, c) if c else (z, y ^ k, x, c))
    for k in (1, 2, 3)
}


def send(value, route):
    return lax.ppermute(value, AXES, route)


def nt(a, b):
    return lax.dot_general(a, b, (((1,), (1,)), ((), ())), preferred_element_type=f32)


def tn(a, b):
    return lax.dot_general(a, b, (((0,), (0,)), ((), ())), preferred_element_type=f32)


def nn(a, b):
    return jnp.dot(a, b, preferred_element_type=f32)


def widen(a):
    return a.astype(f32)


def after(value, others):
    return lax.optimization_barrier((value, others))[0]


def project_kernel(n, *refs):
    rows, weights, out = refs[:n], refs[n : n + 4], refs[n + 4]
    for i in range(WIDTH // TILE):
        tile = slice(i * TILE, (i + 1) * TILE)
        x = jnp.concatenate([r[:, tile] for r in rows], axis=0)
        w = jnp.concatenate([r[:, tile] for r in weights], axis=0)
        if i == 0:
            out[...] = nt(w, x)
        else:
            out[...] += nt(w, x)


def down_kernel(n, place, *refs):
    rows = refs[:n]
    acc, down_w, down_w2, seconds, theirs = refs[n : n + 5]
    if place is None:
        first, second = refs[n + 5 : n + 7]
    else:
        sources = refs[n + 5 : n + 7]
        first, second = refs[2 * n + 7 : 2 * n + 9]
    outs = refs[n + 7 : 2 * n + 7]
    hidden = refs[-1]

    def shards_of(learner, to, groups, base):
        if place is None:
            return
        zh, y, x = learner // 16, (learner // 4) % 4, learner % 4
        dz, dy, dx = zh ^ place[0], y ^ place[1], x ^ place[2]
        for other, src in enumerate(sources):
            along_x = (place[3] ^ other) == 0
            near = jnp.where(along_x, dx, dy)
            far = jnp.where(along_x, dy, dx)
            r = pl.ds(pl.multiple_of((far * 4 + near) * 16, 16), 16)
            for k in range(groups):
                at = pl.multiple_of((base + k) * 512 + dz * 256, 256)
                row = (place[3] ^ other) * 32 + (k // 2) * 64 + (k % 2) * 16
                row = pl.ds(pl.multiple_of(row, 16), 16)
                to[row, learner * 256 : learner * 256 + 256] = src[r, pl.ds(at, 256)]

    low = 0.0
    for i in range(STEPS):
        tile = slice(i * TILE, (i + 1) * TILE)
        for j in range(PARTS):
            shards_of(i * PARTS + j, first, 4, 0)
        x = jnp.concatenate([r[:, tile] for r in rows], axis=0)
        low += nt(first[:, tile], x)

    u = (adapter_scale * low).astype(bf16)
    hs, back = [], 0.0
    for half, (ref, c) in enumerate(((seconds, 0), (theirs, 3072))):
        b = [ref[64 * k : 64 * k + 64, c : c + UNITS] for k in range(3)]
        at = half * UNITS
        g = acc[at : at + UNITS] + tn(b[0], u[:64])
        at += 2 * UNITS
        v = acc[at : at + UNITS] + tn(b[1], u[64:])
        h = g / (1.0 + jnp.exp(-g)) * v
        back += nn(b[2], h.astype(bf16))
        hs.append(h)
    h = jnp.concatenate([*hs, adapter_scale * back], axis=0)
    hidden[...] = h.T.astype(bf16)

    for i in range(STEPS):
        tile = slice(i * TILE, (i + 1) * TILE)
        for j in range(PARTS):
            shards_of(i * PARTS + j, second, 2, 4)
        w = jnp.concatenate([r[:, tile] for r in (down_w, down_w2, second)], axis=0)
        result = nn(hidden[...], w)
        for k, out in enumerate(outs):
            out[:, tile] = result[k * 64 : (k + 1) * 64].astype(out.dtype)


VMEM = pl.BlockSpec(memory_space=pltpu.VMEM)
SMEM = pl.BlockSpec(memory_space=pltpu.SMEM)


def in_vmem(operands):
    return [pltpu.with_memory_space_constraint(a, pltpu.VMEM) for a in operands]


def price_of(us):
    return pl.CostEstimate(
        flops=int(us * 1.15e9), bytes_accessed=int(us * 3.6e6), transcendentals=0
    )


def project(rows, weights, *extra):
    n, more = len(rows), len(extra)
    return pl.pallas_call(
        lambda *refs: project_kernel(n, *refs[more:]),
        in_specs=[VMEM] * (more + n + 4),
        out_specs=VMEM,
        out_shape=jax.ShapeDtypeStruct((4 * UNITS, 64 * n), f32),
        compiler_params=pltpu.CompilerParams(vmem_limit_bytes=10 * 1024 * 1024),
        cost_estimate=price_of(CK),
    )(*extra, *in_vmem([*rows, *weights]))


def down(place, rows, acc, weights, seconds, factors, kinds):
    n = len(rows)
    theirs = factors[1] if place is not None else seconds[1]
    operands = in_vmem([*rows, acc, *weights, seconds[0], theirs, *factors])
    shapes = [((64, WIDTH), kind) for kind in kinds]
    lead = []
    body = lambda *refs: down_kernel(n, None, *refs)
    if place is not None:
        lead = [place]
        body = lambda *refs: down_kernel(n, *refs)
        shapes += [((128, WIDTH), bf16), ((64, WIDTH), bf16)]
    return pl.pallas_call(
        body,
        in_specs=[SMEM] * len(lead) + [VMEM] * len(operands),
        out_specs=[VMEM] * len(shapes),
        out_shape=[jax.ShapeDtypeStruct(s, kind) for s, kind in shapes],
        scratch_shapes=[pltpu.VMEM((64 * n, 512), bf16)],
        compiler_params=pltpu.CompilerParams(vmem_limit_bytes=10 * 1024 * 1024),
        cost_estimate=SMALL,
    )(*lead, *operands)


def local(body, shapes, operands, place=None, price=SMALL, far=(), scratch=()):
    lead = [] if place is None else [place]
    return pl.pallas_call(
        body,
        in_specs=[SMEM] * len(lead)
        + [VMEM] * len(operands)
        + [pl.BlockSpec(memory_space=pltpu.HBM)] * len(far),
        out_specs=[VMEM] * len(shapes),
        out_shape=[jax.ShapeDtypeStruct(s, kind) for s, kind in shapes],
        scratch_shapes=list(scratch),
        compiler_params=pltpu.CompilerParams(vmem_limit_bytes=6 * 1024 * 1024),
        cost_estimate=price,
    )(*lead, *operands, *(pltpu.with_memory_space_constraint(a, pltpu.HBM) for a in far))


def begin_kernel(place, inputs, gate, up, down, own, other, factor, ranks, sems):
    c = place[3]
    half = pl.ds(pl.multiple_of(c * 32, 32), 32)
    copies = [pltpu.make_async_copy(inputs.at[c], own, sems.at[0])]
    copies += [pltpu.make_async_copy(inputs.at[1 - c], other, sems.at[1])]
    for k, r in enumerate((gate, up, down)):
        copies += [pltpu.make_async_copy(r.at[half, :], ranks.at[k], sems.at[2 + k])]
    for copy in copies:
        copy.start()
    for copy in copies:
        copy.wait()
    for i in range(6):
        col = slice(256 * i, 256 * i + 256)
        factor[:, col] = ranks[i // 2, (i % 2) * 16 : (i % 2) * 16 + 16, :]


def shape_kernel(place, own, other, wide):
    c = place[3]
    wide[:, pl.ds(pl.multiple_of(c * QUARTER, QUARTER), QUARTER)] = own[...]
    wide[:, pl.ds(pl.multiple_of((1 - c) * QUARTER, QUARTER), QUARTER)] = other[...]


def pack_kernel(place, wide, z1, z2, z3, out):
    zl = place[4]
    here = pl.ds(pl.multiple_of(zl * HALF, HALF), HALF)
    there = pl.ds(pl.multiple_of((1 - zl) * HALF, HALF), HALF)
    pair = lambda a, b: jnp.concatenate([widen(a[...]), widen(b[...])], 0).astype(bf16)
    out[:, here] = pair(wide, z2)
    out[:, there] = pair(z1, z3)


def pair_kernel(near, far, out):
    for i in range(6):
        out[:, 512 * i : 512 * i + 256] = near[:, 256 * i : 256 * i + 256]
        out[:, 512 * i + 256 : 512 * i + 512] = far[:, 256 * i : 256 * i + 256]


def swap_kernel(a, b, out):
    out[:32, :] = a[...]
    out[32:48, :] = b[16:, :]
    out[48:, :] = b[:16, :]


def rows_kernel(*refs):
    out, step = refs[-1], refs[0].shape[0]
    for k, r in enumerate(refs[:-1]):
        out[step * k : step * k + step, :] = r[...]


def touch_kernel(gate_w, up_w, down_w, out):
    out[...] = jnp.zeros_like(out)


def seconds_kernel(gate, up, down, out):
    out[...] = jnp.zeros_like(out)
    for k, r in enumerate((gate, up, down)):
        out[64 * k : 64 * k + 64, :UNITS] = r[...]


def stack_kernel(f0, f1, f2, f3, seconds, out):
    for k, r in enumerate((f0, f1, f2, f3)):
        out[64 * k : 64 * k + 64, :3072] = r[...]
    out[:, 3072:] = seconds[...]


def add_kernel(own, b1, b3, out):
    out[...] = own[...] + widen(b1[...]) + widen(b3[...])


def sum_kernel(own, b, keep, s1, s2, s3):
    for k, out in enumerate((keep, s1, s2, s3)):
        part = slice(16 * k, 16 * k + 16)
        out[...] = (own[part, :] + widen(b[part, :])).astype(out.dtype)


def split_kernel(place, own, b1, b2, b3, keep, s1, s2, s3):
    zl = place[4]
    here = pl.ds(pl.multiple_of(zl * HALF, HALF), HALF)
    there = pl.ds(pl.multiple_of((1 - zl) * HALF, HALF), HALF)
    for cols, near, far in ((here, keep, s2), (there, s1, s3)):
        total = own[:, cols]
        for b in (b1, b2, b3):
            total += widen(b[:, cols])
        near[...] = total[:8].astype(near.dtype)
        far[...] = total[8:].astype(far.dtype)


def shards(
    inputs,
    frozen_gate_weight,
    frozen_up_weight,
    frozen_down_weight,
    adapter_first_gate,
    adapter_second_gate,
    adapter_first_up,
    adapter_second_up,
    adapter_first_down,
    adapter_second_down,
):
    zh, y, x, zl, c = (lax.axis_index(a) for a in AXES)
    place = jnp.stack([zh, y, x, c, zl]).astype(jnp.int32)

    def ordered(flag, a, b, axis):
        return jnp.where(
            flag == 0, jnp.concatenate([a, b], axis), jnp.concatenate([b, a], axis)
        )

    own, other, factor = local(
        begin_kernel,
        [((8, QUARTER), bf16), ((8, QUARTER), bf16), ((16, 1536), bf16)],
        (),
        place,
        far=(inputs, adapter_first_gate, adapter_first_up, adapter_second_down),
        scratch=[pltpu.VMEM((3, 32, 256), bf16), pltpu.SemaphoreType.DMA((5,))],
    )
    other = send(other, CORE)
    (wide,) = local(shape_kernel, [((8, HALF), bf16)], (own, other), place)

    far_factor = send(factor, ALONG_Z[3])
    z1, z2, z3 = (send(wide, ALONG_Z[k]) for k in (1, 2, 3))
    gate2 = send(after(frozen_gate_weight, wide), CORE)
    (factor,) = local(pair_kernel, [((16, 3072), bf16)], (factor, far_factor))
    near = send(factor, FIRST[1])
    (rows,) = local(
        pack_kernel, [((16, WIDTH), bf16)], (wide, z1, z2, z3), place, price=price_of(C2)
    )

    rows = after(rows, gate2)
    (factor,) = local(rows_kernel, [((32, 3072), bf16)], (factor, near))
    near = send(factor, FIRST[3])
    rows = [rows] + [send(rows, FIRST[k]) for k in (1, 2, 3)]
    (factor,) = local(swap_kernel, [((64, 3072), bf16)], (factor, near))
    factors = {0: factor, 1: send(factor, SECOND[1]), 3: send(factor, SECOND[3])}
    seconds = (adapter_second_gate, adapter_second_up, adapter_first_down)
    (seconds,) = local(
        seconds_kernel, [((256, 256), bf16)], [a.T for a in after(seconds, rows[0])]
    )
    (block,) = local(rows_kernel, [((64, WIDTH), bf16)], rows, price=price_of(C1))

    block, factors = after((block, factors), (block, factors))
    block = after(block, seconds)
    factors[2] = send(factors[0], SECOND[2])
    rows1, rows3 = send(block, SECOND[1]), send(block, SECOND[3])
    frozen = (frozen_gate_weight, frozen_up_weight, frozen_down_weight)
    frozen = after(frozen, block)
    up2, down2 = send(frozen[1], CORE), send(frozen[2], CORE)
    (factor,) = local(
        stack_kernel,
        [((256, 3072 + 256), bf16)],
        (*(factors[k] for k in range(4)), seconds),
    )
    factor2 = send(factor, CORE)
    rows2 = send(after(block, up2), SECOND[2])
    (touched,) = local(touch_kernel, [((8, 128), f32)], in_vmem(frozen))
    owned = frozen

    weights = (owned[0], gate2, owned[1], up2)
    down_weights = (owned[2], down2)

    rows = (block, rows1, rows3)
    acc = project(rows, weights, touched)
    total, part1, part3, first, second = down(
        place, rows, acc, down_weights, (seconds, factor2), (factor, factor2),
        (f32, bf16, bf16),
    )
    back1, back3 = send(part1, SECOND[1]), send(part3, SECOND[3])
    rows = (after(rows2, part1),)
    acc = project(rows, weights)
    (part2,) = down(
        None, rows, acc, down_weights, (seconds, factor2), (first, second), (bf16,)
    )
    back2 = send(part2, SECOND[2])
    (total,) = local(
        add_kernel,
        [((64, WIDTH), f32)],
        (total, back1, back3),
        price=price_of(4.5),
    )
    small = [((16, WIDTH), f32)] + [((16, WIDTH), bf16)] * 3
    mine, *parts = local(sum_kernel, small, (total, back2))
    backs = [send(p, FIRST[k]) for k, p in zip((1, 2, 3), parts, strict=True)]
    small = [((8, HALF), f32)] + [((8, HALF), bf16)] * 3
    done, *parts = local(split_kernel, small, (mine, *backs), place)
    for k, p in zip((1, 2, 3), parts, strict=True):
        done = done + widen(send(p, ALONG_Z[k]))
    done = done.astype(bf16)
    keep = jnp.where(c == 0, done[:, :2048], done[:, 2048:])
    give = jnp.where(c == 0, done[:, 2048:], done[:, :2048])
    got = send(give, CORE)
    return ordered(c, keep[None], got[None], 0)


def solution(mesh):
    fine = Mesh(mesh.devices.reshape(SIZES), AXES)
    learner, tensor = ("zh", "y", "x"), ("zl", "c")
    in_specs = (
        P(None, learner, tensor),
        P(AXES, None),
        P(AXES, None),
        P(AXES, None),
        P(None, learner),
        P(AXES, None),
        P(None, learner),
        P(AXES, None),
        P(AXES, None),
        P(None, learner),
    )
    return jax.shard_map(
        shards,
        mesh=fine,
        in_specs=in_specs,
        out_specs=P(None, learner, tensor),
        check_vma=False,
    )
```

```python
import itertools

import jax
import jax.numpy as jnp
from jax import lax
from jax.experimental import pallas as pl
from jax.experimental.pallas import tpu as pltpu
from jax.sharding import Mesh, PartitionSpec as P

AXES = ("zh", "y", "x", "zl", "c")
SIZES = (2, 4, 4, 2, 2)
adapter_scale = 0.5
WIDTH = 8192
HALF = WIDTH // 2
QUARTER = WIDTH // 4
UNITS = 224
TILE = 4096
STEPS = WIDTH // TILE
PARTS = TILE // 256
f32, bf16 = jnp.float32, jnp.bfloat16
CK = 8
SMALL = pl.CostEstimate(flops=1, bytes_accessed=1, transcendentals=0)


def index(zh, y, x, zl, c):
    return (((zh * 4 + y) * 4 + x) * 2 + zl) * 2 + c


def pairs(partner):
    out = []
    for zh, y, x, zl, c in itertools.product(*map(range, SIZES)):
        z, y2, x2, c2 = partner(zh * 2 + zl, y, x, c)
        out.append((index(zh, y, x, zl, c), index(z >> 1, y2, x2, z & 1, c2)))
    return out


CORE = pairs(lambda z, y, x, c: (z, y, x, 1 - c))
ALONG_Z = {k: pairs(lambda z, y, x, c: (z ^ k, y, x, c)) for k in (1, 2, 3)}
FIRST = {
    k: pairs(lambda z, y, x, c: (z, y ^ k, x, c) if c else (z, y, x ^ k, c))
    for k in (1, 2, 3)
}
SECOND = {
    k: pairs(lambda z, y, x, c: (z, y, x ^ k, c) if c else (z, y ^ k, x, c))
    for k in (1, 2, 3)
}


def send(value, route):
    return lax.ppermute(value, AXES, route)


def nt(a, b):
    return lax.dot_general(a, b, (((1,), (1,)), ((), ())), preferred_element_type=f32)


def tn(a, b):
    return lax.dot_general(a, b, (((0,), (0,)), ((), ())), preferred_element_type=f32)


def nn(a, b):
    return jnp.dot(a, b, preferred_element_type=f32)


def widen(a):
    return a.astype(f32)


def after(value, others):
    return lax.optimization_barrier((value, others))[0]


def project_kernel(n, *refs):
    rows, weights, out = refs[:n], refs[n : n + 4], refs[n + 4]
    for i in range(WIDTH // TILE):
        tile = slice(i * TILE, (i + 1) * TILE)
        x = jnp.concatenate([r[:, tile] for r in rows], axis=0)
        w = jnp.concatenate([r[:, tile] for r in weights], axis=0)
        if i == 0:
            out[...] = nt(w, x)
        else:
            out[...] += nt(w, x)


def down_kernel(n, place, *refs):
    rows = refs[:n]
    acc, down_w, down_w2, seconds, theirs = refs[n : n + 5]
    if place is None:
        first, second = refs[n + 5 : n + 7]
    else:
        sources = refs[n + 5 : n + 7]
        first, second = refs[2 * n + 7 : 2 * n + 9]
    outs = refs[n + 7 : 2 * n + 7]
    hidden = refs[-1]

    def shards_of(learner, to, groups, base):
        if place is None:
            return
        zh, y, x = learner // 16, (learner // 4) % 4, learner % 4
        dz, dy, dx = zh ^ place[0], y ^ place[1], x ^ place[2]
        for other, src in enumerate(sources):
            along_x = (place[3] ^ other) == 0
            near = jnp.where(along_x, dx, dy)
            far = jnp.where(along_x, dy, dx)
            r = pl.ds(pl.multiple_of((far * 4 + near) * 16, 16), 16)
            for k in range(groups):
                at = pl.multiple_of((base + k) * 512 + dz * 256, 256)
                row = (place[3] ^ other) * 32 + (k // 2) * 64 + (k % 2) * 16
                row = pl.ds(pl.multiple_of(row, 16), 16)
                to[row, learner * 256 : learner * 256 + 256] = src[r, pl.ds(at, 256)]

    low = 0.0
    for i in range(STEPS):
        tile = slice(i * TILE, (i + 1) * TILE)
        for j in range(PARTS):
            shards_of(i * PARTS + j, first, 4, 0)
        x = jnp.concatenate([r[:, tile] for r in rows], axis=0)
        low += nt(first[:, tile], x)

    u = (adapter_scale * low).astype(bf16)
    hs, back = [], 0.0
    for half, (ref, c) in enumerate(((seconds, 0), (theirs, 3072))):
        b = [ref[64 * k : 64 * k + 64, c : c + UNITS] for k in range(3)]
        at = half * UNITS
        g = acc[at : at + UNITS] + tn(b[0], u[:64])
        at += 2 * UNITS
        v = acc[at : at + UNITS] + tn(b[1], u[64:])
        h = g / (1.0 + jnp.exp(-g)) * v
        back += nn(b[2], h.astype(bf16))
        hs.append(h)
    h = jnp.concatenate([*hs, adapter_scale * back], axis=0)
    hidden[...] = h.T.astype(bf16)

    for i in range(STEPS):
        tile = slice(i * TILE, (i + 1) * TILE)
        for j in range(PARTS):
            shards_of(i * PARTS + j, second, 2, 4)
        w = jnp.concatenate([r[:, tile] for r in (down_w, down_w2, second)], axis=0)
        result = nn(hidden[...], w)
        for k, out in enumerate(outs):
            out[:, tile] = result[k * 64 : (k + 1) * 64].astype(out.dtype)


VMEM = pl.BlockSpec(memory_space=pltpu.VMEM)
SMEM = pl.BlockSpec(memory_space=pltpu.SMEM)


def in_vmem(operands):
    return [pltpu.with_memory_space_constraint(a, pltpu.VMEM) for a in operands]


def price_of(us):
    return pl.CostEstimate(
        flops=int(us * 1.15e9), bytes_accessed=int(us * 3.6e6), transcendentals=0
    )


def project(rows, weights, *extra):
    n, more = len(rows), len(extra)
    return pl.pallas_call(
        lambda *refs: project_kernel(n, *refs[more:]),
        in_specs=[VMEM] * (more + n + 4),
        out_specs=VMEM,
        out_shape=jax.ShapeDtypeStruct((4 * UNITS, 64 * n), f32),
        compiler_params=pltpu.CompilerParams(vmem_limit_bytes=10 * 1024 * 1024),
        cost_estimate=price_of(CK),
    )(*extra, *in_vmem([*rows, *weights]))


def down(place, rows, acc, weights, seconds, factors, kinds):
    n = len(rows)
    theirs = factors[1] if place is not None else seconds[1]
    operands = in_vmem([*rows, acc, *weights, seconds[0], theirs, *factors])
    shapes = [((64, WIDTH), kind) for kind in kinds]
    lead = []
    body = lambda *refs: down_kernel(n, None, *refs)
    if place is not None:
        lead = [place]
        body = lambda *refs: down_kernel(n, *refs)
        shapes += [((128, WIDTH), bf16), ((64, WIDTH), bf16)]
    return pl.pallas_call(
        body,
        in_specs=[SMEM] * len(lead) + [VMEM] * len(operands),
        out_specs=[VMEM] * len(shapes),
        out_shape=[jax.ShapeDtypeStruct(s, kind) for s, kind in shapes],
        scratch_shapes=[pltpu.VMEM((64 * n, 512), bf16)],
        compiler_params=pltpu.CompilerParams(vmem_limit_bytes=10 * 1024 * 1024),
        cost_estimate=SMALL,
    )(*lead, *operands)


def local(body, shapes, operands, place=None, price=SMALL, far=(), scratch=()):
    lead = [] if place is None else [place]
    return pl.pallas_call(
        body,
        in_specs=[SMEM] * len(lead)
        + [VMEM] * len(operands)
        + [pl.BlockSpec(memory_space=pltpu.HBM)] * len(far),
        out_specs=[VMEM] * len(shapes),
        out_shape=[jax.ShapeDtypeStruct(s, kind) for s, kind in shapes],
        scratch_shapes=list(scratch),
        compiler_params=pltpu.CompilerParams(vmem_limit_bytes=6 * 1024 * 1024),
        cost_estimate=price,
    )(*lead, *operands, *(pltpu.with_memory_space_constraint(a, pltpu.HBM) for a in far))


def begin_kernel(place, inputs, gate, up, down, own, other, factor, ranks, sems):
    c = place[3]
    half = pl.ds(pl.multiple_of(c * 32, 32), 32)
    copies = [pltpu.make_async_copy(inputs.at[c], own, sems.at[0])]
    copies += [pltpu.make_async_copy(inputs.at[1 - c], other, sems.at[1])]
    for k, r in enumerate((gate, up, down)):
        copies += [pltpu.make_async_copy(r.at[half, :], ranks.at[k], sems.at[2 + k])]
    for copy in copies:
        copy.start()
    for copy in copies:
        copy.wait()
    for i in range(6):
        col = slice(256 * i, 256 * i + 256)
        factor[:, col] = ranks[i // 2, (i % 2) * 16 : (i % 2) * 16 + 16, :]


def shape_kernel(place, own, other, factor, wide, message):
    c = place[3]
    wide[:, pl.ds(pl.multiple_of(c * QUARTER, QUARTER), QUARTER)] = own[...]
    wide[:, pl.ds(pl.multiple_of((1 - c) * QUARTER, QUARTER), QUARTER)] = other[...]
    rows = widen(wide[...])
    rows = jnp.concatenate([rows[:, :QUARTER], rows[:, QUARTER:]], axis=0)
    message[:, :QUARTER] = rows.astype(bf16)
    message[:, QUARTER:] = factor[...]


def pack_kernel(place, wide, z1, z2, message, far_message, out):
    zl = place[4]
    here = pl.ds(pl.multiple_of(zl * HALF, HALF), HALF)
    there = pl.ds(pl.multiple_of((1 - zl) * HALF, HALF), HALF)
    z3 = widen(far_message[:, :QUARTER])
    z3 = jnp.concatenate([z3[:8], z3[8:]], axis=1)
    pair = lambda a, b: jnp.concatenate([widen(a), widen(b)], 0).astype(bf16)
    out[:, here] = pair(wide[...], z2[...])
    out[:, there] = pair(z1[...], z3)
    for i in range(6):
        at, col = WIDTH + 512 * i, QUARTER + 256 * i
        out[:, at : at + 256] = message[:, col : col + 256]
        out[:, at + 256 : at + 512] = far_message[:, col : col + 256]


def unpack_kernel(*refs):
    got, (block, factor) = refs[:4], refs[4:]
    for k, g in enumerate(got):
        block[16 * k : 16 * k + 16, :] = g[:, :WIDTH]
        factor[16 * k : 16 * k + 16, :] = g[:, WIDTH:]


def touch_kernel(gate_w, up_w, down_w, out):
    out[...] = jnp.zeros_like(out)


def seconds_kernel(gate, up, down, out):
    out[...] = jnp.zeros_like(out)
    for k, r in enumerate((gate, up, down)):
        out[64 * k : 64 * k + 64, :UNITS] = r[...]


def stack_kernel(f0, f1, f2, f3, seconds, out):
    for k, r in enumerate((f0, f1, f2, f3)):
        out[64 * k : 64 * k + 64, :3072] = r[...]
    out[:, 3072:] = seconds[...]


def add_kernel(own, b1, b3, out):
    out[...] = own[...] + widen(b1[...]) + widen(b3[...])


def sum_kernel(own, b, keep, s1, s2, s3):
    for k, out in enumerate((keep, s1, s2, s3)):
        part = slice(16 * k, 16 * k + 16)
        out[...] = (own[part, :] + widen(b[part, :])).astype(out.dtype)


def split_kernel(place, own, b1, b2, b3, keep, s1, s2, s3):
    zl = place[4]
    here = pl.ds(pl.multiple_of(zl * HALF, HALF), HALF)
    there = pl.ds(pl.multiple_of((1 - zl) * HALF, HALF), HALF)
    for cols, near, far in ((here, keep, s2), (there, s1, s3)):
        total = own[:, cols]
        for b in (b1, b2, b3):
            total += widen(b[:, cols])
        near[...] = total[:8].astype(near.dtype)
        far[...] = total[8:].astype(far.dtype)


def shards(
    inputs,
    frozen_gate_weight,
    frozen_up_weight,
    frozen_down_weight,
    adapter_first_gate,
    adapter_second_gate,
    adapter_first_up,
    adapter_second_up,
    adapter_first_down,
    adapter_second_down,
):
    zh, y, x, zl, c = (lax.axis_index(a) for a in AXES)
    place = jnp.stack([zh, y, x, c, zl]).astype(jnp.int32)

    def ordered(flag, a, b, axis):
        return jnp.where(
            flag == 0, jnp.concatenate([a, b], axis), jnp.concatenate([b, a], axis)
        )

    own, other, factor = local(
        begin_kernel,
        [((8, QUARTER), bf16), ((8, QUARTER), bf16), ((16, 1536), bf16)],
        (),
        place,
        far=(inputs, adapter_first_gate, adapter_first_up, adapter_second_down),
        scratch=[pltpu.VMEM((3, 32, 256), bf16), pltpu.SemaphoreType.DMA((5,))],
    )
    other = send(other, CORE)
    wide, message = local(
        shape_kernel,
        [((8, HALF), bf16), ((16, QUARTER + 1536), bf16)],
        (own, other, factor),
        place,
    )

    z1, z2, z3 = (
        send(v, ALONG_Z[k]) for k, v in ((1, wide), (2, wide), (3, message))
    )
    gate2 = send(after(frozen_gate_weight, wide), CORE)
    up2 = send(after(frozen_up_weight, wide), CORE)
    (packed,) = local(
        pack_kernel, [((16, WIDTH + 3072), bf16)], (wide, z1, z2, message, z3), place
    )

    packed = after(packed, gate2)
    got = [packed] + [send(packed, FIRST[k]) for k in (1, 2, 3)]
    down2 = send(after(frozen_down_weight, packed), CORE)
    seconds = (adapter_second_gate, adapter_second_up, adapter_first_down)
    (seconds,) = local(
        seconds_kernel, [((256, 256), bf16)], [a.T for a in after(seconds, packed)]
    )
    block, factor = local(unpack_kernel, [((64, WIDTH), bf16), ((64, 3072), bf16)], got)

    block, factor = after((block, factor), (up2, down2, seconds))
    factors = [factor] + [send(factor, SECOND[k]) for k in (1, 2, 3)]
    rows1, rows3 = send(block, SECOND[1]), send(block, SECOND[3])
    (factor,) = local(stack_kernel, [((256, 3072 + 256), bf16)], (*factors, seconds))
    factor2 = send(factor, CORE)
    rows2 = send(after(block, factor), SECOND[2])
    frozen = (frozen_gate_weight, frozen_up_weight, frozen_down_weight)
    owned = after(frozen, block)
    (touched,) = local(touch_kernel, [((8, 128), f32)], in_vmem(owned))

    weights = (owned[0], gate2, owned[1], up2)
    down_weights = (owned[2], down2)

    rows = (block, rows1, rows3)
    acc = project(rows, weights, touched)
    total, part1, part3, first, second = down(
        place, rows, acc, down_weights, (seconds, factor2), (factor, factor2),
        (f32, bf16, bf16),
    )
    back1, back3 = send(part1, SECOND[1]), send(part3, SECOND[3])
    rows = (after(rows2, part1),)
    acc = project(rows, weights)
    (part2,) = down(
        None, rows, acc, down_weights, (seconds, factor2), (first, second), (bf16,)
    )
    back2 = send(part2, SECOND[2])
    (total,) = local(
        add_kernel,
        [((64, WIDTH), f32)],
        (total, back1, back3),
        price=price_of(4.5),
    )
    small = [((16, WIDTH), f32)] + [((16, WIDTH), bf16)] * 3
    mine, *parts = local(sum_kernel, small, (total, back2))
    backs = [send(p, FIRST[k]) for k, p in zip((1, 2, 3), parts, strict=True)]
    small = [((8, HALF), f32)] + [((8, HALF), bf16)] * 3
    done, *parts = local(split_kernel, small, (mine, *backs), place)
    for k, p in zip((1, 2, 3), parts, strict=True):
        done = done + widen(send(p, ALONG_Z[k]))
    done = done.astype(bf16)
    keep = jnp.where(c == 0, done[:, :2048], done[:, 2048:])
    give = jnp.where(c == 0, done[:, 2048:], done[:, :2048])
    got = send(give, CORE)
    return ordered(c, keep[None], got[None], 0)


def solution(mesh):
    fine = Mesh(mesh.devices.reshape(SIZES), AXES)
    learner, tensor = ("zh", "y", "x"), ("zl", "c")
    in_specs = (
        P(None, learner, tensor),
        P(AXES, None),
        P(AXES, None),
        P(AXES, None),
        P(None, learner),
        P(AXES, None),
        P(None, learner),
        P(AXES, None),
        P(AXES, None),
        P(None, learner),
    )
    return jax.shard_map(
        shards,
        mesh=fine,
        in_specs=in_specs,
        out_specs=P(None, learner, tensor),
        check_vma=False,
    )
```

```python
import itertools

import jax
import jax.numpy as jnp
from jax import lax
from jax.experimental import pallas as pl
from jax.experimental.pallas import tpu as pltpu
from jax.sharding import Mesh, PartitionSpec as P

AXES = ("zh", "y", "x", "zl", "c")
SIZES = (2, 4, 4, 2, 2)
adapter_scale = 0.5
WIDTH = 8192
HALF = WIDTH // 2
QUARTER = WIDTH // 4
UNITS = 224
TILE = 4096
STEPS = WIDTH // TILE
PARTS = TILE // 256
f32, bf16 = jnp.float32, jnp.bfloat16
CK = 8
SMALL = pl.CostEstimate(flops=1, bytes_accessed=1, transcendentals=0)


def index(zh, y, x, zl, c):
    return (((zh * 4 + y) * 4 + x) * 2 + zl) * 2 + c


def pairs(partner):
    out = []
    for zh, y, x, zl, c in itertools.product(*map(range, SIZES)):
        z, y2, x2, c2 = partner(zh * 2 + zl, y, x, c)
        out.append((index(zh, y, x, zl, c), index(z >> 1, y2, x2, z & 1, c2)))
    return out


CORE = pairs(lambda z, y, x, c: (z, y, x, 1 - c))
ALONG_Z = {k: pairs(lambda z, y, x, c: (z ^ k, y, x, c)) for k in (1, 2, 3)}
FIRST = {
    k: pairs(lambda z, y, x, c: (z, y ^ k, x, c) if c else (z, y, x ^ k, c))
    for k in (1, 2, 3)
}
SECOND = {
    k: pairs(lambda z, y, x, c: (z, y, x ^ k, c) if c else (z, y ^ k, x, c))
    for k in (1, 2, 3)
}


def send(value, route):
    return lax.ppermute(value, AXES, route)


def spread(value, routes):
    got = {k: send(value, routes[k]) for k in (2, 1, 3)}
    return [value, got[1], got[2], got[3]]


def nt(a, b):
    return lax.dot_general(a, b, (((1,), (1,)), ((), ())), preferred_element_type=f32)


def tn(a, b):
    return lax.dot_general(a, b, (((0,), (0,)), ((), ())), preferred_element_type=f32)


def nn(a, b):
    return jnp.dot(a, b, preferred_element_type=f32)


def widen(a):
    return a.astype(f32)


def after(value, others):
    return lax.optimization_barrier((value, others))[0]


def project_kernel(n, *refs):
    rows, weights, out = refs[:n], refs[n : n + 4], refs[n + 4]
    for i in range(WIDTH // TILE):
        tile = slice(i * TILE, (i + 1) * TILE)
        x = jnp.concatenate([r[:, tile] for r in rows], axis=0)
        w = jnp.concatenate([r[:, tile] for r in weights], axis=0)
        if i == 0:
            out[...] = nt(w, x)
        else:
            out[...] += nt(w, x)


def down_kernel(n, n_out, place, *refs):
    rows = refs[:n]
    acc, down_w, down_w2, seconds, theirs = refs[n : n + 5]
    if place is None:
        first, second = refs[n + 5 : n + 7]
    else:
        sources = refs[n + 5 : n + 7]
        first, second = refs[n + 7 + n_out : n + 9 + n_out]
    outs = refs[n + 7 : n + 7 + n_out]
    hidden = refs[-1]

    def shards_of(learner, to, groups, base):
        if place is None:
            return
        zh, y, x = learner // 16, (learner // 4) % 4, learner % 4
        dz, dy, dx = zh ^ place[0], y ^ place[1], x ^ place[2]
        for other, src in enumerate(sources):
            along_x = (place[3] ^ other) == 0
            near = jnp.where(along_x, dx, dy)
            far = jnp.where(along_x, dy, dx)
            r = pl.ds(pl.multiple_of((far * 4 + near) * 16, 16), 16)
            for k in range(groups):
                at = pl.multiple_of((base + k) * 512 + dz * 256, 256)
                row = (place[3] ^ other) * 32 + (k // 2) * 64 + (k % 2) * 16
                row = pl.ds(pl.multiple_of(row, 16), 16)
                to[row, learner * 256 : learner * 256 + 256] = src[r, pl.ds(at, 256)]

    low = 0.0
    for i in range(STEPS):
        tile = slice(i * TILE, (i + 1) * TILE)
        for j in range(PARTS):
            shards_of(i * PARTS + j, first, 4, 0)
        x = jnp.concatenate([r[:, tile] for r in rows], axis=0)
        low += nt(first[:, tile], x)

    u = (adapter_scale * low).astype(bf16)
    hs, back = [], 0.0
    for half, (ref, c) in enumerate(((seconds, 0), (theirs, 3072))):
        b = [ref[64 * k : 64 * k + 64, c : c + UNITS] for k in range(3)]
        at = half * UNITS
        g = acc[at : at + UNITS] + tn(b[0], u[:64])
        at += 2 * UNITS
        v = acc[at : at + UNITS] + tn(b[1], u[64:])
        h = g / (1.0 + jnp.exp(-g)) * v
        back += nn(b[2], h.astype(bf16))
        hs.append(h)
    h = jnp.concatenate([*hs, adapter_scale * back], axis=0)
    hidden[...] = h.T.astype(bf16)

    for i in range(STEPS):
        tile = slice(i * TILE, (i + 1) * TILE)
        for j in range(PARTS):
            shards_of(i * PARTS + j, second, 2, 4)
        w = jnp.concatenate([r[:, tile] for r in (down_w, down_w2, second)], axis=0)
        result = nn(hidden[...], w)
        for k, out in enumerate(outs):
            out[:, tile] = result[k * 64 : (k + 1) * 64].astype(out.dtype)


VMEM = pl.BlockSpec(memory_space=pltpu.VMEM)
SMEM = pl.BlockSpec(memory_space=pltpu.SMEM)


def in_vmem(operands):
    return [pltpu.with_memory_space_constraint(a, pltpu.VMEM) for a in operands]


def price_of(us):
    return pl.CostEstimate(
        flops=int(us * 1.15e9), bytes_accessed=int(us * 3.6e6), transcendentals=0
    )


def project(rows, weights, *extra):
    n, more = len(rows), len(extra)
    return pl.pallas_call(
        lambda *refs: project_kernel(n, *refs[more:]),
        in_specs=[VMEM] * (more + n + 4),
        out_specs=VMEM,
        out_shape=jax.ShapeDtypeStruct((4 * UNITS, sum(r.shape[0] for r in rows)), f32),
        compiler_params=pltpu.CompilerParams(vmem_limit_bytes=10 * 1024 * 1024),
        cost_estimate=price_of(CK),
    )(*extra, *in_vmem([*rows, *weights]))


def down(place, rows, acc, weights, seconds, factors, kinds):
    n = len(rows)
    theirs = factors[1] if place is not None else seconds[1]
    operands = in_vmem([*rows, acc, *weights, seconds[0], theirs, *factors])
    shapes = [((64, WIDTH), kind) for kind in kinds]
    lead = []
    n_out = len(kinds)
    body = lambda *refs: down_kernel(n, n_out, None, *refs)
    if place is not None:
        lead = [place]
        body = lambda *refs: down_kernel(n, n_out, *refs)
        shapes += [((128, WIDTH), bf16), ((64, WIDTH), bf16)]
    return pl.pallas_call(
        body,
        in_specs=[SMEM] * len(lead) + [VMEM] * len(operands),
        out_specs=[VMEM] * len(shapes),
        out_shape=[jax.ShapeDtypeStruct(s, kind) for s, kind in shapes],
        scratch_shapes=[pltpu.VMEM((64 * n_out, 512), bf16)],
        compiler_params=pltpu.CompilerParams(vmem_limit_bytes=10 * 1024 * 1024),
        cost_estimate=SMALL,
    )(*lead, *operands)


def local(body, shapes, operands, place=None, price=SMALL, far=(), scratch=()):
    lead = [] if place is None else [place]
    return pl.pallas_call(
        body,
        in_specs=[SMEM] * len(lead)
        + [VMEM] * len(operands)
        + [pl.BlockSpec(memory_space=pltpu.HBM)] * len(far),
        out_specs=[VMEM] * len(shapes),
        out_shape=[jax.ShapeDtypeStruct(s, kind) for s, kind in shapes],
        scratch_shapes=list(scratch),
        compiler_params=pltpu.CompilerParams(vmem_limit_bytes=6 * 1024 * 1024),
        cost_estimate=price,
    )(*lead, *operands, *(pltpu.with_memory_space_constraint(a, pltpu.HBM) for a in far))


def begin_kernel(place, inputs, gate, up, down, own, other, factor, ranks, sems):
    c = place[3]
    half = pl.ds(pl.multiple_of(c * 32, 32), 32)
    copies = [pltpu.make_async_copy(inputs.at[c], own, sems.at[0])]
    copies += [pltpu.make_async_copy(inputs.at[1 - c], other, sems.at[1])]
    for k, r in enumerate((gate, up, down)):
        copies += [pltpu.make_async_copy(r.at[half, :], ranks.at[k], sems.at[2 + k])]
    for copy in copies:
        copy.start()
    for copy in copies:
        copy.wait()
    for i in range(6):
        col = slice(256 * i, 256 * i + 256)
        factor[:, col] = ranks[i // 2, (i % 2) * 16 : (i % 2) * 16 + 16, :]


def shape_kernel(place, own, other, factor, wide, message):
    c = place[3]
    wide[:, pl.ds(pl.multiple_of(c * QUARTER, QUARTER), QUARTER)] = own[...]
    wide[:, pl.ds(pl.multiple_of((1 - c) * QUARTER, QUARTER), QUARTER)] = other[...]
    rows = widen(wide[...])
    rows = jnp.concatenate([rows[:, :QUARTER], rows[:, QUARTER:]], axis=0)
    message[:, :QUARTER] = rows.astype(bf16)
    message[:, QUARTER:] = factor[...]


def pack_kernel(place, wide, z1, z2, message, far_message, out):
    zl = place[4]
    here = pl.ds(pl.multiple_of(zl * HALF, HALF), HALF)
    there = pl.ds(pl.multiple_of((1 - zl) * HALF, HALF), HALF)
    z3 = widen(far_message[:, :QUARTER])
    z3 = jnp.concatenate([z3[:8], z3[8:]], axis=1)
    pair = lambda a, b: jnp.concatenate([widen(a), widen(b)], 0).astype(bf16)
    out[:, here] = pair(wide[...], z2[...])
    out[:, there] = pair(z1[...], z3)
    for i in range(6):
        at, col = WIDTH + 512 * i, QUARTER + 256 * i
        out[:, at : at + 256] = message[:, col : col + 256]
        out[:, at + 256 : at + 512] = far_message[:, col : col + 256]


def unpack_kernel(*refs):
    got, (block, factor) = refs[:4], refs[4:]
    for k, g in enumerate(got):
        block[16 * k : 16 * k + 16, :] = g[:, :WIDTH]
        factor[16 * k : 16 * k + 16, :] = g[:, WIDTH:]


def halves_kernel(rows3, rows1, to1, to3):
    to1[...] = rows3[:32, :]
    to3[...] = rows1[32:, :]


def touch_kernel(gate_w, up_w, down_w, out):
    out[...] = jnp.zeros_like(out)


def seconds_kernel(gate, up, down, out):
    out[...] = jnp.zeros_like(out)
    for k, r in enumerate((gate, up, down)):
        out[64 * k : 64 * k + 64, :UNITS] = r[...]


def stack_kernel(f0, f1, f2, f3, seconds, out):
    for k, r in enumerate((f0, f1, f2, f3)):
        out[64 * k : 64 * k + 64, :3072] = r[...]
    out[:, 3072:] = seconds[...]


def add_kernel(own, b1, b3, out):
    out[...] = own[...] + widen(b1[...]) + widen(b3[...])


def sum_kernel(own, b, keep, s1, s2, s3):
    for k, out in enumerate((keep, s1, s2, s3)):
        part = slice(16 * k, 16 * k + 16)
        out[...] = (own[part, :] + widen(b[part, :])).astype(out.dtype)


def split_kernel(place, own, b1, b2, b3, keep, s1, s2, s3):
    zl = place[4]
    here = pl.ds(pl.multiple_of(zl * HALF, HALF), HALF)
    there = pl.ds(pl.multiple_of((1 - zl) * HALF, HALF), HALF)
    for cols, near, far in ((here, keep, s2), (there, s1, s3)):
        total = own[:, cols]
        for b in (b1, b2, b3):
            total += widen(b[:, cols])
        near[...] = total[:8].astype(near.dtype)
        far[...] = total[8:].astype(far.dtype)


def shards(
    inputs,
    frozen_gate_weight,
    frozen_up_weight,
    frozen_down_weight,
    adapter_first_gate,
    adapter_second_gate,
    adapter_first_up,
    adapter_second_up,
    adapter_first_down,
    adapter_second_down,
):
    zh, y, x, zl, c = (lax.axis_index(a) for a in AXES)
    place = jnp.stack([zh, y, x, c, zl]).astype(jnp.int32)

    def ordered(flag, a, b, axis):
        return jnp.where(
            flag == 0, jnp.concatenate([a, b], axis), jnp.concatenate([b, a], axis)
        )

    own, other, factor = local(
        begin_kernel,
        [((8, QUARTER), bf16), ((8, QUARTER), bf16), ((16, 1536), bf16)],
        (),
        place,
        far=(inputs, adapter_first_gate, adapter_first_up, adapter_second_down),
        scratch=[pltpu.VMEM((3, 32, 256), bf16), pltpu.SemaphoreType.DMA((5,))],
    )
    other = send(other, CORE)
    wide, message = local(
        shape_kernel,
        [((8, HALF), bf16), ((16, QUARTER + 1536), bf16)],
        (own, other, factor),
        place,
    )

    z1, z2, z3 = (
        send(v, ALONG_Z[k]) for k, v in ((1, wide), (2, wide), (3, message))
    )
    gate2 = send(after(frozen_gate_weight, wide), CORE)
    up2 = send(after(frozen_up_weight, wide), CORE)
    (packed,) = local(
        pack_kernel, [((16, WIDTH + 3072), bf16)], (wide, z1, z2, message, z3), place
    )

    packed = after(packed, gate2)
    got = spread(packed, FIRST)
    down2 = send(after(frozen_down_weight, packed), CORE)
    seconds = (adapter_second_gate, adapter_second_up, adapter_first_down)
    (seconds,) = local(
        seconds_kernel, [((256, 256), bf16)], [a.T for a in after(seconds, packed)]
    )
    block, factor = local(unpack_kernel, [((64, WIDTH), bf16), ((64, 3072), bf16)], got)

    block, factor = after((block, factor), (up2, down2, seconds))
    factors = spread(factor, SECOND)
    rows1, rows3 = send(block, SECOND[1]), send(block, SECOND[3])
    (factor,) = local(stack_kernel, [((256, 3072 + 256), bf16)], (*factors, seconds))
    factor2 = send(factor, CORE)
    to1, to3 = local(halves_kernel, [((32, WIDTH), bf16)] * 2, (rows3, rows1))
    rows2 = (send(to1, SECOND[1]), send(to3, SECOND[3]))
    frozen = (frozen_gate_weight, frozen_up_weight, frozen_down_weight)
    owned = after(frozen, block)
    (touched,) = local(touch_kernel, [((8, 128), f32)], in_vmem(owned))

    weights = (owned[0], gate2, owned[1], up2)
    down_weights = (owned[2], down2)

    rows = (block, rows1, rows3)
    acc = project(rows, weights, touched)
    total, part1, part3, first, second = down(
        place, rows, acc, down_weights, (seconds, factor2), (factor, factor2),
        (f32, bf16, bf16),
    )
    back1, back3 = send(part1, SECOND[1]), send(part3, SECOND[3])
    rows = after(rows2, part1)
    acc = project(rows, weights)
    (part2,) = down(
        None, rows, acc, down_weights, (seconds, factor2), (first, second), (bf16,)
    )
    back2 = send(part2, SECOND[2])
    (total,) = local(
        add_kernel,
        [((64, WIDTH), f32)],
        (total, back1, back3),
        price=price_of(4.5),
    )
    small = [((16, WIDTH), f32)] + [((16, WIDTH), bf16)] * 3
    mine, *parts = local(sum_kernel, small, (total, back2))
    backs = [send(p, FIRST[k]) for k, p in zip((1, 2, 3), parts, strict=True)]
    small = [((8, HALF), f32)] + [((8, HALF), bf16)] * 3
    done, *parts = local(split_kernel, small, (mine, *backs), place)
    for k, p in zip((1, 2, 3), parts, strict=True):
        done = done + widen(send(p, ALONG_Z[k]))
    done = done.astype(bf16)
    keep = jnp.where(c == 0, done[:, :2048], done[:, 2048:])
    give = jnp.where(c == 0, done[:, 2048:], done[:, :2048])
    got = send(give, CORE)
    return ordered(c, keep[None], got[None], 0)


def solution(mesh):
    fine = Mesh(mesh.devices.reshape(SIZES), AXES)
    learner, tensor = ("zh", "y", "x"), ("zl", "c")
    in_specs = (
        P(None, learner, tensor),
        P(AXES, None),
        P(AXES, None),
        P(AXES, None),
        P(None, learner),
        P(AXES, None),
        P(None, learner),
        P(AXES, None),
        P(AXES, None),
        P(None, learner),
    )
    return jax.shard_map(
        shards,
        mesh=fine,
        in_specs=in_specs,
        out_specs=P(None, learner, tensor),
        check_vma=False,
    )
```

```python
import itertools

import jax
import jax.numpy as jnp
from jax import lax
from jax.experimental import pallas as pl
from jax.experimental.pallas import tpu as pltpu
from jax.sharding import Mesh, PartitionSpec as P

AXES = ("zh", "y", "x", "zl", "c")
SIZES = (2, 4, 4, 2, 2)
adapter_scale = 0.5
WIDTH = 8192
HALF = WIDTH // 2
QUARTER = WIDTH // 4
CUT = (WIDTH + 3072) // 2
UNITS = 224
TILE = 4096
STEPS = WIDTH // TILE
PARTS = TILE // 256
f32, bf16 = jnp.float32, jnp.bfloat16
CK = 8
SMALL = pl.CostEstimate(flops=1, bytes_accessed=1, transcendentals=0)


def index(zh, y, x, zl, c):
    return (((zh * 4 + y) * 4 + x) * 2 + zl) * 2 + c


def pairs(partner):
    out = []
    for zh, y, x, zl, c in itertools.product(*map(range, SIZES)):
        z, y2, x2, c2 = partner(zh * 2 + zl, y, x, c)
        out.append((index(zh, y, x, zl, c), index(z >> 1, y2, x2, z & 1, c2)))
    return out


CORE = pairs(lambda z, y, x, c: (z, y, x, 1 - c))
ALONG_Z = {k: pairs(lambda z, y, x, c: (z ^ k, y, x, c)) for k in (1, 2, 3)}
FIRST = {
    k: pairs(lambda z, y, x, c: (z, y ^ k, x, c) if c else (z, y, x ^ k, c))
    for k in (1, 2, 3)
}
SECOND = {
    k: pairs(lambda z, y, x, c: (z, y, x ^ k, c) if c else (z, y ^ k, x, c))
    for k in (1, 2, 3)
}


def send(value, route):
    return lax.ppermute(value, AXES, route)


def nt(a, b):
    return lax.dot_general(a, b, (((1,), (1,)), ((), ())), preferred_element_type=f32)


def tn(a, b):
    return lax.dot_general(a, b, (((0,), (0,)), ((), ())), preferred_element_type=f32)


def nn(a, b):
    return jnp.dot(a, b, preferred_element_type=f32)


def widen(a):
    return a.astype(f32)


def after(value, others):
    return lax.optimization_barrier((value, others))[0]


def project_kernel(n, *refs):
    rows, weights, out = refs[:n], refs[n : n + 4], refs[n + 4]
    for i in range(WIDTH // TILE):
        tile = slice(i * TILE, (i + 1) * TILE)
        x = jnp.concatenate([r[:, tile] for r in rows], axis=0)
        w = jnp.concatenate([r[:, tile] for r in weights], axis=0)
        if i == 0:
            out[...] = nt(w, x)
        else:
            out[...] += nt(w, x)


def down_kernel(n, n_out, place, *refs):
    rows = refs[:n]
    acc, down_w, down_w2, seconds, theirs = refs[n : n + 5]
    if place is None:
        first, second = refs[n + 5 : n + 7]
    else:
        sources = refs[n + 5 : n + 7]
        first, second = refs[n + 7 + n_out : n + 9 + n_out]
    outs = refs[n + 7 : n + 7 + n_out]
    hidden = refs[-1]

    def shards_of(learner, to, groups, base):
        if place is None:
            return
        zh, y, x = learner // 16, (learner // 4) % 4, learner % 4
        dz, dy, dx = zh ^ place[0], y ^ place[1], x ^ place[2]
        for other, src in enumerate(sources):
            along_x = (place[3] ^ other) == 0
            near = jnp.where(along_x, dx, dy)
            far = jnp.where(along_x, dy, dx)
            r = pl.ds(pl.multiple_of((far * 4 + near) * 16, 16), 16)
            for k in range(groups):
                at = pl.multiple_of((base + k) * 512 + dz * 256, 256)
                row = (place[3] ^ other) * 32 + (k // 2) * 64 + (k % 2) * 16
                row = pl.ds(pl.multiple_of(row, 16), 16)
                to[row, learner * 256 : learner * 256 + 256] = src[r, pl.ds(at, 256)]

    low = 0.0
    for i in range(STEPS):
        tile = slice(i * TILE, (i + 1) * TILE)
        for j in range(PARTS):
            shards_of(i * PARTS + j, first, 4, 0)
        x = jnp.concatenate([r[:, tile] for r in rows], axis=0)
        low += nt(first[:, tile], x)

    u = (adapter_scale * low).astype(bf16)
    hs, back = [], 0.0
    for half, (ref, c) in enumerate(((seconds, 0), (theirs, 3072))):
        b = [ref[64 * k : 64 * k + 64, c : c + UNITS] for k in range(3)]
        at = half * UNITS
        g = acc[at : at + UNITS] + tn(b[0], u[:64])
        at += 2 * UNITS
        v = acc[at : at + UNITS] + tn(b[1], u[64:])
        h = g / (1.0 + jnp.exp(-g)) * v
        back += nn(b[2], h.astype(bf16))
        hs.append(h)
    h = jnp.concatenate([*hs, adapter_scale * back], axis=0)
    hidden[...] = h.T.astype(bf16)

    for i in range(STEPS):
        tile = slice(i * TILE, (i + 1) * TILE)
        for j in range(PARTS):
            shards_of(i * PARTS + j, second, 2, 4)
        w = jnp.concatenate([r[:, tile] for r in (down_w, down_w2, second)], axis=0)
        result = nn(hidden[...], w)
        for k, out in enumerate(outs):
            out[:, tile] = result[k * 64 : (k + 1) * 64].astype(out.dtype)


VMEM = pl.BlockSpec(memory_space=pltpu.VMEM)
SMEM = pl.BlockSpec(memory_space=pltpu.SMEM)


def in_vmem(operands):
    return [pltpu.with_memory_space_constraint(a, pltpu.VMEM) for a in operands]


def price_of(us):
    return pl.CostEstimate(
        flops=int(us * 1.15e9), bytes_accessed=int(us * 3.6e6), transcendentals=0
    )


def project(rows, weights, *extra):
    n, more = len(rows), len(extra)
    return pl.pallas_call(
        lambda *refs: project_kernel(n, *refs[more:]),
        in_specs=[VMEM] * (more + n + 4),
        out_specs=VMEM,
        out_shape=jax.ShapeDtypeStruct((4 * UNITS, sum(r.shape[0] for r in rows)), f32),
        compiler_params=pltpu.CompilerParams(vmem_limit_bytes=10 * 1024 * 1024),
        cost_estimate=price_of(CK),
    )(*extra, *in_vmem([*rows, *weights]))


def down(place, rows, acc, weights, seconds, factors, kinds):
    n = len(rows)
    theirs = factors[1] if place is not None else seconds[1]
    operands = in_vmem([*rows, acc, *weights, seconds[0], theirs, *factors])
    shapes = [((64, WIDTH), kind) for kind in kinds]
    lead = []
    n_out = len(kinds)
    body = lambda *refs: down_kernel(n, n_out, None, *refs)
    if place is not None:
        lead = [place]
        body = lambda *refs: down_kernel(n, n_out, *refs)
        shapes += [((128, WIDTH), bf16), ((64, WIDTH), bf16)]
    return pl.pallas_call(
        body,
        in_specs=[SMEM] * len(lead) + [VMEM] * len(operands),
        out_specs=[VMEM] * len(shapes),
        out_shape=[jax.ShapeDtypeStruct(s, kind) for s, kind in shapes],
        scratch_shapes=[pltpu.VMEM((64 * n_out, 512), bf16)],
        compiler_params=pltpu.CompilerParams(vmem_limit_bytes=10 * 1024 * 1024),
        cost_estimate=SMALL,
    )(*lead, *operands)


def local(body, shapes, operands, place=None, price=SMALL, far=(), scratch=()):
    lead = [] if place is None else [place]
    return pl.pallas_call(
        body,
        in_specs=[SMEM] * len(lead)
        + [VMEM] * len(operands)
        + [pl.BlockSpec(memory_space=pltpu.HBM)] * len(far),
        out_specs=[VMEM] * len(shapes),
        out_shape=[jax.ShapeDtypeStruct(s, kind) for s, kind in shapes],
        scratch_shapes=list(scratch),
        compiler_params=pltpu.CompilerParams(vmem_limit_bytes=6 * 1024 * 1024),
        cost_estimate=price,
    )(*lead, *operands, *(pltpu.with_memory_space_constraint(a, pltpu.HBM) for a in far))


def begin_kernel(place, inputs, gate, up, down, own, other, factor, ranks, sems):
    c = place[3]
    half = pl.ds(pl.multiple_of(c * 32, 32), 32)
    copies = [pltpu.make_async_copy(inputs.at[c], own, sems.at[0])]
    copies += [pltpu.make_async_copy(inputs.at[1 - c], other, sems.at[1])]
    for k, r in enumerate((gate, up, down)):
        copies += [pltpu.make_async_copy(r.at[half, :], ranks.at[k], sems.at[2 + k])]
    for copy in copies:
        copy.start()
    for copy in copies:
        copy.wait()
    for i in range(6):
        col = slice(256 * i, 256 * i + 256)
        factor[:, col] = ranks[i // 2, (i % 2) * 16 : (i % 2) * 16 + 16, :]


def shape_kernel(place, own, other, factor, wide, message):
    c = place[3]
    wide[:, pl.ds(pl.multiple_of(c * QUARTER, QUARTER), QUARTER)] = own[...]
    wide[:, pl.ds(pl.multiple_of((1 - c) * QUARTER, QUARTER), QUARTER)] = other[...]
    rows = widen(wide[...])
    rows = jnp.concatenate([rows[:, :QUARTER], rows[:, QUARTER:]], axis=0)
    message[:, :QUARTER] = rows.astype(bf16)
    message[:, QUARTER:] = factor[...]


def pack_kernel(place, wide, z1, z2, message, far_message, out):
    zl = place[4]
    here = pl.ds(pl.multiple_of(zl * HALF, HALF), HALF)
    there = pl.ds(pl.multiple_of((1 - zl) * HALF, HALF), HALF)
    z3 = widen(far_message[:, :QUARTER])
    z3 = jnp.concatenate([z3[:8], z3[8:]], axis=1)
    pair = lambda a, b: jnp.concatenate([widen(a), widen(b)], 0).astype(bf16)
    out[:, here] = pair(wide[...], z2[...])
    out[:, there] = pair(z1[...], z3)
    for i in range(6):
        at, col = WIDTH + 512 * i, QUARTER + 256 * i
        out[:, at : at + 256] = message[:, col : col + 256]
        out[:, at + 256 : at + 512] = far_message[:, col : col + 256]


def unpack_kernel(own, got1, left, right, got3, block, factor):
    for k, g in ((0, own), (1, got1), (3, got3)):
        block[16 * k : 16 * k + 16, :] = g[:, :WIDTH]
        factor[16 * k : 16 * k + 16, :] = g[:, WIDTH:]
    block[32:48, :CUT] = left[...]
    block[32:48, CUT:] = right[:, : WIDTH - CUT]
    factor[32:48, :] = right[:, WIDTH - CUT :]


def halves_kernel(from1, from3, to1, to3):
    rows, cols = to1.shape
    to1[...] = from3[:rows, :cols]
    to3[...] = from1[-rows:, -cols:]


def relay(from1, from3, routes, shape):
    to1, to3 = local(halves_kernel, [(shape, bf16)] * 2, (from1, from3))
    return send(to1, routes[1]), send(to3, routes[3])


def touch_kernel(gate_w, up_w, down_w, out):
    out[...] = jnp.zeros_like(out)


def seconds_kernel(gate, up, down, out):
    out[...] = jnp.zeros_like(out)
    for k, r in enumerate((gate, up, down)):
        out[64 * k : 64 * k + 64, :UNITS] = r[...]


def stack_kernel(f0, f1, f2, f2b, f3, seconds, out):
    for at, r in ((0, f0), (64, f1), (128, f2), (160, f2b), (192, f3)):
        out[at : at + r.shape[0], :3072] = r[...]
    out[:, 3072:] = seconds[...]


def add_kernel(own, b1, b3, out):
    out[...] = own[...] + widen(b1[...]) + widen(b3[...])


def sum_kernel(own, b, keep, s1, s2, s3):
    for k, out in enumerate((keep, s1, s2, s3)):
        part = slice(16 * k, 16 * k + 16)
        out[...] = (own[part, :] + widen(b[part, :])).astype(out.dtype)


def split_kernel(place, own, b1, b2, b3, keep, s1, s2, s3):
    zl = place[4]
    here = pl.ds(pl.multiple_of(zl * HALF, HALF), HALF)
    there = pl.ds(pl.multiple_of((1 - zl) * HALF, HALF), HALF)
    for cols, near, far in ((here, keep, s2), (there, s1, s3)):
        total = own[:, cols]
        for b in (b1, b2, b3):
            total += widen(b[:, cols])
        near[...] = total[:8].astype(near.dtype)
        far[...] = total[8:].astype(far.dtype)


def shards(
    inputs,
    frozen_gate_weight,
    frozen_up_weight,
    frozen_down_weight,
    adapter_first_gate,
    adapter_second_gate,
    adapter_first_up,
    adapter_second_up,
    adapter_first_down,
    adapter_second_down,
):
    zh, y, x, zl, c = (lax.axis_index(a) for a in AXES)
    place = jnp.stack([zh, y, x, c, zl]).astype(jnp.int32)

    def ordered(flag, a, b, axis):
        return jnp.where(
            flag == 0, jnp.concatenate([a, b], axis), jnp.concatenate([b, a], axis)
        )

    own, other, factor = local(
        begin_kernel,
        [((8, QUARTER), bf16), ((8, QUARTER), bf16), ((16, 1536), bf16)],
        (),
        place,
        far=(inputs, adapter_first_gate, adapter_first_up, adapter_second_down),
        scratch=[pltpu.VMEM((3, 32, 256), bf16), pltpu.SemaphoreType.DMA((5,))],
    )
    other = send(other, CORE)
    wide, message = local(
        shape_kernel,
        [((8, HALF), bf16), ((16, QUARTER + 1536), bf16)],
        (own, other, factor),
        place,
    )

    z1, z2, z3 = (
        send(v, ALONG_Z[k]) for k, v in ((1, wide), (2, wide), (3, message))
    )
    gate2 = send(after(frozen_gate_weight, wide), CORE)
    up2 = send(after(frozen_up_weight, wide), CORE)
    (packed,) = local(
        pack_kernel, [((16, WIDTH + 3072), bf16)], (wide, z1, z2, message, z3), place
    )

    packed = after(packed, gate2)
    got1, got3 = send(packed, FIRST[1]), send(packed, FIRST[3])
    got = relay(got1, got3, FIRST, (16, CUT))
    seconds = (adapter_second_gate, adapter_second_up, adapter_first_down)
    (seconds,) = local(
        seconds_kernel, [((256, 256), bf16)], [a.T for a in after(seconds, packed)]
    )
    block, factor = local(
        unpack_kernel,
        [((64, WIDTH), bf16), ((64, 3072), bf16)],
        (packed, got1, *got, got3),
    )

    block, factor = after((block, factor), (up2, seconds))
    near1, near3 = send(factor, SECOND[1]), send(factor, SECOND[3])
    rows1, rows3 = send(block, SECOND[1]), send(block, SECOND[3])
    frozen = (frozen_gate_weight, frozen_up_weight, frozen_down_weight)
    owned = after(frozen, block)
    down2 = send(owned[2], CORE)
    far = relay(near1, near3, SECOND, (32, 3072))
    (factor,) = local(
        stack_kernel, [((256, 3072 + 256), bf16)], (factor, near1, *far, near3, seconds)
    )
    factor2 = send(factor, CORE)
    rows2 = relay(rows1, rows3, SECOND, (32, WIDTH))
    (touched,) = local(touch_kernel, [((8, 128), f32)], in_vmem(owned))

    weights = (owned[0], gate2, owned[1], up2)
    down_weights = (owned[2], down2)

    rows = (block, rows1, rows3)
    acc = project(rows, weights, touched)
    total, part1, part3, first, second = down(
        place, rows, acc, down_weights, (seconds, factor2), (factor, factor2),
        (f32, bf16, bf16),
    )
    back1, back3 = send(part1, SECOND[1]), send(part3, SECOND[3])
    rows = after(rows2, part1)
    acc = project(rows, weights)
    (part2,) = down(
        None, rows, acc, down_weights, (seconds, factor2), (first, second), (bf16,)
    )
    back2 = send(part2, SECOND[2])
    (total,) = local(
        add_kernel,
        [((64, WIDTH), f32)],
        (total, back1, back3),
        price=price_of(4.5),
    )
    small = [((16, WIDTH), f32)] + [((16, WIDTH), bf16)] * 3
    mine, *parts = local(sum_kernel, small, (total, back2))
    backs = [send(p, FIRST[k]) for k, p in zip((1, 2, 3), parts, strict=True)]
    small = [((8, HALF), f32)] + [((8, HALF), bf16)] * 3
    done, *parts = local(split_kernel, small, (mine, *backs), place)
    for k, p in zip((1, 2, 3), parts, strict=True):
        done = done + widen(send(p, ALONG_Z[k]))
    done = done.astype(bf16)
    keep = jnp.where(c == 0, done[:, :2048], done[:, 2048:])
    give = jnp.where(c == 0, done[:, 2048:], done[:, :2048])
    got = send(give, CORE)
    return ordered(c, keep[None], got[None], 0)


def solution(mesh):
    fine = Mesh(mesh.devices.reshape(SIZES), AXES)
    learner, tensor = ("zh", "y", "x"), ("zl", "c")
    in_specs = (
        P(None, learner, tensor),
        P(AXES, None),
        P(AXES, None),
        P(AXES, None),
        P(None, learner),
        P(AXES, None),
        P(None, learner),
        P(AXES, None),
        P(AXES, None),
        P(None, learner),
    )
    return jax.shard_map(
        shards,
        mesh=fine,
        in_specs=in_specs,
        out_specs=P(None, learner, tensor),
        check_vma=False,
    )
```

```python
import itertools

import jax
import jax.numpy as jnp
from jax import lax
from jax.experimental import pallas as pl
from jax.experimental.pallas import tpu as pltpu
from jax.sharding import Mesh, PartitionSpec as P

AXES = ("zh", "y", "x", "zl", "c")
SIZES = (2, 4, 4, 2, 2)
adapter_scale = 0.5
WIDTH = 8192
HALF = WIDTH // 2
QUARTER = WIDTH // 4
UNITS = 224
TILE = 4096
STEPS = WIDTH // TILE
PARTS = TILE // 256
f32, bf16 = jnp.float32, jnp.bfloat16
CK = 8
SMALL = pl.CostEstimate(flops=1, bytes_accessed=1, transcendentals=0)


def index(zh, y, x, zl, c):
    return (((zh * 4 + y) * 4 + x) * 2 + zl) * 2 + c


def pairs(partner):
    out = []
    for zh, y, x, zl, c in itertools.product(*map(range, SIZES)):
        z, y2, x2, c2 = partner(zh * 2 + zl, y, x, c)
        out.append((index(zh, y, x, zl, c), index(z >> 1, y2, x2, z & 1, c2)))
    return out


CORE = pairs(lambda z, y, x, c: (z, y, x, 1 - c))
ALONG_Z = {k: pairs(lambda z, y, x, c: (z ^ k, y, x, c)) for k in (1, 2, 3)}
FIRST = {
    k: pairs(lambda z, y, x, c: (z, y ^ k, x, c) if c else (z, y, x ^ k, c))
    for k in (1, 2, 3)
}
SECOND = {
    k: pairs(lambda z, y, x, c: (z, y, x ^ k, c) if c else (z, y ^ k, x, c))
    for k in (1, 2, 3)
}


def send(value, route):
    return lax.ppermute(value, AXES, route)


def nt(a, b):
    return lax.dot_general(a, b, (((1,), (1,)), ((), ())), preferred_element_type=f32)


def tn(a, b):
    return lax.dot_general(a, b, (((0,), (0,)), ((), ())), preferred_element_type=f32)


def nn(a, b):
    return jnp.dot(a, b, preferred_element_type=f32)


def widen(a):
    return a.astype(f32)


def after(value, others):
    return lax.optimization_barrier((value, others))[0]


def project_kernel(n, *refs):
    rows, weights, out = refs[:n], refs[n : n + 4], refs[n + 4]
    for i in range(WIDTH // TILE):
        tile = slice(i * TILE, (i + 1) * TILE)
        x = jnp.concatenate([r[:, tile] for r in rows], axis=0)
        w = jnp.concatenate([r[:, tile] for r in weights], axis=0)
        if i == 0:
            out[...] = nt(w, x)
        else:
            out[...] += nt(w, x)


def down_kernel(n, n_out, place, *refs):
    rows, refs = refs[:n], refs[n:]
    if place is None:
        weights, refs = refs[:4], refs[4:]
    else:
        acc, refs = refs[0], refs[1:]
    down_w, down_w2, seconds, theirs = refs[:4]
    if place is None:
        first, second = refs[4:6]
    else:
        sources = refs[4:6]
        first, second = refs[6 + n_out : 8 + n_out]
    outs = refs[6 : 6 + n_out]
    hidden = refs[-1]

    def shards_of(learner, to, groups, base):
        if place is None:
            return
        zh, y, x = learner // 16, (learner // 4) % 4, learner % 4
        dz, dy, dx = zh ^ place[0], y ^ place[1], x ^ place[2]
        for other, src in enumerate(sources):
            along_x = (place[3] ^ other) == 0
            near = jnp.where(along_x, dx, dy)
            far = jnp.where(along_x, dy, dx)
            r = pl.ds(pl.multiple_of((far * 4 + near) * 16, 16), 16)
            for k in range(groups):
                at = pl.multiple_of((base + k) * 512 + dz * 256, 256)
                row = (place[3] ^ other) * 32 + (k // 2) * 64 + (k % 2) * 16
                row = pl.ds(pl.multiple_of(row, 16), 16)
                to[row, learner * 256 : learner * 256 + 256] = src[r, pl.ds(at, 256)]

    low = 0.0
    for i in range(STEPS):
        tile = slice(i * TILE, (i + 1) * TILE)
        for j in range(PARTS):
            shards_of(i * PARTS + j, first, 4, 0)
        x = jnp.concatenate([r[:, tile] for r in rows], axis=0)
        if place is None:
            low += nt(jnp.concatenate([r[:, tile] for r in (*weights, first)], axis=0), x)
        else:
            low += nt(first[:, tile], x)

    if place is None:
        acc, low = low[: 4 * UNITS], low[4 * UNITS :]
    u = (adapter_scale * low).astype(bf16)
    hs, back = [], 0.0
    for half, (ref, c) in enumerate(((seconds, 0), (theirs, 3072))):
        b = [ref[64 * k : 64 * k + 64, c : c + UNITS] for k in range(3)]
        at = half * UNITS
        g = acc[at : at + UNITS] + tn(b[0], u[:64])
        at += 2 * UNITS
        v = acc[at : at + UNITS] + tn(b[1], u[64:])
        h = g / (1.0 + jnp.exp(-g)) * v
        back += nn(b[2], h.astype(bf16))
        hs.append(h)
    h = jnp.concatenate([*hs, adapter_scale * back], axis=0)
    hidden[...] = h.T.astype(bf16)

    for i in range(STEPS):
        tile = slice(i * TILE, (i + 1) * TILE)
        for j in range(PARTS):
            shards_of(i * PARTS + j, second, 2, 4)
        w = jnp.concatenate([r[:, tile] for r in (down_w, down_w2, second)], axis=0)
        result = nn(hidden[...], w)
        for k, out in enumerate(outs):
            out[:, tile] = result[k * 64 : (k + 1) * 64].astype(out.dtype)


VMEM = pl.BlockSpec(memory_space=pltpu.VMEM)
SMEM = pl.BlockSpec(memory_space=pltpu.SMEM)


def in_vmem(operands):
    return [pltpu.with_memory_space_constraint(a, pltpu.VMEM) for a in operands]


def price_of(us):
    return pl.CostEstimate(
        flops=int(us * 1.15e9), bytes_accessed=int(us * 3.6e6), transcendentals=0
    )


def project(rows, weights, *extra):
    n, more = len(rows), len(extra)
    return pl.pallas_call(
        lambda *refs: project_kernel(n, *refs[more:]),
        in_specs=[VMEM] * (more + n + 4),
        out_specs=VMEM,
        out_shape=jax.ShapeDtypeStruct((4 * UNITS, sum(r.shape[0] for r in rows)), f32),
        compiler_params=pltpu.CompilerParams(vmem_limit_bytes=10 * 1024 * 1024),
        cost_estimate=price_of(CK),
    )(*extra, *in_vmem([*rows, *weights]))


def down(place, rows, lead_in, weights, seconds, factors, kinds):
    n = len(rows)
    theirs = factors[1] if place is not None else seconds[1]
    operands = in_vmem([*rows, *lead_in, *weights, seconds[0], theirs, *factors])
    shapes = [((64, WIDTH), kind) for kind in kinds]
    lead = []
    n_out = len(kinds)
    body = lambda *refs: down_kernel(n, n_out, None, *refs)
    if place is not None:
        lead = [place]
        body = lambda *refs: down_kernel(n, n_out, *refs)
        shapes += [((128, WIDTH), bf16), ((64, WIDTH), bf16)]
    return pl.pallas_call(
        body,
        in_specs=[SMEM] * len(lead) + [VMEM] * len(operands),
        out_specs=[VMEM] * len(shapes),
        out_shape=[jax.ShapeDtypeStruct(s, kind) for s, kind in shapes],
        scratch_shapes=[pltpu.VMEM((64 * n_out, 512), bf16)],
        compiler_params=pltpu.CompilerParams(vmem_limit_bytes=10 * 1024 * 1024),
        cost_estimate=SMALL,
    )(*lead, *operands)


def local(body, shapes, operands, place=None, price=SMALL, far=(), scratch=()):
    lead = [] if place is None else [place]
    return pl.pallas_call(
        body,
        in_specs=[SMEM] * len(lead)
        + [VMEM] * len(operands)
        + [pl.BlockSpec(memory_space=pltpu.HBM)] * len(far),
        out_specs=[VMEM] * len(shapes),
        out_shape=[jax.ShapeDtypeStruct(s, kind) for s, kind in shapes],
        scratch_shapes=list(scratch),
        compiler_params=pltpu.CompilerParams(vmem_limit_bytes=6 * 1024 * 1024),
        cost_estimate=price,
    )(*lead, *operands, *(pltpu.with_memory_space_constraint(a, pltpu.HBM) for a in far))


def begin_kernel(place, inputs, gate, up, down, own, other, factor, ranks, sems):
    c = place[3]
    half = pl.ds(pl.multiple_of(c * 32, 32), 32)
    copies = [pltpu.make_async_copy(inputs.at[c], own, sems.at[0])]
    copies += [pltpu.make_async_copy(inputs.at[1 - c], other, sems.at[1])]
    for k, r in enumerate((gate, up, down)):
        copies += [pltpu.make_async_copy(r.at[half, :], ranks.at[k], sems.at[2 + k])]
    for copy in copies:
        copy.start()
    for copy in copies:
        copy.wait()
    for i in range(6):
        col = slice(256 * i, 256 * i + 256)
        factor[:, col] = ranks[i // 2, (i % 2) * 16 : (i % 2) * 16 + 16, :]


def shape_kernel(place, own, other, factor, wide, message):
    c = place[3]
    wide[:, pl.ds(pl.multiple_of(c * QUARTER, QUARTER), QUARTER)] = own[...]
    wide[:, pl.ds(pl.multiple_of((1 - c) * QUARTER, QUARTER), QUARTER)] = other[...]
    rows = widen(wide[...])
    rows = jnp.concatenate([rows[:, :QUARTER], rows[:, QUARTER:]], axis=0)
    message[:, :QUARTER] = rows.astype(bf16)
    message[:, QUARTER:] = factor[...]


def pack_kernel(place, wide, z1, z2, message, far_message, out):
    zl = place[4]
    here = pl.ds(pl.multiple_of(zl * HALF, HALF), HALF)
    there = pl.ds(pl.multiple_of((1 - zl) * HALF, HALF), HALF)
    z3 = widen(far_message[:, :QUARTER])
    z3 = jnp.concatenate([z3[:8], z3[8:]], axis=1)
    pair = lambda a, b: jnp.concatenate([widen(a), widen(b)], 0).astype(bf16)
    out[:, here] = pair(wide[...], z2[...])
    out[:, there] = pair(z1[...], z3)
    for i in range(6):
        at, col = WIDTH + 512 * i, QUARTER + 256 * i
        out[:, at : at + 256] = message[:, col : col + 256]
        out[:, at + 256 : at + 512] = far_message[:, col : col + 256]


def unpack_kernel(own, got2, got1, got3, block, factor, packed):
    for k, g in enumerate((own, got1, got2, got3)):
        at = slice(16 * k, 16 * k + 16)
        block[at, :] = g[:, :WIDTH]
        factor[at, :] = g[:, WIDTH:]
        packed[at, :] = g[...]


def rows_kernel(rows, out):
    out[...] = rows[...]


def halves_kernel(from1, from3, to1, to3):
    to1[...] = from3[:32, :WIDTH]
    to3[...] = from1[32:, :WIDTH]


def relay(from1, from3, routes, shape):
    to1, to3 = local(halves_kernel, [(shape, bf16)] * 2, (from1, from3))
    return send(to1, routes[1]), send(to3, routes[3])


def touch_kernel(gate_w, up_w, down_w, out):
    out[...] = jnp.zeros_like(out)


def seconds_kernel(gate, up, down, out):
    out[...] = jnp.zeros_like(out)
    for k, r in enumerate((gate, up, down)):
        out[64 * k : 64 * k + 64, :UNITS] = r[...]


def stack_kernel(f0, packed1, f2, packed3, seconds, out):
    for k, r in enumerate((f0, packed1, f2, packed3)):
        out[64 * k : 64 * k + 64, :3072] = r[:, -3072:]
    out[:, 3072:] = seconds[...]


def add_kernel(own, b1, b3, out):
    out[...] = own[...] + widen(b1[...]) + widen(b3[...])


def sum_kernel(own, b, keep, s1, s2, s3):
    for k, out in enumerate((keep, s1, s2, s3)):
        part = slice(16 * k, 16 * k + 16)
        out[...] = (own[part, :] + widen(b[part, :])).astype(out.dtype)


def split_kernel(place, own, b1, b2, b3, keep, s1, s2, s3):
    zl = place[4]
    here = pl.ds(pl.multiple_of(zl * HALF, HALF), HALF)
    there = pl.ds(pl.multiple_of((1 - zl) * HALF, HALF), HALF)
    for cols, near, far in ((here, keep, s2), (there, s1, s3)):
        total = own[:, cols]
        for b in (b1, b2, b3):
            total += widen(b[:, cols])
        near[...] = total[:8].astype(near.dtype)
        far[...] = total[8:].astype(far.dtype)


def shards(
    inputs,
    frozen_gate_weight,
    frozen_up_weight,
    frozen_down_weight,
    adapter_first_gate,
    adapter_second_gate,
    adapter_first_up,
    adapter_second_up,
    adapter_first_down,
    adapter_second_down,
):
    zh, y, x, zl, c = (lax.axis_index(a) for a in AXES)
    place = jnp.stack([zh, y, x, c, zl]).astype(jnp.int32)

    def ordered(flag, a, b, axis):
        return jnp.where(
            flag == 0, jnp.concatenate([a, b], axis), jnp.concatenate([b, a], axis)
        )

    own, other, factor = local(
        begin_kernel,
        [((8, QUARTER), bf16), ((8, QUARTER), bf16), ((16, 1536), bf16)],
        (),
        place,
        far=(inputs, adapter_first_gate, adapter_first_up, adapter_second_down),
        scratch=[pltpu.VMEM((3, 32, 256), bf16), pltpu.SemaphoreType.DMA((5,))],
    )
    other = send(other, CORE)
    wide, message = local(
        shape_kernel,
        [((8, HALF), bf16), ((16, QUARTER + 1536), bf16)],
        (own, other, factor),
        place,
    )

    z1, z2, z3 = (
        send(v, ALONG_Z[k]) for k, v in ((1, wide), (2, wide), (3, message))
    )
    gate2 = send(after(frozen_gate_weight, wide), CORE)
    up2 = send(after(frozen_up_weight, wide), CORE)
    (packed,) = local(
        pack_kernel, [((16, WIDTH + 3072), bf16)], (wide, z1, z2, message, z3), place
    )

    packed = after(packed, gate2)
    got = {k: send(packed, FIRST[k]) for k in (1, 2, 3)}
    seconds = (adapter_second_gate, adapter_second_up, adapter_first_down)
    (seconds,) = local(
        seconds_kernel, [((256, 256), bf16)], [a.T for a in after(seconds, packed)]
    )
    block, factor, packed = local(
        unpack_kernel,
        [((64, WIDTH), bf16), ((64, 3072), bf16), ((64, WIDTH + 3072), bf16)],
        (packed, got[2], got[1], got[3]),
    )

    block, factor, packed = after((block, factor, packed), (up2, seconds))
    far = send(factor, SECOND[2])
    packed1, packed3 = send(packed, SECOND[1]), send(packed, SECOND[3])
    frozen = (frozen_gate_weight, frozen_up_weight, frozen_down_weight)
    owned = after(frozen, block)
    down2 = send(owned[2], CORE)
    (far,) = local(rows_kernel, [((64, 3072), bf16)], (far,), price=price_of(11))
    (factor,) = local(
        stack_kernel, [((256, 3072 + 256), bf16)], (factor, packed1, far, packed3, seconds)
    )
    factor2 = send(factor, CORE)
    rows2 = relay(packed1, packed3, SECOND, (32, WIDTH))
    (touched,) = local(touch_kernel, [((8, 128), f32)], in_vmem(owned))

    weights = (owned[0], gate2, owned[1], up2)
    down_weights = (owned[2], down2)

    rows = (block, packed1, packed3)
    acc = project(rows, weights, touched)
    total, part1, part3, first, second = down(
        place, rows, (acc,), down_weights, (seconds, factor2), (factor, factor2),
        (f32, bf16, bf16),
    )
    back1, back3 = send(part1, SECOND[1]), send(part3, SECOND[3])
    (part2,) = down(
        None, after(rows2, part1), weights, down_weights, (seconds, factor2),
        (first, second), (bf16,),
    )
    back2 = send(part2, SECOND[2])
    (total,) = local(
        add_kernel,
        [((64, WIDTH), f32)],
        (total, back1, back3),
        price=price_of(4.5),
    )
    small = [((16, WIDTH), f32)] + [((16, WIDTH), bf16)] * 3
    mine, *parts = local(sum_kernel, small, (total, back2))
    backs = [send(p, FIRST[k]) for k, p in zip((1, 2, 3), parts, strict=True)]
    small = [((8, HALF), f32)] + [((8, HALF), bf16)] * 3
    done, *parts = local(split_kernel, small, (mine, *backs), place)
    for k, p in zip((1, 2, 3), parts, strict=True):
        done = done + widen(send(p, ALONG_Z[k]))
    done = done.astype(bf16)
    keep = jnp.where(c == 0, done[:, :2048], done[:, 2048:])
    give = jnp.where(c == 0, done[:, 2048:], done[:, :2048])
    got = send(give, CORE)
    return ordered(c, keep[None], got[None], 0)


def solution(mesh):
    fine = Mesh(mesh.devices.reshape(SIZES), AXES)
    learner, tensor = ("zh", "y", "x"), ("zl", "c")
    in_specs = (
        P(None, learner, tensor),
        P(AXES, None),
        P(AXES, None),
        P(AXES, None),
        P(None, learner),
        P(AXES, None),
        P(None, learner),
        P(AXES, None),
        P(AXES, None),
        P(None, learner),
    )
    return jax.shard_map(
        shards,
        mesh=fine,
        in_specs=in_specs,
        out_specs=P(None, learner, tensor),
        check_vma=False,
    )
```

```python
import itertools

import jax
import jax.numpy as jnp
from jax import lax
from jax.experimental import pallas as pl
from jax.experimental.pallas import tpu as pltpu
from jax.sharding import Mesh, PartitionSpec as P

AXES = ("zh", "y", "x", "zl", "c")
SIZES = (2, 4, 4, 2, 2)
adapter_scale = 0.5
WIDTH = 8192
HALF = WIDTH // 2
QUARTER = WIDTH // 4
UNITS = 224
TILE = 4096
STEPS = WIDTH // TILE
PARTS = TILE // 256
f32, bf16 = jnp.float32, jnp.bfloat16
CK = 8
SMALL = pl.CostEstimate(flops=1, bytes_accessed=1, transcendentals=0)


def index(zh, y, x, zl, c):
    return (((zh * 4 + y) * 4 + x) * 2 + zl) * 2 + c


def pairs(partner):
    out = []
    for zh, y, x, zl, c in itertools.product(*map(range, SIZES)):
        z, y2, x2, c2 = partner(zh * 2 + zl, y, x, c)
        out.append((index(zh, y, x, zl, c), index(z >> 1, y2, x2, z & 1, c2)))
    return out


CORE = pairs(lambda z, y, x, c: (z, y, x, 1 - c))
ALONG_Z = {k: pairs(lambda z, y, x, c: (z ^ k, y, x, c)) for k in (1, 2, 3)}
FIRST = {
    k: pairs(lambda z, y, x, c: (z, y ^ k, x, c) if c else (z, y, x ^ k, c))
    for k in (1, 2, 3)
}
SECOND = {
    k: pairs(lambda z, y, x, c: (z, y, x ^ k, c) if c else (z, y ^ k, x, c))
    for k in (1, 2, 3)
}


def send(value, route):
    return lax.ppermute(value, AXES, route)


def nt(a, b):
    return lax.dot_general(a, b, (((1,), (1,)), ((), ())), preferred_element_type=f32)


def tn(a, b):
    return lax.dot_general(a, b, (((0,), (0,)), ((), ())), preferred_element_type=f32)


def nn(a, b):
    return jnp.dot(a, b, preferred_element_type=f32)


def widen(a):
    return a.astype(f32)


def after(value, others):
    return lax.optimization_barrier((value, others))[0]


def project_kernel(n, *refs):
    rows, weights, out = refs[:n], refs[n : n + 4], refs[n + 4]
    for i in range(WIDTH // TILE):
        tile = slice(i * TILE, (i + 1) * TILE)
        x = jnp.concatenate([r[:, tile] for r in rows], axis=0)
        w = jnp.concatenate([r[:, tile] for r in weights], axis=0)
        if i == 0:
            out[...] = nt(w, x)
        else:
            out[...] += nt(w, x)


def shard_homes(place):
    out = []
    for other in range(2):
        along_x = (place[3] ^ other) == 0
        cols = [
            [pl.ds(pl.multiple_of(g * 512 + (zh ^ place[0]) * 256, 256), 256) for zh in (0, 1)]
            for g in range(6)
        ]
        rows_at = []
        for y in range(4):
            for x in range(4):
                dy, dx = y ^ place[1], x ^ place[2]
                row = jnp.where(along_x, dy * 64 + dx * 16, dx * 64 + dy * 16)
                rows_at.append(pl.ds(pl.multiple_of(row, 16), 16))
        rank = (place[3] ^ other) * 32
        to_at = [
            pl.ds(pl.multiple_of(rank + (k // 2) * 64 + (k % 2) * 16, 16), 16)
            for k in range(4)
        ]
        out.append((cols, rows_at, to_at))
    return out


def down_kernel(n, n_out, place, *refs):
    rows = refs[:n]
    acc, down_w, down_w2, seconds, theirs = refs[n : n + 5]
    if place is None:
        first, second = refs[n + 5 : n + 7]
    else:
        sources = refs[n + 5 : n + 7]
        first, second = refs[n + 7 + n_out : n + 9 + n_out]
        homes = shard_homes(place)
    outs = refs[n + 7 : n + 7 + n_out]
    hidden = refs[-1]

    def shards_of(learner, to, groups, base):
        if place is None:
            return
        for other, src in enumerate(sources):
            cols, rows_at, to_at = homes[other]
            for k in range(groups):
                piece = src[rows_at[learner % 16], cols[base + k][learner // 16]]
                to[to_at[k], learner * 256 : learner * 256 + 256] = piece

    low = 0.0
    for i in range(STEPS):
        tile = slice(i * TILE, (i + 1) * TILE)
        for j in range(PARTS):
            shards_of(i * PARTS + j, first, 4, 0)
        x = jnp.concatenate([r[:, tile] for r in rows], axis=0)
        low += nt(first[:, tile], x)

    u = (adapter_scale * low).astype(bf16)
    hs, back = [], 0.0
    for half, (ref, c) in enumerate(((seconds, 0), (theirs, 3072))):
        b = [ref[64 * k : 64 * k + 64, c : c + UNITS] for k in range(3)]
        at = half * UNITS
        g = acc[at : at + UNITS] + tn(b[0], u[:64])
        at += 2 * UNITS
        v = acc[at : at + UNITS] + tn(b[1], u[64:])
        h = g / (1.0 + jnp.exp(-g)) * v
        back += nn(b[2], h.astype(bf16))
        hs.append(h)
    h = jnp.concatenate([*hs, adapter_scale * back], axis=0)
    hidden[...] = h.T.astype(bf16)

    for i in range(STEPS):
        tile = slice(i * TILE, (i + 1) * TILE)
        for j in range(PARTS):
            shards_of(i * PARTS + j, second, 2, 4)
        w = jnp.concatenate([r[:, tile] for r in (down_w, down_w2, second)], axis=0)
        result = nn(hidden[...], w)
        for k, out in enumerate(outs):
            out[:, tile] = result[k * 64 : (k + 1) * 64].astype(out.dtype)


VMEM = pl.BlockSpec(memory_space=pltpu.VMEM)
SMEM = pl.BlockSpec(memory_space=pltpu.SMEM)


def in_vmem(operands):
    return [pltpu.with_memory_space_constraint(a, pltpu.VMEM) for a in operands]


def price_of(us):
    return pl.CostEstimate(
        flops=int(us * 1.15e9), bytes_accessed=int(us * 3.6e6), transcendentals=0
    )


def project(rows, weights, *extra):
    n, more = len(rows), len(extra)
    return pl.pallas_call(
        lambda *refs: project_kernel(n, *refs[more:]),
        in_specs=[VMEM] * (more + n + 4),
        out_specs=VMEM,
        out_shape=jax.ShapeDtypeStruct((4 * UNITS, sum(r.shape[0] for r in rows)), f32),
        compiler_params=pltpu.CompilerParams(vmem_limit_bytes=10 * 1024 * 1024),
        cost_estimate=price_of(CK),
    )(*extra, *in_vmem([*rows, *weights]))


def down(place, rows, acc, weights, seconds, factors, kinds):
    n = len(rows)
    theirs = factors[1] if place is not None else seconds[1]
    operands = in_vmem([*rows, acc, *weights, seconds[0], theirs, *factors])
    shapes = [((64, WIDTH), kind) for kind in kinds]
    lead = []
    n_out = len(kinds)
    body = lambda *refs: down_kernel(n, n_out, None, *refs)
    if place is not None:
        lead = [place]
        body = lambda *refs: down_kernel(n, n_out, *refs)
        shapes += [((128, WIDTH), bf16), ((64, WIDTH), bf16)]
    return pl.pallas_call(
        body,
        in_specs=[SMEM] * len(lead) + [VMEM] * len(operands),
        out_specs=[VMEM] * len(shapes),
        out_shape=[jax.ShapeDtypeStruct(s, kind) for s, kind in shapes],
        scratch_shapes=[pltpu.VMEM((64 * n_out, 512), bf16)],
        compiler_params=pltpu.CompilerParams(vmem_limit_bytes=10 * 1024 * 1024),
        cost_estimate=SMALL,
    )(*lead, *operands)


def local(body, shapes, operands, place=None, price=SMALL, far=(), scratch=()):
    lead = [] if place is None else [place]
    return pl.pallas_call(
        body,
        in_specs=[SMEM] * len(lead)
        + [VMEM] * len(operands)
        + [pl.BlockSpec(memory_space=pltpu.HBM)] * len(far),
        out_specs=[VMEM] * len(shapes),
        out_shape=[jax.ShapeDtypeStruct(s, kind) for s, kind in shapes],
        scratch_shapes=list(scratch),
        compiler_params=pltpu.CompilerParams(vmem_limit_bytes=6 * 1024 * 1024),
        cost_estimate=price,
    )(*lead, *operands, *(pltpu.with_memory_space_constraint(a, pltpu.HBM) for a in far))


def begin_kernel(place, inputs, gate, up, down, own, other, factor, ranks, sems):
    c = place[3]
    half = pl.ds(pl.multiple_of(c * 32, 32), 32)
    copies = [pltpu.make_async_copy(inputs.at[c], own, sems.at[0])]
    copies += [pltpu.make_async_copy(inputs.at[1 - c], other, sems.at[1])]
    for k, r in enumerate((gate, up, down)):
        copies += [pltpu.make_async_copy(r.at[half, :], ranks.at[k], sems.at[2 + k])]
    for copy in copies:
        copy.start()
    for copy in copies:
        copy.wait()
    for i in range(6):
        col = slice(256 * i, 256 * i + 256)
        factor[:, col] = ranks[i // 2, (i % 2) * 16 : (i % 2) * 16 + 16, :]


def shape_kernel(place, own, other, factor, wide, message):
    c = place[3]
    wide[:, pl.ds(pl.multiple_of(c * QUARTER, QUARTER), QUARTER)] = own[...]
    wide[:, pl.ds(pl.multiple_of((1 - c) * QUARTER, QUARTER), QUARTER)] = other[...]
    rows = widen(wide[...])
    rows = jnp.concatenate([rows[:, :QUARTER], rows[:, QUARTER:]], axis=0)
    message[:, :QUARTER] = rows.astype(bf16)
    message[:, QUARTER:] = factor[...]


def pack_kernel(place, wide, z1, z2, message, far_message, out):
    zl = place[4]
    here = pl.ds(pl.multiple_of(zl * HALF, HALF), HALF)
    there = pl.ds(pl.multiple_of((1 - zl) * HALF, HALF), HALF)
    z3 = widen(far_message[:, :QUARTER])
    z3 = jnp.concatenate([z3[:8], z3[8:]], axis=1)
    pair = lambda a, b: jnp.concatenate([widen(a), widen(b)], 0).astype(bf16)
    out[:, here] = pair(wide[...], z2[...])
    out[:, there] = pair(z1[...], z3)
    for i in range(6):
        at, col = WIDTH + 512 * i, QUARTER + 256 * i
        out[:, at : at + 256] = message[:, col : col + 256]
        out[:, at + 256 : at + 512] = far_message[:, col : col + 256]


def unpack_kernel(own, got2, got1, got3, block, factor, packed):
    for k, g in enumerate((own, got1, got2, got3)):
        at = slice(16 * k, 16 * k + 16)
        block[at, :] = g[:, :WIDTH]
        factor[at, :] = g[:, WIDTH:]
        packed[at, :] = g[...]


def rows_kernel(rows, out):
    out[...] = rows[...]


def halves_kernel(from1, from3, to1, to3):
    to1[...] = from3[:32, :WIDTH]
    to3[...] = from1[32:, :WIDTH]


def relay(from1, from3, routes, shape):
    to1, to3 = local(halves_kernel, [(shape, bf16)] * 2, (from1, from3))
    return send(to1, routes[1]), send(to3, routes[3])


def touch_kernel(gate_w, up_w, down_w, out):
    out[...] = jnp.zeros_like(out)


def seconds_kernel(gate, up, down, out):
    out[...] = jnp.zeros_like(out)
    for k, r in enumerate((gate, up, down)):
        out[64 * k : 64 * k + 64, :UNITS] = r[...]


def stack_kernel(f0, packed1, f2, packed3, seconds, out):
    for k, r in enumerate((f0, packed1, f2, packed3)):
        out[64 * k : 64 * k + 64, :3072] = r[:, -3072:]
    out[:, 3072:] = seconds[...]


def add_kernel(own, b1, b3, out):
    out[...] = own[...] + widen(b1[...]) + widen(b3[...])


def sum_kernel(own, b, keep, s1, s2, s3):
    for k, out in enumerate((keep, s1, s2, s3)):
        part = slice(16 * k, 16 * k + 16)
        out[...] = (own[part, :] + widen(b[part, :])).astype(out.dtype)


def split_kernel(place, own, b2, b1, b3, keep, s1, s2, s3):
    zl = place[4]
    here = pl.ds(pl.multiple_of(zl * HALF, HALF), HALF)
    there = pl.ds(pl.multiple_of((1 - zl) * HALF, HALF), HALF)
    for cols, near, far in ((here, keep, s2), (there, s1, s3)):
        total = own[:, cols]
        for b in (b1, b2, b3):
            total += widen(b[:, cols])
        near[...] = total[:8].astype(near.dtype)
        far[...] = total[8:].astype(far.dtype)


def last_kernel(place, own, b2, b1, b3, keep, give):
    c = place[3]
    for at, out in ((c, keep), (1 - c, give)):
        cols = pl.ds(pl.multiple_of(at * QUARTER, QUARTER), QUARTER)
        total = own[:, cols] + widen(b1[:, cols])
        total += widen(b2[:, cols]) + widen(b3[:, cols])
        out[...] = total.astype(bf16)


def join_kernel(place, keep, got, out):
    c = place[3]
    out[c] = keep[...]
    out[1 - c] = got[...]


def shards(
    inputs,
    frozen_gate_weight,
    frozen_up_weight,
    frozen_down_weight,
    adapter_first_gate,
    adapter_second_gate,
    adapter_first_up,
    adapter_second_up,
    adapter_first_down,
    adapter_second_down,
):
    zh, y, x, zl, c = (lax.axis_index(a) for a in AXES)
    place = jnp.stack([zh, y, x, c, zl]).astype(jnp.int32)

    own, other, factor = local(
        begin_kernel,
        [((8, QUARTER), bf16), ((8, QUARTER), bf16), ((16, 1536), bf16)],
        (),
        place,
        far=(inputs, adapter_first_gate, adapter_first_up, adapter_second_down),
        scratch=[pltpu.VMEM((3, 32, 256), bf16), pltpu.SemaphoreType.DMA((5,))],
    )
    other = send(other, CORE)
    wide, message = local(
        shape_kernel,
        [((8, HALF), bf16), ((16, QUARTER + 1536), bf16)],
        (own, other, factor),
        place,
    )

    z1, z2, z3 = (
        send(v, ALONG_Z[k]) for k, v in ((1, wide), (2, wide), (3, message))
    )
    gate2 = send(after(frozen_gate_weight, wide), CORE)
    up2 = send(after(frozen_up_weight, wide), CORE)
    (packed,) = local(
        pack_kernel, [((16, WIDTH + 3072), bf16)], (wide, z1, z2, message, z3), place
    )

    packed = after(packed, gate2)
    got = {k: send(packed, FIRST[k]) for k in (1, 2, 3)}
    seconds = (adapter_second_gate, adapter_second_up, adapter_first_down)
    (seconds,) = local(
        seconds_kernel, [((256, 256), bf16)], [a.T for a in after(seconds, packed)]
    )
    block, factor, packed = local(
        unpack_kernel,
        [((64, WIDTH), bf16), ((64, 3072), bf16), ((64, WIDTH + 3072), bf16)],
        (packed, got[2], got[1], got[3]),
    )

    block, factor, packed = after((block, factor, packed), (up2, seconds))
    far = send(factor, SECOND[2])
    packed1, packed3 = send(packed, SECOND[1]), send(packed, SECOND[3])
    frozen = (frozen_gate_weight, frozen_up_weight, frozen_down_weight)
    owned = after(frozen, block)
    down2 = send(owned[2], CORE)
    (far,) = local(rows_kernel, [((64, 3072), bf16)], (far,), price=price_of(11))
    (factor,) = local(
        stack_kernel, [((256, 3072 + 256), bf16)], (factor, packed1, far, packed3, seconds)
    )
    factor2 = send(factor, CORE)
    rows2 = relay(packed1, packed3, SECOND, (32, WIDTH))
    (touched,) = local(touch_kernel, [((8, 128), f32)], in_vmem(owned))

    weights = (owned[0], gate2, owned[1], up2)
    down_weights = (owned[2], down2)

    rows = (block, packed1, packed3)
    acc = project(rows, weights, touched)
    total, part1, part3, first, second = down(
        place, rows, acc, down_weights, (seconds, factor2), (factor, factor2),
        (f32, bf16, bf16),
    )
    back1, back3 = send(part1, SECOND[1]), send(part3, SECOND[3])
    rows = after(rows2, part1)
    acc = project(rows, weights)
    (part2,) = down(
        None, rows, acc, down_weights, (seconds, factor2), (first, second), (bf16,)
    )
    back2 = send(part2, SECOND[2])
    (total,) = local(
        add_kernel,
        [((64, WIDTH), f32)],
        (total, back1, back3),
        price=price_of(4.5),
    )
    small = [((16, WIDTH), f32)] + [((16, WIDTH), bf16)] * 3
    mine, *parts = local(sum_kernel, small, (total, back2))
    b1, b2, b3 = (send(p, FIRST[k]) for k, p in zip((1, 2, 3), parts, strict=True))
    small = [((8, HALF), f32)] + [((8, HALF), bf16)] * 3
    done, *parts = local(split_kernel, small, (mine, b2, b1, b3), place)
    b1, b2, b3 = (send(p, ALONG_Z[k]) for k, p in zip((1, 2, 3), parts, strict=True))
    small = [((8, QUARTER), bf16)] * 2
    keep, give = local(last_kernel, small, (done, b2, b1, b3), place)
    (out,) = local(
        join_kernel, [((2, 8, QUARTER), bf16)], (keep, send(give, CORE)), place
    )
    return out


def solution(mesh):
    fine = Mesh(mesh.devices.reshape(SIZES), AXES)
    learner, tensor = ("zh", "y", "x"), ("zl", "c")
    in_specs = (
        P(None, learner, tensor),
        P(AXES, None),
        P(AXES, None),
        P(AXES, None),
        P(None, learner),
        P(AXES, None),
        P(None, learner),
        P(AXES, None),
        P(AXES, None),
        P(None, learner),
    )
    return jax.shard_map(
        shards,
        mesh=fine,
        in_specs=in_specs,
        out_specs=P(None, learner, tensor),
        check_vma=False,
    )
```

```python
import itertools

import jax
import jax.numpy as jnp
from jax import lax
from jax.experimental import pallas as pl
from jax.experimental.pallas import tpu as pltpu
from jax.sharding import Mesh, PartitionSpec as P

AXES = ("zh", "y", "x", "zl", "c")
SIZES = (2, 4, 4, 2, 2)
adapter_scale = 0.5
WIDTH = 8192
HALF = WIDTH // 2
QUARTER = WIDTH // 4
UNITS = 224
TILE = 4096
STEPS = WIDTH // TILE
PARTS = TILE // 256
f32, bf16 = jnp.float32, jnp.bfloat16
CK = 8
SMALL = pl.CostEstimate(flops=1, bytes_accessed=1, transcendentals=0)


def index(zh, y, x, zl, c):
    return (((zh * 4 + y) * 4 + x) * 2 + zl) * 2 + c


def pairs(partner):
    out = []
    for zh, y, x, zl, c in itertools.product(*map(range, SIZES)):
        z, y2, x2, c2 = partner(zh * 2 + zl, y, x, c)
        out.append((index(zh, y, x, zl, c), index(z >> 1, y2, x2, z & 1, c2)))
    return out


CORE = pairs(lambda z, y, x, c: (z, y, x, 1 - c))
ALONG_Z = {k: pairs(lambda z, y, x, c: (z ^ k, y, x, c)) for k in (1, 2, 3)}
FIRST = {
    k: pairs(lambda z, y, x, c: (z, y ^ k, x, c) if c else (z, y, x ^ k, c))
    for k in (1, 2, 3)
}
SECOND = {
    k: pairs(lambda z, y, x, c: (z, y, x ^ k, c) if c else (z, y ^ k, x, c))
    for k in (1, 2, 3)
}


def send(value, route):
    return lax.ppermute(value, AXES, route)


def nt(a, b):
    return lax.dot_general(a, b, (((1,), (1,)), ((), ())), preferred_element_type=f32)


def tn(a, b):
    return lax.dot_general(a, b, (((0,), (0,)), ((), ())), preferred_element_type=f32)


def nn(a, b):
    return jnp.dot(a, b, preferred_element_type=f32)


def widen(a):
    return a.astype(f32)


def after(value, others):
    return lax.optimization_barrier((value, others))[0]


def project_kernel(n, *refs):
    rows, weights, out = refs[:n], refs[n:-1], refs[-1]
    for i in range(WIDTH // TILE):
        tile = slice(i * TILE, (i + 1) * TILE)
        x = jnp.concatenate([r[:, tile] for r in rows], axis=0)
        w = jnp.concatenate([r[:, tile] for r in weights], axis=0)
        if i == 0:
            out[...] = nt(w, x)
        else:
            out[...] += nt(w, x)


def shard_homes(place):
    out = []
    for other in range(2):
        along_x = (place[3] ^ other) == 0
        cols = [
            [pl.ds(pl.multiple_of(g * 512 + (zh ^ place[0]) * 256, 256), 256) for zh in (0, 1)]
            for g in range(6)
        ]
        rows_at = []
        for y in range(4):
            for x in range(4):
                dy, dx = y ^ place[1], x ^ place[2]
                row = jnp.where(along_x, dy * 64 + dx * 16, dx * 64 + dy * 16)
                rows_at.append(pl.ds(pl.multiple_of(row, 16), 16))
        rank = (place[3] ^ other) * 32
        to_at = [
            pl.ds(pl.multiple_of(rank + (k // 2) * 64 + (k % 2) * 16, 16), 16)
            for k in range(4)
        ]
        out.append((cols, rows_at, to_at))
    return out


def low_rows(rows, first, prepare=None):
    low = 0.0
    for i in range(STEPS):
        tile = slice(i * TILE, (i + 1) * TILE)
        if prepare is not None:
            prepare(i)
        x = jnp.concatenate([r[:, tile] for r in rows], axis=0)
        low += nt(first[:, tile], x)
    return low


def finish(acc, low, seconds, theirs, hidden):
    u = (adapter_scale * low).astype(bf16)
    hs, back = [], 0.0
    for half, (ref, c) in enumerate(((seconds, 0), (theirs, 3072))):
        b = [ref[64 * k : 64 * k + 64, c : c + UNITS] for k in range(3)]
        at = half * UNITS
        g = acc[at : at + UNITS] + tn(b[0], u[:64])
        at += 2 * UNITS
        v = acc[at : at + UNITS] + tn(b[1], u[64:])
        h = g / (1.0 + jnp.exp(-g)) * v
        back += nn(b[2], h.astype(bf16))
        hs.append(h)
    h = jnp.concatenate([*hs, adapter_scale * back], axis=0)
    hidden[...] = h.T.astype(bf16)


def first_down_kernel(
    place, rows1, rows3, acc, down_w, down_w2, seconds, theirs, factor,
    out1, out3, first, second, hidden,
):
    homes = shard_homes(place)

    def gather(i, to, groups, base):
        for learner in range(i * PARTS, (i + 1) * PARTS):
            for src, (cols, rows_at, to_at) in zip((factor, theirs), homes, strict=True):
                for k in range(groups):
                    piece = src[rows_at[learner % 16], cols[base + k][learner // 16]]
                    to[to_at[k], learner * 256 : learner * 256 + 256] = piece

    low = low_rows((rows1, rows3), first, lambda i: gather(i, first, 4, 0))
    finish(acc[:, :128], low, seconds, theirs, hidden)
    for i in range(STEPS):
        tile = slice(i * TILE, (i + 1) * TILE)
        gather(i, second, 2, 4)
        w = jnp.concatenate([r[:, tile] for r in (down_w, down_w2, second)], axis=0)
        result = nn(hidden[...], w)
        out1[:, tile] = result[:64].astype(bf16)
        out3[:, tile] = result[64:].astype(bf16)


def last_down_kernel(
    own, acc, acc2, down_w, down_w2, seconds, theirs, first, second, total, out2, hidden
):
    low = jnp.concatenate([low_rows((own,), first), acc2[4 * UNITS :, :]], axis=1)
    both = jnp.concatenate([acc[:, 128:], acc2[: 4 * UNITS, :]], axis=1)
    finish(both, low, seconds, theirs, hidden)
    for i in range(STEPS):
        tile = slice(i * TILE, (i + 1) * TILE)
        w = jnp.concatenate([r[:, tile] for r in (down_w, down_w2, second)], axis=0)
        result = nn(hidden[...], w)
        total[:, tile] = result[:64]
        out2[:, tile] = result[64:].astype(bf16)


VMEM = pl.BlockSpec(memory_space=pltpu.VMEM)
SMEM = pl.BlockSpec(memory_space=pltpu.SMEM)


def in_vmem(operands):
    return [pltpu.with_memory_space_constraint(a, pltpu.VMEM) for a in operands]


def price_of(us):
    return pl.CostEstimate(
        flops=int(us * 1.15e9), bytes_accessed=int(us * 3.6e6), transcendentals=0
    )


def project(rows, weights, price, *extra):
    n, more, heights = len(rows), len(extra), sum(w.shape[0] for w in weights)
    return pl.pallas_call(
        lambda *refs: project_kernel(n, *refs[more:]),
        in_specs=[VMEM] * (more + n + len(weights)),
        out_specs=VMEM,
        out_shape=jax.ShapeDtypeStruct((heights, sum(r.shape[0] for r in rows)), f32),
        compiler_params=pltpu.CompilerParams(vmem_limit_bytes=10 * 1024 * 1024),
        cost_estimate=price,
    )(*extra, *in_vmem([*rows, *weights]))


def down(body, shapes, operands, *lead):
    return pl.pallas_call(
        body,
        in_specs=[SMEM] * len(lead) + [VMEM] * len(operands),
        out_specs=[VMEM] * len(shapes),
        out_shape=[jax.ShapeDtypeStruct(s, kind) for s, kind in shapes],
        scratch_shapes=[pltpu.VMEM((128, 512), bf16)],
        compiler_params=pltpu.CompilerParams(vmem_limit_bytes=10 * 1024 * 1024),
        cost_estimate=SMALL,
    )(*lead, *in_vmem(operands))


def local(body, shapes, operands, place=None, price=SMALL, far=(), scratch=()):
    lead = [] if place is None else [place]
    return pl.pallas_call(
        body,
        in_specs=[SMEM] * len(lead)
        + [VMEM] * len(operands)
        + [pl.BlockSpec(memory_space=pltpu.HBM)] * len(far),
        out_specs=[VMEM] * len(shapes),
        out_shape=[jax.ShapeDtypeStruct(s, kind) for s, kind in shapes],
        scratch_shapes=list(scratch),
        compiler_params=pltpu.CompilerParams(vmem_limit_bytes=6 * 1024 * 1024),
        cost_estimate=price,
    )(*lead, *operands, *(pltpu.with_memory_space_constraint(a, pltpu.HBM) for a in far))


def begin_kernel(place, inputs, gate, up, down, own, other, factor, ranks, sems):
    c = place[3]
    half = pl.ds(pl.multiple_of(c * 32, 32), 32)
    copies = [pltpu.make_async_copy(inputs.at[c], own, sems.at[0])]
    copies += [pltpu.make_async_copy(inputs.at[1 - c], other, sems.at[1])]
    for k, r in enumerate((gate, up, down)):
        copies += [pltpu.make_async_copy(r.at[half, :], ranks.at[k], sems.at[2 + k])]
    for copy in copies:
        copy.start()
    for copy in copies:
        copy.wait()
    for i in range(6):
        col = slice(256 * i, 256 * i + 256)
        factor[:, col] = ranks[i // 2, (i % 2) * 16 : (i % 2) * 16 + 16, :]


def shape_kernel(place, own, other, factor, wide, message):
    c = place[3]
    wide[:, pl.ds(pl.multiple_of(c * QUARTER, QUARTER), QUARTER)] = own[...]
    wide[:, pl.ds(pl.multiple_of((1 - c) * QUARTER, QUARTER), QUARTER)] = other[...]
    rows = widen(wide[...])
    rows = jnp.concatenate([rows[:, :QUARTER], rows[:, QUARTER:]], axis=0)
    message[:, :QUARTER] = rows.astype(bf16)
    message[:, QUARTER:] = factor[...]


def pack_kernel(place, wide, z1, z2, message, far_message, out):
    zl = place[4]
    here = pl.ds(pl.multiple_of(zl * HALF, HALF), HALF)
    there = pl.ds(pl.multiple_of((1 - zl) * HALF, HALF), HALF)
    z3 = widen(far_message[:, :QUARTER])
    z3 = jnp.concatenate([z3[:8], z3[8:]], axis=1)
    pair = lambda a, b: jnp.concatenate([widen(a), widen(b)], 0).astype(bf16)
    out[:, here] = pair(wide[...], z2[...])
    out[:, there] = pair(z1[...], z3)
    for i in range(6):
        at, col = WIDTH + 512 * i, QUARTER + 256 * i
        out[:, at : at + 256] = message[:, col : col + 256]
        out[:, at + 256 : at + 512] = far_message[:, col : col + 256]


def unpack_kernel(own, got2, got1, got3, block, factor, packed):
    for k, g in enumerate((own, got1, got2, got3)):
        at = slice(16 * k, 16 * k + 16)
        block[at, :] = g[:, :WIDTH]
        factor[at, :] = g[:, WIDTH:]
        packed[at, :] = g[...]


def part_kernel(rows, out):
    out[...] = rows[:, : out.shape[1]]


def touch_kernel(gate_w, up_w, down_w, out):
    out[...] = jnp.zeros_like(out)


def seconds_kernel(gate, up, down, out):
    out[...] = jnp.zeros_like(out)
    for k, r in enumerate((gate, up, down)):
        out[64 * k : 64 * k + 64, :UNITS] = r[...]


def stack_kernel(f0, packed1, f2, packed3, seconds, out):
    for k, r in enumerate((f0, packed1, f2, packed3)):
        out[64 * k : 64 * k + 64, :3072] = r[:, -3072:]
    out[:, 3072:] = seconds[...]


def add_kernel(own, b1, b3, out):
    out[...] = own[...] + widen(b1[...]) + widen(b3[...])


def sum_kernel(own, b, keep, s1, s2, s3):
    for k, out in enumerate((keep, s1, s2, s3)):
        part = slice(16 * k, 16 * k + 16)
        out[...] = (own[part, :] + widen(b[part, :])).astype(out.dtype)


def split_kernel(place, own, b2, b1, b3, keep, s1, s2, s3):
    zl = place[4]
    here = pl.ds(pl.multiple_of(zl * HALF, HALF), HALF)
    there = pl.ds(pl.multiple_of((1 - zl) * HALF, HALF), HALF)
    for cols, near, far in ((here, keep, s2), (there, s1, s3)):
        total = own[:, cols]
        for b in (b1, b2, b3):
            total += widen(b[:, cols])
        near[...] = total[:8].astype(near.dtype)
        far[...] = total[8:].astype(far.dtype)


def last_kernel(place, own, b2, b1, b3, keep, give):
    c = place[3]
    for at, out in ((c, keep), (1 - c, give)):
        cols = pl.ds(pl.multiple_of(at * QUARTER, QUARTER), QUARTER)
        total = own[:, cols] + widen(b1[:, cols])
        total += widen(b2[:, cols]) + widen(b3[:, cols])
        out[...] = total.astype(bf16)


def shards(
    inputs,
    frozen_gate_weight,
    frozen_up_weight,
    frozen_down_weight,
    adapter_first_gate,
    adapter_second_gate,
    adapter_first_up,
    adapter_second_up,
    adapter_first_down,
    adapter_second_down,
):
    zh, y, x, zl, c = (lax.axis_index(a) for a in AXES)
    place = jnp.stack([zh, y, x, c, zl]).astype(jnp.int32)

    own, other, factor = local(
        begin_kernel,
        [((8, QUARTER), bf16), ((8, QUARTER), bf16), ((16, 1536), bf16)],
        (),
        place,
        far=(inputs, adapter_first_gate, adapter_first_up, adapter_second_down),
        scratch=[pltpu.VMEM((3, 32, 256), bf16), pltpu.SemaphoreType.DMA((5,))],
    )
    other = send(other, CORE)
    wide, message = local(
        shape_kernel,
        [((8, HALF), bf16), ((16, QUARTER + 1536), bf16)],
        (own, other, factor),
        place,
    )

    z1, z2, z3 = (
        send(v, ALONG_Z[k]) for k, v in ((1, wide), (2, wide), (3, message))
    )
    gate2 = send(after(frozen_gate_weight, wide), CORE)
    up2 = send(after(frozen_up_weight, wide), CORE)
    (packed,) = local(
        pack_kernel, [((16, WIDTH + 3072), bf16)], (wide, z1, z2, message, z3), place
    )

    packed = after(packed, gate2)
    got = {k: send(packed, FIRST[k]) for k in (1, 2, 3)}
    seconds = (adapter_second_gate, adapter_second_up, adapter_first_down)
    (seconds,) = local(
        seconds_kernel, [((256, 256), bf16)], [a.T for a in after(seconds, packed)]
    )
    block, factor, packed = local(
        unpack_kernel,
        [((64, WIDTH), bf16), ((64, 3072), bf16), ((64, WIDTH + 3072), bf16)],
        (packed, got[2], got[1], got[3]),
    )

    block, factor, packed = after((block, factor, packed), (up2, seconds))
    far = send(factor, SECOND[2])
    packed1, packed3 = send(packed, SECOND[1]), send(packed, SECOND[3])
    frozen = (frozen_gate_weight, frozen_up_weight, frozen_down_weight)
    owned = after(frozen, block)
    down2 = send(owned[2], CORE)
    (far,) = local(part_kernel, [((64, 3072), bf16)], (far,), price=price_of(11))
    (factor,) = local(
        stack_kernel, [((256, 3072 + 256), bf16)], (factor, packed1, far, packed3, seconds)
    )
    factor2 = send(factor, CORE)
    (rows3,) = local(part_kernel, [((64, WIDTH), bf16)], (packed3,))
    rows2 = send(rows3, SECOND[1])
    (touched,) = local(touch_kernel, [((8, 128), f32)], in_vmem(owned))

    weights = (owned[0], gate2, owned[1], up2)
    down_weights = (owned[2], down2)

    acc = project((packed1, packed3, block), weights, price_of(CK), touched)
    part1, part3, first, second = down(
        first_down_kernel,
        [((64, WIDTH), bf16)] * 2 + [((128, WIDTH), bf16), ((64, WIDTH), bf16)],
        (packed1, packed3, acc, *down_weights, seconds, factor2, factor),
        place,
    )
    back1, back3 = send(part1, SECOND[1]), send(part3, SECOND[3])
    acc2 = project((after(rows2, part1),), (*weights, first), SMALL)
    total, part2 = down(
        last_down_kernel,
        [((64, WIDTH), f32), ((64, WIDTH), bf16)],
        (block, acc, acc2, *down_weights, seconds, factor2, first, second),
    )
    back2 = send(part2, SECOND[2])
    (total,) = local(
        add_kernel,
        [((64, WIDTH), f32)],
        (total, back1, back3),
        price=price_of(4.5),
    )
    small = [((16, WIDTH), f32)] + [((16, WIDTH), bf16)] * 3
    mine, *parts = local(sum_kernel, small, (total, back2))
    b1, b2, b3 = (send(p, FIRST[k]) for k, p in zip((1, 2, 3), parts, strict=True))
    small = [((8, HALF), f32)] + [((8, HALF), bf16)] * 3
    done, *parts = local(split_kernel, small, (mine, b2, b1, b3), place)
    b1, b2, b3 = (send(p, ALONG_Z[k]) for k, p in zip((1, 2, 3), parts, strict=True))
    small = [((8, QUARTER), bf16)] * 2
    keep, give = local(last_kernel, small, (done, b2, b1, b3), place)
    got = send(give, CORE)
    return jnp.where(c == 0, jnp.stack([keep, got]), jnp.stack([got, keep]))


def solution(mesh):
    fine = Mesh(mesh.devices.reshape(SIZES), AXES)
    learner, tensor = ("zh", "y", "x"), ("zl", "c")
    in_specs = (
        P(None, learner, tensor),
        P(AXES, None),
        P(AXES, None),
        P(AXES, None),
        P(None, learner),
        P(AXES, None),
        P(None, learner),
        P(AXES, None),
        P(AXES, None),
        P(None, learner),
    )
    return jax.shard_map(
        shards,
        mesh=fine,
        in_specs=in_specs,
        out_specs=P(None, learner, tensor),
        check_vma=False,
    )
```

```python
import itertools

import jax
import jax.numpy as jnp
from jax import lax
from jax.experimental import pallas as pl
from jax.experimental.pallas import tpu as pltpu
from jax.sharding import Mesh, PartitionSpec as P

AXES = ("zh", "y", "x", "zl", "c")
SIZES = (2, 4, 4, 2, 2)
adapter_scale = 0.5
WIDTH = 8192
HALF = WIDTH // 2
QUARTER = WIDTH // 4
UNITS = 224
TILE = 4096
STEPS = WIDTH // TILE
PARTS = TILE // 256
f32, bf16 = jnp.float32, jnp.bfloat16
CK, CU = 8, 2
SMALL = pl.CostEstimate(flops=1, bytes_accessed=1, transcendentals=0)


def index(zh, y, x, zl, c):
    return (((zh * 4 + y) * 4 + x) * 2 + zl) * 2 + c


def pairs(partner):
    out = []
    for zh, y, x, zl, c in itertools.product(*map(range, SIZES)):
        z, y2, x2, c2 = partner(zh * 2 + zl, y, x, c)
        out.append((index(zh, y, x, zl, c), index(z >> 1, y2, x2, z & 1, c2)))
    return out


CORE = pairs(lambda z, y, x, c: (z, y, x, 1 - c))
ALONG_Z = {k: pairs(lambda z, y, x, c: (z ^ k, y, x, c)) for k in (1, 2, 3)}
FIRST = {
    k: pairs(lambda z, y, x, c: (z, y ^ k, x, c) if c else (z, y, x ^ k, c))
    for k in (1, 2, 3)
}
SECOND = {
    k: pairs(lambda z, y, x, c: (z, y, x ^ k, c) if c else (z, y ^ k, x, c))
    for k in (1, 2, 3)
}


def send(value, route):
    return lax.ppermute(value, AXES, route)


def nt(a, b):
    return lax.dot_general(a, b, (((1,), (1,)), ((), ())), preferred_element_type=f32)


def tn(a, b):
    return lax.dot_general(a, b, (((0,), (0,)), ((), ())), preferred_element_type=f32)


def nn(a, b):
    return jnp.dot(a, b, preferred_element_type=f32)


def widen(a):
    return a.astype(f32)


def after(value, others):
    return lax.optimization_barrier((value, others))[0]


def project_kernel(n, *refs):
    rows, weights, out = refs[:n], refs[n:-1], refs[-1]
    for i in range(WIDTH // TILE):
        tile = slice(i * TILE, (i + 1) * TILE)
        x = jnp.concatenate([r[:, tile] for r in rows], axis=0)
        w = jnp.concatenate([r[:, tile] for r in weights], axis=0)
        if i == 0:
            out[...] = nt(w, x)
        else:
            out[...] += nt(w, x)


def shard_homes(place):
    out = []
    for other in range(2):
        along_x = (place[3] ^ other) == 0
        cols = [
            [pl.ds(pl.multiple_of(g * 512 + (zh ^ place[0]) * 256, 256), 256) for zh in (0, 1)]
            for g in range(6)
        ]
        rows_at = []
        for y in range(4):
            for x in range(4):
                dy, dx = y ^ place[1], x ^ place[2]
                row = jnp.where(along_x, dy * 64 + dx * 16, dx * 64 + dy * 16)
                rows_at.append(pl.ds(pl.multiple_of(row, 16), 16))
        rank = (place[3] ^ other) * 32
        to_at = [
            pl.ds(pl.multiple_of(rank + (k // 2) * 64 + (k % 2) * 16, 16), 16)
            for k in range(4)
        ]
        out.append((cols, rows_at, to_at))
    return out


def low_rows(rows, first, prepare=None):
    low = 0.0
    for i in range(STEPS):
        tile = slice(i * TILE, (i + 1) * TILE)
        if prepare is not None:
            prepare(i)
        x = jnp.concatenate([r[:, tile] for r in rows], axis=0)
        low += nt(first[:, tile], x)
    return low


def finish(acc, low, seconds, theirs, hidden):
    u = (adapter_scale * low).astype(bf16)
    hs, back = [], 0.0
    for half, (ref, c) in enumerate(((seconds, 0), (theirs, 3072))):
        b = [ref[64 * k : 64 * k + 64, c : c + UNITS] for k in range(3)]
        at = half * UNITS
        g = acc[at : at + UNITS] + tn(b[0], u[:64])
        at += 2 * UNITS
        v = acc[at : at + UNITS] + tn(b[1], u[64:])
        h = g / (1.0 + jnp.exp(-g)) * v
        back += nn(b[2], h.astype(bf16))
        hs.append(h)
    h = jnp.concatenate([*hs, adapter_scale * back], axis=0)
    hidden[...] = h.T.astype(bf16)


def first_down_kernel(
    place, own1, rest1, own3, rest3, own, got1, got2, got3, acc, down_w, down_w2, seconds,
    theirs, factor, out1, out3, total, first, second, hidden,
):
    homes = shard_homes(place)

    def gather(i, to, groups, base):
        for learner in range(i * PARTS, (i + 1) * PARTS):
            for src, (cols, rows_at, to_at) in zip((factor, theirs), homes, strict=True):
                for k in range(groups):
                    piece = src[rows_at[learner % 16], cols[base + k][learner // 16]]
                    to[to_at[k], learner * 256 : learner * 256 + 256] = piece

    rows = (own1, rest1, own3, rest3, own, got1, got2, got3)
    low = low_rows(rows, first, lambda i: gather(i, first, 4, 0))
    finish(acc, low, seconds, theirs, hidden)
    for i in range(STEPS):
        tile = slice(i * TILE, (i + 1) * TILE)
        gather(i, second, 2, 4)
        w = jnp.concatenate([r[:, tile] for r in (down_w, down_w2, second)], axis=0)
        result = nn(hidden[...], w)
        out1[:, tile] = result[:64].astype(bf16)
        out3[:, tile] = result[64:128].astype(bf16)
        total[:, tile] = result[128:]


def last_down_kernel(acc, down_w, down_w2, seconds, theirs, second, out2, hidden):
    finish(acc[: 4 * UNITS, :], acc[4 * UNITS :, :], seconds, theirs, hidden)
    for i in range(STEPS):
        tile = slice(i * TILE, (i + 1) * TILE)
        w = jnp.concatenate([r[:, tile] for r in (down_w, down_w2, second)], axis=0)
        out2[:, tile] = nn(hidden[...], w).astype(bf16)


VMEM = pl.BlockSpec(memory_space=pltpu.VMEM)
SMEM = pl.BlockSpec(memory_space=pltpu.SMEM)


def in_vmem(operands):
    return [pltpu.with_memory_space_constraint(a, pltpu.VMEM) for a in operands]


def price_of(us):
    return pl.CostEstimate(
        flops=int(us * 1.15e9), bytes_accessed=int(us * 3.6e6), transcendentals=0
    )


def project(rows, weights, price, *extra):
    n, more, heights = len(rows), len(extra), sum(w.shape[0] for w in weights)
    return pl.pallas_call(
        lambda *refs: project_kernel(n, *refs[more:]),
        in_specs=[VMEM] * (more + n + len(weights)),
        out_specs=VMEM,
        out_shape=jax.ShapeDtypeStruct((heights, sum(r.shape[0] for r in rows)), f32),
        compiler_params=pltpu.CompilerParams(vmem_limit_bytes=10 * 1024 * 1024),
        cost_estimate=price,
    )(*extra, *in_vmem([*rows, *weights]))


def down(body, m, shapes, operands, *lead):
    return pl.pallas_call(
        body,
        in_specs=[SMEM] * len(lead) + [VMEM] * len(operands),
        out_specs=[VMEM] * len(shapes),
        out_shape=[jax.ShapeDtypeStruct(s, kind) for s, kind in shapes],
        scratch_shapes=[pltpu.VMEM((m, 512), bf16)],
        compiler_params=pltpu.CompilerParams(vmem_limit_bytes=10 * 1024 * 1024),
        cost_estimate=SMALL,
    )(*lead, *in_vmem(operands))


def local(body, shapes, operands, place=None, price=SMALL, far=(), scratch=()):
    lead = [] if place is None else [place]
    return pl.pallas_call(
        body,
        in_specs=[SMEM] * len(lead)
        + [VMEM] * len(operands)
        + [pl.BlockSpec(memory_space=pltpu.HBM)] * len(far),
        out_specs=[VMEM] * len(shapes),
        out_shape=[jax.ShapeDtypeStruct(s, kind) for s, kind in shapes],
        scratch_shapes=list(scratch),
        compiler_params=pltpu.CompilerParams(vmem_limit_bytes=6 * 1024 * 1024),
        cost_estimate=price,
    )(*lead, *operands, *(pltpu.with_memory_space_constraint(a, pltpu.HBM) for a in far))


def begin_kernel(place, inputs, gate, up, down, own, other, factor, ranks, sems):
    c = place[3]
    half = pl.ds(pl.multiple_of(c * 32, 32), 32)
    copies = [pltpu.make_async_copy(inputs.at[c], own, sems.at[0])]
    copies += [pltpu.make_async_copy(inputs.at[1 - c], other, sems.at[1])]
    for k, r in enumerate((gate, up, down)):
        copies += [pltpu.make_async_copy(r.at[half, :], ranks.at[k], sems.at[2 + k])]
    for copy in copies:
        copy.start()
    for copy in copies:
        copy.wait()
    for i in range(6):
        col = slice(256 * i, 256 * i + 256)
        factor[:, col] = ranks[i // 2, (i % 2) * 16 : (i % 2) * 16 + 16, :]


def shape_kernel(place, own, other, factor, wide, message):
    c = place[3]
    wide[:, pl.ds(pl.multiple_of(c * QUARTER, QUARTER), QUARTER)] = own[...]
    wide[:, pl.ds(pl.multiple_of((1 - c) * QUARTER, QUARTER), QUARTER)] = other[...]
    rows = widen(wide[...])
    rows = jnp.concatenate([rows[:, :QUARTER], rows[:, QUARTER:]], axis=0)
    message[:, :QUARTER] = rows.astype(bf16)
    message[:, QUARTER:] = factor[...]


def pack_kernel(place, wide, z1, z2, message, far_message, out):
    zl = place[4]
    here = pl.ds(pl.multiple_of(zl * HALF, HALF), HALF)
    there = pl.ds(pl.multiple_of((1 - zl) * HALF, HALF), HALF)
    z3 = widen(far_message[:, :QUARTER])
    z3 = jnp.concatenate([z3[:8], z3[8:]], axis=1)
    pair = lambda a, b: jnp.concatenate([widen(a), widen(b)], 0).astype(bf16)
    out[:, here] = pair(wide[...], z2[...])
    out[:, there] = pair(z1[...], z3)
    for i in range(6):
        at, col = WIDTH + 512 * i, QUARTER + 256 * i
        out[:, at : at + 256] = message[:, col : col + 256]
        out[:, at + 256 : at + 512] = far_message[:, col : col + 256]


def unpack_kernel(own, got2, got1, got3, factor, packed):
    for k, g in enumerate((own, got1, got2, got3)):
        factor[16 * k : 16 * k + 16, :] = g[:, WIDTH:]
        if k:
            packed[16 * k - 16 : 16 * k, :] = g[...]


def part_kernel(*refs):
    at, out = 0, refs[-1]
    for r in refs[:-1]:
        out[at : at + r.shape[0], :] = r[:, : out.shape[1]]
        at += r.shape[0]


def touch_kernel(gate_w, up_w, down_w, out):
    out[...] = jnp.zeros_like(out)


def seconds_kernel(gate, up, down, out):
    out[...] = jnp.zeros_like(out)
    for k, r in enumerate((gate, up, down)):
        out[64 * k : 64 * k + 64, :UNITS] = r[...]


def stack_kernel(f0, own1, rest1, f2, own3, rest3, seconds, out):
    at = 0
    for r in (f0, own1, rest1, f2, own3, rest3):
        out[at : at + r.shape[0], :3072] = r[:, -3072:]
        at += r.shape[0]
    out[:, 3072:] = seconds[...]


def add_kernel(own, b1, b3, out):
    out[...] = own[...] + widen(b1[...]) + widen(b3[...])


def sum_kernel(own, b, keep, s1, s2, s3):
    for k, out in enumerate((keep, s1, s2, s3)):
        part = slice(16 * k, 16 * k + 16)
        out[...] = (own[part, :] + widen(b[part, :])).astype(out.dtype)


def split_kernel(place, own, b2, b1, b3, keep, s1, s2, s3):
    zl = place[4]
    here = pl.ds(pl.multiple_of(zl * HALF, HALF), HALF)
    there = pl.ds(pl.multiple_of((1 - zl) * HALF, HALF), HALF)
    for cols, near, far in ((here, keep, s2), (there, s1, s3)):
        total = own[:, cols]
        for b in (b1, b2, b3):
            total += widen(b[:, cols])
        near[...] = total[:8].astype(near.dtype)
        far[...] = total[8:].astype(far.dtype)


def last_kernel(place, own, b2, b1, b3, keep, give):
    c = place[3]
    for at, out in ((c, keep), (1 - c, give)):
        cols = pl.ds(pl.multiple_of(at * QUARTER, QUARTER), QUARTER)
        total = own[:, cols] + widen(b1[:, cols])
        total += widen(b2[:, cols]) + widen(b3[:, cols])
        out[...] = total.astype(bf16)


def shards(
    inputs,
    frozen_gate_weight,
    frozen_up_weight,
    frozen_down_weight,
    adapter_first_gate,
    adapter_second_gate,
    adapter_first_up,
    adapter_second_up,
    adapter_first_down,
    adapter_second_down,
):
    zh, y, x, zl, c = (lax.axis_index(a) for a in AXES)
    place = jnp.stack([zh, y, x, c, zl]).astype(jnp.int32)

    own, other, factor = local(
        begin_kernel,
        [((8, QUARTER), bf16), ((8, QUARTER), bf16), ((16, 1536), bf16)],
        (),
        place,
        far=(inputs, adapter_first_gate, adapter_first_up, adapter_second_down),
        scratch=[pltpu.VMEM((3, 32, 256), bf16), pltpu.SemaphoreType.DMA((5,))],
    )
    other = send(other, CORE)
    wide, message = local(
        shape_kernel,
        [((8, HALF), bf16), ((16, QUARTER + 1536), bf16)],
        (own, other, factor),
        place,
    )

    z1, z2, z3 = (
        send(v, ALONG_Z[k]) for k, v in ((1, wide), (2, wide), (3, message))
    )
    gate2 = send(after(frozen_gate_weight, wide), CORE)
    (packed,) = local(
        pack_kernel, [((16, WIDTH + 3072), bf16)], (wide, z1, z2, message, z3), place
    )

    packed = after(packed, gate2)
    own = packed
    got = {k: send(packed, FIRST[k]) for k in (1, 2, 3)}
    seconds = (adapter_second_gate, adapter_second_up, adapter_first_down)
    (seconds,) = local(
        seconds_kernel, [((256, 256), bf16)], [a.T for a in after(seconds, packed)]
    )
    factor, packed = local(
        unpack_kernel,
        [((64, 3072), bf16), ((48, WIDTH + 3072), bf16)],
        (own, got[2], got[1], got[3]),
        price=price_of(CU),
    )

    own1, own3 = send(own, SECOND[1]), send(own, SECOND[3])
    factor, packed = after((factor, packed), (own1, own3, seconds))
    far = send(factor, SECOND[2])
    rest1, rest3 = send(packed, SECOND[1]), send(packed, SECOND[3])
    frozen = (frozen_gate_weight, frozen_up_weight, frozen_down_weight)
    owned = after(frozen, packed)
    up2, down2 = send(owned[1], CORE), send(owned[2], CORE)
    (far,) = local(part_kernel, [((64, 3072), bf16)], (far,), price=price_of(11))
    (factor,) = local(
        stack_kernel,
        [((256, 3072 + 256), bf16)],
        (factor, own1, rest1, far, own3, rest3, seconds),
    )
    factor2 = send(factor, CORE)
    (rows3,) = local(part_kernel, [((64, WIDTH), bf16)], (own3, rest3))
    rows2 = send(rows3, SECOND[1])
    (touched,) = local(touch_kernel, [((8, 128), f32)], in_vmem(owned))

    weights = (owned[0], gate2, owned[1], up2)
    down_weights = (owned[2], down2)

    rows = (own1, rest1, own3, rest3, own, got[1], got[2], got[3])
    acc = project(rows, weights, price_of(CK), touched)
    part1, part3, total, first, second = down(
        first_down_kernel,
        192,
        [((64, WIDTH), bf16)] * 2
        + [((64, WIDTH), f32), ((128, WIDTH), bf16), ((64, WIDTH), bf16)],
        (*rows, acc, *down_weights, seconds, factor2, factor),
        place,
    )
    back1, back3 = send(part1, SECOND[1]), send(part3, SECOND[3])
    acc = project((after(rows2, part1),), (*weights, first), SMALL)
    (part2,) = down(
        last_down_kernel,
        64,
        [((64, WIDTH), bf16)],
        (acc, *down_weights, seconds, factor2, second),
    )
    back2 = send(part2, SECOND[2])
    (total,) = local(
        add_kernel,
        [((64, WIDTH), f32)],
        (total, back1, back3),
        price=price_of(4.5),
    )
    small = [((16, WIDTH), f32)] + [((16, WIDTH), bf16)] * 3
    mine, *parts = local(sum_kernel, small, (total, back2))
    b1, b2, b3 = (send(p, FIRST[k]) for k, p in zip((1, 2, 3), parts, strict=True))
    small = [((8, HALF), f32)] + [((8, HALF), bf16)] * 3
    done, *parts = local(split_kernel, small, (mine, b2, b1, b3), place)
    b1, b2, b3 = (send(p, ALONG_Z[k]) for k, p in zip((1, 2, 3), parts, strict=True))
    small = [((8, QUARTER), bf16)] * 2
    keep, give = local(last_kernel, small, (done, b2, b1, b3), place)
    got = send(give, CORE)
    return jnp.where(c == 0, jnp.stack([keep, got]), jnp.stack([got, keep]))


def solution(mesh):
    fine = Mesh(mesh.devices.reshape(SIZES), AXES)
    learner, tensor = ("zh", "y", "x"), ("zl", "c")
    in_specs = (
        P(None, learner, tensor),
        P(AXES, None),
        P(AXES, None),
        P(AXES, None),
        P(None, learner),
        P(AXES, None),
        P(None, learner),
        P(AXES, None),
        P(AXES, None),
        P(None, learner),
    )
    return jax.shard_map(
        shards,
        mesh=fine,
        in_specs=in_specs,
        out_specs=P(None, learner, tensor),
        check_vma=False,
    )
```

```python
import itertools

import jax
import jax.numpy as jnp
from jax import lax
from jax.experimental import pallas as pl
from jax.experimental.pallas import tpu as pltpu
from jax.sharding import Mesh, PartitionSpec as P

AXES = ("zh", "y", "x", "zl", "c")
SIZES = (2, 4, 4, 2, 2)
adapter_scale = 0.5
WIDTH = 8192
HALF = WIDTH // 2
QUARTER = WIDTH // 4
UNITS = 224
TILE = 4096
STEPS = WIDTH // TILE
PARTS = TILE // 256
f32, bf16 = jnp.float32, jnp.bfloat16
CK = 8
SMALL = pl.CostEstimate(flops=1, bytes_accessed=1, transcendentals=0)


def index(zh, y, x, zl, c):
    return (((zh * 4 + y) * 4 + x) * 2 + zl) * 2 + c


def pairs(partner):
    out = []
    for zh, y, x, zl, c in itertools.product(*map(range, SIZES)):
        z, y2, x2, c2 = partner(zh * 2 + zl, y, x, c)
        out.append((index(zh, y, x, zl, c), index(z >> 1, y2, x2, z & 1, c2)))
    return out


CORE = pairs(lambda z, y, x, c: (z, y, x, 1 - c))
ALONG_Z = {k: pairs(lambda z, y, x, c: (z ^ k, y, x, c)) for k in (1, 2, 3)}
FIRST = {
    k: pairs(lambda z, y, x, c: (z, y ^ k, x, c) if c else (z, y, x ^ k, c))
    for k in (1, 2, 3)
}
SECOND = {
    k: pairs(lambda z, y, x, c: (z, y, x ^ k, c) if c else (z, y ^ k, x, c))
    for k in (1, 2, 3)
}


def send(value, route):
    return lax.ppermute(value, AXES, route)


def nt(a, b):
    return lax.dot_general(a, b, (((1,), (1,)), ((), ())), preferred_element_type=f32)


def tn(a, b):
    return lax.dot_general(a, b, (((0,), (0,)), ((), ())), preferred_element_type=f32)


def nn(a, b):
    return jnp.dot(a, b, preferred_element_type=f32)


def widen(a):
    return a.astype(f32)


def after(value, others):
    return lax.optimization_barrier((value, others))[0]


def project_kernel(n, *refs):
    rows, weights, out = refs[:n], refs[n:-1], refs[-1]
    for i in range(WIDTH // TILE):
        tile = slice(i * TILE, (i + 1) * TILE)
        x = jnp.concatenate([r[:, tile] for r in rows], axis=0)
        w = jnp.concatenate([r[:, tile] for r in weights], axis=0)
        if i == 0:
            out[...] = nt(w, x)
        else:
            out[...] += nt(w, x)


def shard_homes(place):
    out = []
    for other in range(2):
        along_x = (place[3] ^ other) == 0
        cols = [
            [pl.ds(pl.multiple_of(g * 512 + (zh ^ place[0]) * 256, 256), 256) for zh in (0, 1)]
            for g in range(6)
        ]
        rows_at = []
        for y in range(4):
            for x in range(4):
                dy, dx = y ^ place[1], x ^ place[2]
                row = jnp.where(along_x, dy * 64 + dx * 16, dx * 64 + dy * 16)
                rows_at.append(pl.ds(pl.multiple_of(row, 16), 16))
        rank = (place[3] ^ other) * 32
        to_at = [
            pl.ds(pl.multiple_of(rank + (k // 2) * 64 + (k % 2) * 16, 16), 16)
            for k in range(4)
        ]
        out.append((cols, rows_at, to_at))
    return out


def low_rows(rows, first, prepare=None):
    low = 0.0
    for i in range(STEPS):
        tile = slice(i * TILE, (i + 1) * TILE)
        if prepare is not None:
            prepare(i)
        x = jnp.concatenate([r[:, tile] for r in rows], axis=0)
        low += nt(first[:, tile], x)
    return low


def finish(acc, low, seconds, theirs, hidden):
    u = (adapter_scale * low).astype(bf16)
    hs, back = [], 0.0
    for half, (ref, c) in enumerate(((seconds, 0), (theirs, 3072))):
        b = [ref[64 * k : 64 * k + 64, c : c + UNITS] for k in range(3)]
        at = half * UNITS
        g = acc[at : at + UNITS] + tn(b[0], u[:64])
        at += 2 * UNITS
        v = acc[at : at + UNITS] + tn(b[1], u[64:])
        h = g / (1.0 + jnp.exp(-g)) * v
        back += nn(b[2], h.astype(bf16))
        hs.append(h)
    h = jnp.concatenate([*hs, adapter_scale * back], axis=0)
    hidden[...] = h.T.astype(bf16)


def first_down_kernel(
    place, rows1, rows3, own, acc, down_w, down_w2, seconds, theirs, factor,
    out1, out3, total, first, second, hidden,
):
    homes = shard_homes(place)

    def gather(i, to, groups, base):
        for learner in range(i * PARTS, (i + 1) * PARTS):
            for src, (cols, rows_at, to_at) in zip((factor, theirs), homes, strict=True):
                for k in range(groups):
                    piece = src[rows_at[learner % 16], cols[base + k][learner // 16]]
                    to[to_at[k], learner * 256 : learner * 256 + 256] = piece

    low = low_rows((rows1, rows3, own), first, lambda i: gather(i, first, 4, 0))
    finish(acc, low, seconds, theirs, hidden)
    for i in range(STEPS):
        tile = slice(i * TILE, (i + 1) * TILE)
        gather(i, second, 2, 4)
        w = jnp.concatenate([r[:, tile] for r in (down_w, down_w2, second)], axis=0)
        result = nn(hidden[...], w)
        out1[:, tile] = result[:64].astype(bf16)
        out3[:, tile] = result[64:128].astype(bf16)
        total[:, tile] = result[128:]


def last_down_kernel(acc, down_w, down_w2, seconds, theirs, second, out2, hidden):
    finish(acc[: 4 * UNITS, :], acc[4 * UNITS :, :], seconds, theirs, hidden)
    for i in range(STEPS):
        tile = slice(i * TILE, (i + 1) * TILE)
        w = jnp.concatenate([r[:, tile] for r in (down_w, down_w2, second)], axis=0)
        out2[:, tile] = nn(hidden[...], w).astype(bf16)


VMEM = pl.BlockSpec(memory_space=pltpu.VMEM)
SMEM = pl.BlockSpec(memory_space=pltpu.SMEM)


def in_vmem(operands):
    return [pltpu.with_memory_space_constraint(a, pltpu.VMEM) for a in operands]


def price_of(us):
    return pl.CostEstimate(
        flops=int(us * 1.15e9), bytes_accessed=int(us * 3.6e6), transcendentals=0
    )


def project(rows, weights, price, *extra):
    n, more, heights = len(rows), len(extra), sum(w.shape[0] for w in weights)
    return pl.pallas_call(
        lambda *refs: project_kernel(n, *refs[more:]),
        in_specs=[VMEM] * (more + n + len(weights)),
        out_specs=VMEM,
        out_shape=jax.ShapeDtypeStruct((heights, sum(r.shape[0] for r in rows)), f32),
        compiler_params=pltpu.CompilerParams(vmem_limit_bytes=10 * 1024 * 1024),
        cost_estimate=price,
    )(*extra, *in_vmem([*rows, *weights]))


def down(body, m, shapes, operands, *lead):
    return pl.pallas_call(
        body,
        in_specs=[SMEM] * len(lead) + [VMEM] * len(operands),
        out_specs=[VMEM] * len(shapes),
        out_shape=[jax.ShapeDtypeStruct(s, kind) for s, kind in shapes],
        scratch_shapes=[pltpu.VMEM((m, 512), bf16)],
        compiler_params=pltpu.CompilerParams(vmem_limit_bytes=10 * 1024 * 1024),
        cost_estimate=SMALL,
    )(*lead, *in_vmem(operands))


def local(body, shapes, operands, place=None, price=SMALL, far=(), scratch=()):
    lead = [] if place is None else [place]
    return pl.pallas_call(
        body,
        in_specs=[SMEM] * len(lead)
        + [VMEM] * len(operands)
        + [pl.BlockSpec(memory_space=pltpu.HBM)] * len(far),
        out_specs=[VMEM] * len(shapes),
        out_shape=[jax.ShapeDtypeStruct(s, kind) for s, kind in shapes],
        scratch_shapes=list(scratch),
        compiler_params=pltpu.CompilerParams(vmem_limit_bytes=6 * 1024 * 1024),
        cost_estimate=price,
    )(*lead, *operands, *(pltpu.with_memory_space_constraint(a, pltpu.HBM) for a in far))


def begin_kernel(place, inputs, gate, up, down, own, other, factor, ranks, sems):
    c = place[3]
    half = pl.ds(pl.multiple_of(c * 32, 32), 32)
    copies = [pltpu.make_async_copy(inputs.at[c], own, sems.at[0])]
    copies += [pltpu.make_async_copy(inputs.at[1 - c], other, sems.at[1])]
    for k, r in enumerate((gate, up, down)):
        copies += [pltpu.make_async_copy(r.at[half, :], ranks.at[k], sems.at[2 + k])]
    for copy in copies:
        copy.start()
    for copy in copies:
        copy.wait()
    for i in range(6):
        col = slice(256 * i, 256 * i + 256)
        factor[:, col] = ranks[i // 2, (i % 2) * 16 : (i % 2) * 16 + 16, :]


def shape_kernel(place, own, other, factor, wide, message):
    c = place[3]
    wide[:, pl.ds(pl.multiple_of(c * QUARTER, QUARTER), QUARTER)] = own[...]
    wide[:, pl.ds(pl.multiple_of((1 - c) * QUARTER, QUARTER), QUARTER)] = other[...]
    rows = widen(wide[...])
    rows = jnp.concatenate([rows[:, :QUARTER], rows[:, QUARTER:]], axis=0)
    message[:, :QUARTER] = rows.astype(bf16)
    message[:, QUARTER:] = factor[...]


def pack_kernel(place, wide, z1, z2, message, far_message, out):
    zl = place[4]
    here = pl.ds(pl.multiple_of(zl * HALF, HALF), HALF)
    there = pl.ds(pl.multiple_of((1 - zl) * HALF, HALF), HALF)
    z3 = widen(far_message[:, :QUARTER])
    z3 = jnp.concatenate([z3[:8], z3[8:]], axis=1)
    pair = lambda a, b: jnp.concatenate([widen(a), widen(b)], 0).astype(bf16)
    out[:, here] = pair(wide[...], z2[...])
    out[:, there] = pair(z1[...], z3)
    for i in range(6):
        at, col = WIDTH + 512 * i, QUARTER + 256 * i
        out[:, at : at + 256] = message[:, col : col + 256]
        out[:, at + 256 : at + 512] = far_message[:, col : col + 256]


def unpack_kernel(own, got2, got1, got3, factor, packed):
    for k, g in enumerate((own, got1, got2, got3)):
        factor[16 * k : 16 * k + 16, :] = g[:, WIDTH:]
        packed[16 * k : 16 * k + 16, :] = g[...]


def part_kernel(*refs):
    at, out = 0, refs[-1]
    for r in refs[:-1]:
        out[at : at + r.shape[0], :] = r[:, : out.shape[1]]
        at += r.shape[0]


def touch_kernel(gate_w, up_w, down_w, out):
    out[...] = jnp.zeros_like(out)


def seconds_kernel(gate, up, down, out):
    out[...] = jnp.zeros_like(out)
    for k, r in enumerate((gate, up, down)):
        out[64 * k : 64 * k + 64, :UNITS] = r[...]


def stack_kernel(f0, packed1, f2, packed3, seconds, out):
    at = 0
    for r in (f0, packed1, f2, packed3):
        out[at : at + r.shape[0], :3072] = r[:, -3072:]
        at += r.shape[0]
    out[:, 3072:] = seconds[...]


def add_kernel(own, b1, b3, out):
    out[...] = own[...] + widen(b1[...]) + widen(b3[...])


def sum_kernel(own, b, keep, s1, s2, s3):
    for k, out in enumerate((keep, s1, s2, s3)):
        part = slice(16 * k, 16 * k + 16)
        out[...] = (own[part, :] + widen(b[part, :])).astype(out.dtype)


def split_kernel(place, own, b2, b1, b3, keep, s1, s2, s3):
    zl = place[4]
    here = pl.ds(pl.multiple_of(zl * HALF, HALF), HALF)
    there = pl.ds(pl.multiple_of((1 - zl) * HALF, HALF), HALF)
    for cols, near, far in ((here, keep, s2), (there, s1, s3)):
        total = own[:, cols]
        for b in (b1, b2, b3):
            total += widen(b[:, cols])
        near[...] = total[:8].astype(near.dtype)
        far[...] = total[8:].astype(far.dtype)


def last_kernel(place, own, b2, b1, b3, keep, give):
    c = place[3]
    for at, out in ((c, keep), (1 - c, give)):
        cols = pl.ds(pl.multiple_of(at * QUARTER, QUARTER), QUARTER)
        total = own[:, cols] + widen(b1[:, cols])
        total += widen(b2[:, cols]) + widen(b3[:, cols])
        out[...] = total.astype(bf16)


def shards(
    inputs,
    frozen_gate_weight,
    frozen_up_weight,
    frozen_down_weight,
    adapter_first_gate,
    adapter_second_gate,
    adapter_first_up,
    adapter_second_up,
    adapter_first_down,
    adapter_second_down,
):
    zh, y, x, zl, c = (lax.axis_index(a) for a in AXES)
    place = jnp.stack([zh, y, x, c, zl]).astype(jnp.int32)

    own, other, factor = local(
        begin_kernel,
        [((8, QUARTER), bf16), ((8, QUARTER), bf16), ((16, 1536), bf16)],
        (),
        place,
        far=(inputs, adapter_first_gate, adapter_first_up, adapter_second_down),
        scratch=[pltpu.VMEM((3, 32, 256), bf16), pltpu.SemaphoreType.DMA((5,))],
    )
    other = send(other, CORE)
    wide, message = local(
        shape_kernel,
        [((8, HALF), bf16), ((16, QUARTER + 1536), bf16)],
        (own, other, factor),
        place,
    )

    z1, z2, z3 = (
        send(v, ALONG_Z[k]) for k, v in ((1, wide), (2, wide), (3, message))
    )
    gate2 = send(after(frozen_gate_weight, wide), CORE)
    (packed,) = local(
        pack_kernel, [((16, WIDTH + 3072), bf16)], (wide, z1, z2, message, z3), place
    )

    packed = after(packed, gate2)
    got = {k: send(packed, FIRST[k]) for k in (1, 2, 3)}
    seconds = (adapter_second_gate, adapter_second_up, adapter_first_down)
    (seconds,) = local(
        seconds_kernel, [((256, 256), bf16)], [a.T for a in after(seconds, packed)]
    )
    factor, packed = local(
        unpack_kernel,
        [((64, 3072), bf16), ((64, WIDTH + 3072), bf16)],
        (packed, got[2], got[1], got[3]),
    )

    factor, packed = after((factor, packed), seconds)
    far = send(factor, SECOND[2])
    packed1, packed3 = send(packed, SECOND[1]), send(packed, SECOND[3])
    frozen = (frozen_gate_weight, frozen_up_weight, frozen_down_weight)
    owned = after(frozen, packed)
    up2, down2 = send(owned[1], CORE), send(owned[2], CORE)
    (far,) = local(part_kernel, [((64, 3072), bf16)], (far,), price=price_of(11))
    (factor,) = local(
        stack_kernel,
        [((256, 3072 + 256), bf16)],
        (factor, packed1, far, packed3, seconds),
    )
    factor2 = send(factor, CORE)
    (rows3,) = local(part_kernel, [((64, WIDTH), bf16)], (packed3,))
    rows2 = send(rows3, SECOND[1])
    (touched,) = local(touch_kernel, [((8, 128), f32)], in_vmem(owned))

    weights = (owned[0], gate2, owned[1], up2)
    down_weights = (owned[2], down2)

    rows = (packed1, packed3, packed)
    acc = project(rows, weights, price_of(CK), touched)
    part1, part3, total, first, second = down(
        first_down_kernel,
        192,
        [((64, WIDTH), bf16)] * 2
        + [((64, WIDTH), f32), ((128, WIDTH), bf16), ((64, WIDTH), bf16)],
        (*rows, acc, *down_weights, seconds, factor2, factor),
        place,
    )
    back1, back3 = send(part1, SECOND[1]), send(part3, SECOND[3])
    acc = project((after(rows2, part1),), (*weights, first), SMALL)
    (part2,) = down(
        last_down_kernel,
        64,
        [((64, WIDTH), bf16)],
        (acc, *down_weights, seconds, factor2, second),
    )
    back2 = send(part2, SECOND[2])
    (total,) = local(
        add_kernel,
        [((64, WIDTH), f32)],
        (total, back3, back1),
        price=price_of(4.5),
    )
    small = [((16, WIDTH), f32)] + [((16, WIDTH), bf16)] * 3
    mine, *parts = local(sum_kernel, small, (total, back2))
    b1, b2, b3 = (send(p, FIRST[k]) for k, p in zip((1, 2, 3), parts, strict=True))
    small = [((8, HALF), f32)] + [((8, HALF), bf16)] * 3
    done, *parts = local(split_kernel, small, (mine, b2, b1, b3), place)
    b1, b2, b3 = (send(p, ALONG_Z[k]) for k, p in zip((1, 2, 3), parts, strict=True))
    small = [((8, QUARTER), bf16)] * 2
    keep, give = local(last_kernel, small, (done, b2, b1, b3), place)
    got = send(give, CORE)
    return jnp.where(c == 0, jnp.stack([keep, got]), jnp.stack([got, keep]))


def solution(mesh):
    fine = Mesh(mesh.devices.reshape(SIZES), AXES)
    learner, tensor = ("zh", "y", "x"), ("zl", "c")
    in_specs = (
        P(None, learner, tensor),
        P(AXES, None),
        P(AXES, None),
        P(AXES, None),
        P(None, learner),
        P(AXES, None),
        P(None, learner),
        P(AXES, None),
        P(AXES, None),
        P(None, learner),
    )
    return jax.shard_map(
        shards,
        mesh=fine,
        in_specs=in_specs,
        out_specs=P(None, learner, tensor),
        check_vma=False,
    )
```

```python
import itertools

import jax
import jax.numpy as jnp
from jax import lax
from jax.experimental import pallas as pl
from jax.experimental.pallas import tpu as pltpu
from jax.sharding import Mesh, PartitionSpec as P

AXES = ("zh", "y", "x", "zl", "c")
SIZES = (2, 4, 4, 2, 2)
adapter_scale = 0.5
WIDTH = 8192
HALF = WIDTH // 2
QUARTER = WIDTH // 4
UNITS = 224
TILE = 4096
STEPS = WIDTH // TILE
PARTS = TILE // 256
f32, bf16 = jnp.float32, jnp.bfloat16
CK = 8
SMALL = pl.CostEstimate(flops=1, bytes_accessed=1, transcendentals=0)


def index(zh, y, x, zl, c):
    return (((zh * 4 + y) * 4 + x) * 2 + zl) * 2 + c


def pairs(partner):
    out = []
    for zh, y, x, zl, c in itertools.product(*map(range, SIZES)):
        z, y2, x2, c2 = partner(zh * 2 + zl, y, x, c)
        out.append((index(zh, y, x, zl, c), index(z >> 1, y2, x2, z & 1, c2)))
    return out


CORE = pairs(lambda z, y, x, c: (z, y, x, 1 - c))
ALONG_Z = {k: pairs(lambda z, y, x, c: (z ^ k, y, x, c)) for k in (1, 2, 3)}
FIRST = {
    k: pairs(lambda z, y, x, c: (z, y ^ k, x, c) if c else (z, y, x ^ k, c))
    for k in (1, 2, 3)
}
SECOND = {
    k: pairs(lambda z, y, x, c: (z, y, x ^ k, c) if c else (z, y ^ k, x, c))
    for k in (1, 2, 3)
}


def send(value, route):
    return lax.ppermute(value, AXES, route)


def nt(a, b):
    return lax.dot_general(a, b, (((1,), (1,)), ((), ())), preferred_element_type=f32)


def tn(a, b):
    return lax.dot_general(a, b, (((0,), (0,)), ((), ())), preferred_element_type=f32)


def nn(a, b):
    return jnp.dot(a, b, preferred_element_type=f32)


def widen(a):
    return a.astype(f32)


def after(value, others):
    return lax.optimization_barrier((value, others))[0]


def project_kernel(n, *refs):
    rows, weights, out = refs[:n], refs[n:-1], refs[-1]
    for i in range(WIDTH // TILE):
        tile = slice(i * TILE, (i + 1) * TILE)
        x = jnp.concatenate([r[:, tile] for r in rows], axis=0)
        w = jnp.concatenate([r[:, tile] for r in weights], axis=0)
        if i == 0:
            out[...] = nt(w, x)
        else:
            out[...] += nt(w, x)


def shard_homes(place):
    out = []
    for other in range(2):
        along_x = (place[3] ^ other) == 0
        cols = [
            [pl.ds(pl.multiple_of(g * 512 + (zh ^ place[0]) * 256, 256), 256) for zh in (0, 1)]
            for g in range(6)
        ]
        rows_at = []
        for y in range(4):
            for x in range(4):
                dy, dx = y ^ place[1], x ^ place[2]
                row = jnp.where(along_x, dy * 64 + dx * 16, dx * 64 + dy * 16)
                rows_at.append(pl.ds(pl.multiple_of(row, 16), 16))
        rank = (place[3] ^ other) * 32
        to_at = [
            pl.ds(pl.multiple_of(rank + (k // 2) * 64 + (k % 2) * 16, 16), 16)
            for k in range(4)
        ]
        out.append((cols, rows_at, to_at))
    return out


def low_rows(rows, first, prepare=None):
    low = 0.0
    for i in range(STEPS):
        tile = slice(i * TILE, (i + 1) * TILE)
        if prepare is not None:
            prepare(i)
        x = jnp.concatenate([r[:, tile] for r in rows], axis=0)
        low += nt(first[:, tile], x)
    return low


def finish(acc, low, seconds, theirs, hidden):
    u = (adapter_scale * low).astype(bf16)
    hs, back = [], 0.0
    for half, (ref, c) in enumerate(((seconds, 0), (theirs, 3072))):
        b = [ref[64 * k : 64 * k + 64, c : c + UNITS] for k in range(3)]
        at = half * UNITS
        g = acc[at : at + UNITS] + tn(b[0], u[:64])
        at += 2 * UNITS
        v = acc[at : at + UNITS] + tn(b[1], u[64:])
        h = g / (1.0 + jnp.exp(-g)) * v
        back += nn(b[2], h.astype(bf16))
        hs.append(h)
    h = jnp.concatenate([*hs, adapter_scale * back], axis=0)
    hidden[...] = h.T.astype(bf16)


def first_down_kernel(
    place, rows1, rows3, acc, down_w, down_w2, seconds, theirs, factor,
    out1, out3, first, second, hidden,
):
    homes = shard_homes(place)

    def gather(i, to, groups, base):
        for learner in range(i * PARTS, (i + 1) * PARTS):
            for src, (cols, rows_at, to_at) in zip((factor, theirs), homes, strict=True):
                for k in range(groups):
                    piece = src[rows_at[learner % 16], cols[base + k][learner // 16]]
                    to[to_at[k], learner * 256 : learner * 256 + 256] = piece

    low = low_rows((rows1, rows3), first, lambda i: gather(i, first, 4, 0))
    finish(acc[:, :128], low, seconds, theirs, hidden)
    for i in range(STEPS):
        tile = slice(i * TILE, (i + 1) * TILE)
        gather(i, second, 2, 4)
        w = jnp.concatenate([r[:, tile] for r in (down_w, down_w2, second)], axis=0)
        result = nn(hidden[...], w)
        out1[:, tile] = result[:64].astype(bf16)
        out3[:, tile] = result[64:].astype(bf16)


def own_down_kernel(
    own, acc, down_w, down_w2, seconds, theirs, first, second, total, hidden
):
    finish(acc[:, 128:], low_rows((own,), first), seconds, theirs, hidden)
    for i in range(STEPS):
        tile = slice(i * TILE, (i + 1) * TILE)
        w = jnp.concatenate([r[:, tile] for r in (down_w, down_w2, second)], axis=0)
        total[:, tile] = nn(hidden[...], w)


def last_down_kernel(acc, down_w, down_w2, seconds, theirs, second, out2, hidden):
    finish(acc[: 4 * UNITS, :], acc[4 * UNITS :, :], seconds, theirs, hidden)
    for i in range(STEPS):
        tile = slice(i * TILE, (i + 1) * TILE)
        w = jnp.concatenate([r[:, tile] for r in (down_w, down_w2, second)], axis=0)
        out2[:, tile] = nn(hidden[...], w).astype(bf16)


VMEM = pl.BlockSpec(memory_space=pltpu.VMEM)
SMEM = pl.BlockSpec(memory_space=pltpu.SMEM)


def in_vmem(operands):
    return [pltpu.with_memory_space_constraint(a, pltpu.VMEM) for a in operands]


def price_of(us):
    return pl.CostEstimate(
        flops=int(us * 1.15e9), bytes_accessed=int(us * 3.6e6), transcendentals=0
    )


def project(rows, weights, price, *extra):
    n, more, heights = len(rows), len(extra), sum(w.shape[0] for w in weights)
    return pl.pallas_call(
        lambda *refs: project_kernel(n, *refs[more:]),
        in_specs=[VMEM] * (more + n + len(weights)),
        out_specs=VMEM,
        out_shape=jax.ShapeDtypeStruct((heights, sum(r.shape[0] for r in rows)), f32),
        compiler_params=pltpu.CompilerParams(vmem_limit_bytes=10 * 1024 * 1024),
        cost_estimate=price,
    )(*extra, *in_vmem([*rows, *weights]))


def down(body, m, shapes, operands, *lead):
    return pl.pallas_call(
        body,
        in_specs=[SMEM] * len(lead) + [VMEM] * len(operands),
        out_specs=[VMEM] * len(shapes),
        out_shape=[jax.ShapeDtypeStruct(s, kind) for s, kind in shapes],
        scratch_shapes=[pltpu.VMEM((m, 512), bf16)],
        compiler_params=pltpu.CompilerParams(vmem_limit_bytes=10 * 1024 * 1024),
        cost_estimate=SMALL,
    )(*lead, *in_vmem(operands))


def local(body, shapes, operands, place=None, price=SMALL, far=(), scratch=()):
    lead = [] if place is None else [place]
    return pl.pallas_call(
        body,
        in_specs=[SMEM] * len(lead)
        + [VMEM] * len(operands)
        + [pl.BlockSpec(memory_space=pltpu.HBM)] * len(far),
        out_specs=[VMEM] * len(shapes),
        out_shape=[jax.ShapeDtypeStruct(s, kind) for s, kind in shapes],
        scratch_shapes=list(scratch),
        compiler_params=pltpu.CompilerParams(vmem_limit_bytes=6 * 1024 * 1024),
        cost_estimate=price,
    )(*lead, *operands, *(pltpu.with_memory_space_constraint(a, pltpu.HBM) for a in far))


def half_kernel(place, gate, up, down, factor, ranks, sems):
    half = pl.ds(pl.multiple_of(place[3] * 32, 32), 32)
    copies = [
        pltpu.make_async_copy(r.at[half, :], ranks.at[k], sems.at[k])
        for k, r in enumerate((gate, up, down))
    ]
    for copy in copies:
        copy.start()
    for copy in copies:
        copy.wait()
    for i in range(6):
        col = slice(256 * i, 256 * i + 256)
        factor[:, col] = ranks[i // 2, (i % 2) * 16 : (i % 2) * 16 + 16, :]


def shape_kernel(place, own, other, factor, wide, message):
    c = place[3]
    wide[:, pl.ds(pl.multiple_of(c * QUARTER, QUARTER), QUARTER)] = own[...]
    wide[:, pl.ds(pl.multiple_of((1 - c) * QUARTER, QUARTER), QUARTER)] = other[...]
    rows = widen(wide[...])
    rows = jnp.concatenate([rows[:, :QUARTER], rows[:, QUARTER:]], axis=0)
    message[:, :QUARTER] = rows.astype(bf16)
    message[:, QUARTER:] = factor[...]


def pack_kernel(place, wide, z1, z2, message, far_message, out):
    zl = place[4]
    here = pl.ds(pl.multiple_of(zl * HALF, HALF), HALF)
    there = pl.ds(pl.multiple_of((1 - zl) * HALF, HALF), HALF)
    z3 = widen(far_message[:, :QUARTER])
    z3 = jnp.concatenate([z3[:8], z3[8:]], axis=1)
    pair = lambda a, b: jnp.concatenate([widen(a), widen(b)], 0).astype(bf16)
    out[:, here] = pair(wide[...], z2[...])
    out[:, there] = pair(z1[...], z3)
    for i in range(6):
        at, col = WIDTH + 512 * i, QUARTER + 256 * i
        out[:, at : at + 256] = message[:, col : col + 256]
        out[:, at + 256 : at + 512] = far_message[:, col : col + 256]


def unpack_kernel(own, got2, got1, got3, factor, packed):
    for k, g in enumerate((own, got1, got2, got3)):
        factor[16 * k : 16 * k + 16, :] = g[:, WIDTH:]
        packed[16 * k : 16 * k + 16, :] = g[...]


def part_kernel(*refs):
    at, out = 0, refs[-1]
    for r in refs[:-1]:
        out[at : at + r.shape[0], :] = r[:, : out.shape[1]]
        at += r.shape[0]


def touch_kernel(gate_w, up_w, down_w, out):
    out[...] = jnp.zeros_like(out)


def seconds_kernel(gate, up, down, out):
    out[...] = jnp.zeros_like(out)
    for k, r in enumerate((gate, up, down)):
        out[64 * k : 64 * k + 64, :UNITS] = r[...]


def stack_kernel(f0, packed1, f2, packed3, seconds, out):
    at = 0
    for r in (f0, packed1, f2, packed3):
        out[at : at + r.shape[0], :3072] = r[:, -3072:]
        at += r.shape[0]
    out[:, 3072:] = seconds[...]


def add_kernel(own, b1, b3, out):
    out[...] = own[...] + widen(b1[...]) + widen(b3[...])


def sum_kernel(own, b, keep, s1, s2, s3):
    for k, out in enumerate((keep, s1, s2, s3)):
        part = slice(16 * k, 16 * k + 16)
        out[...] = (own[part, :] + widen(b[part, :])).astype(out.dtype)


def split_kernel(place, own, b2, b1, b3, keep, s1, s2, s3):
    zl = place[4]
    here = pl.ds(pl.multiple_of(zl * HALF, HALF), HALF)
    there = pl.ds(pl.multiple_of((1 - zl) * HALF, HALF), HALF)
    for cols, near, far in ((here, keep, s2), (there, s1, s3)):
        total = own[:, cols]
        for b in (b1, b2, b3):
            total += widen(b[:, cols])
        near[...] = total[:8].astype(near.dtype)
        far[...] = total[8:].astype(far.dtype)


def last_kernel(place, own, b2, b1, b3, keep, give):
    c = place[3]
    for at, out in ((c, keep), (1 - c, give)):
        cols = pl.ds(pl.multiple_of(at * QUARTER, QUARTER), QUARTER)
        total = own[:, cols] + widen(b1[:, cols])
        total += widen(b2[:, cols]) + widen(b3[:, cols])
        out[...] = total.astype(bf16)


def shards(
    inputs,
    frozen_gate_weight,
    frozen_up_weight,
    frozen_down_weight,
    adapter_first_gate,
    adapter_second_gate,
    adapter_first_up,
    adapter_second_up,
    adapter_first_down,
    adapter_second_down,
):
    zh, y, x, zl, c = (lax.axis_index(a) for a in AXES)
    place = jnp.stack([zh, y, x, c, zl]).astype(jnp.int32)

    own = jnp.where(c == 0, inputs[0], inputs[1])
    other = send(jnp.where(c == 0, inputs[1], inputs[0]), CORE)
    (factor,) = local(
        half_kernel,
        [((16, 1536), bf16)],
        (),
        place,
        far=(adapter_first_gate, adapter_first_up, adapter_second_down),
        scratch=[pltpu.VMEM((3, 32, 256), bf16), pltpu.SemaphoreType.DMA((3,))],
    )
    wide, message = local(
        shape_kernel,
        [((8, HALF), bf16), ((16, QUARTER + 1536), bf16)],
        (own, other, factor),
        place,
    )

    z1, z2, z3 = (
        send(v, ALONG_Z[k]) for k, v in ((1, wide), (2, wide), (3, message))
    )
    gate2 = send(after(frozen_gate_weight, wide), CORE)
    (packed,) = local(
        pack_kernel, [((16, WIDTH + 3072), bf16)], (wide, z1, z2, message, z3), place
    )

    packed = after(packed, gate2)
    got = {k: send(packed, FIRST[k]) for k in (1, 2, 3)}
    seconds = (adapter_second_gate, adapter_second_up, adapter_first_down)
    (seconds,) = local(
        seconds_kernel, [((256, 256), bf16)], [a.T for a in after(seconds, packed)]
    )
    factor, packed = local(
        unpack_kernel,
        [((64, 3072), bf16), ((64, WIDTH + 3072), bf16)],
        (packed, got[2], got[1], got[3]),
    )

    factor, packed = after((factor, packed), seconds)
    far = send(factor, SECOND[2])
    packed1, packed3 = send(packed, SECOND[1]), send(packed, SECOND[3])
    frozen = (frozen_gate_weight, frozen_up_weight, frozen_down_weight)
    owned = after(frozen, packed)
    up2, down2 = send(owned[1], CORE), send(owned[2], CORE)
    (far,) = local(part_kernel, [((64, 3072), bf16)], (far,), price=price_of(11))
    (factor,) = local(
        stack_kernel,
        [((256, 3072 + 256), bf16)],
        (factor, packed1, far, packed3, seconds),
    )
    factor2 = send(factor, CORE)
    (rows3,) = local(part_kernel, [((64, WIDTH), bf16)], (packed3,))
    rows2 = send(rows3, SECOND[1])
    (touched,) = local(touch_kernel, [((8, 128), f32)], in_vmem(owned))

    weights = (owned[0], gate2, owned[1], up2)
    down_weights = (owned[2], down2)

    acc = project((packed1, packed3, packed), weights, price_of(CK), touched)
    part1, part3, first, second = down(
        first_down_kernel,
        128,
        [((64, WIDTH), bf16)] * 2 + [((128, WIDTH), bf16), ((64, WIDTH), bf16)],
        (packed1, packed3, acc, *down_weights, seconds, factor2, factor),
        place,
    )
    back1, back3 = send(part1, SECOND[1]), send(part3, SECOND[3])
    acc2 = project((after(rows2, part1),), (*weights, first), SMALL)
    (part2,) = down(
        last_down_kernel,
        64,
        [((64, WIDTH), bf16)],
        (acc2, *down_weights, seconds, factor2, second),
    )
    back2 = send(part2, SECOND[2])
    (total,) = down(
        own_down_kernel,
        64,
        [((64, WIDTH), f32)],
        (packed, after(acc, part2), *down_weights, seconds, factor2, first, second),
    )
    (total,) = local(
        add_kernel,
        [((64, WIDTH), f32)],
        (total, back1, back3),
        price=price_of(4.5),
    )
    small = [((16, WIDTH), f32)] + [((16, WIDTH), bf16)] * 3
    mine, *parts = local(sum_kernel, small, (total, back2))
    b1, b2, b3 = (send(p, FIRST[k]) for k, p in zip((1, 2, 3), parts, strict=True))
    small = [((8, HALF), f32)] + [((8, HALF), bf16)] * 3
    done, *parts = local(split_kernel, small, (mine, b2, b1, b3), place)
    b1, b2, b3 = (send(p, ALONG_Z[k]) for k, p in zip((1, 2, 3), parts, strict=True))
    small = [((8, QUARTER), bf16)] * 2
    keep, give = local(last_kernel, small, (done, b2, b1, b3), place)
    got = send(give, CORE)
    return jnp.where(c == 0, jnp.stack([keep, got]), jnp.stack([got, keep]))


def solution(mesh):
    fine = Mesh(mesh.devices.reshape(SIZES), AXES)
    learner, tensor = ("zh", "y", "x"), ("zl", "c")
    in_specs = (
        P(None, learner, tensor),
        P(AXES, None),
        P(AXES, None),
        P(AXES, None),
        P(None, learner),
        P(AXES, None),
        P(None, learner),
        P(AXES, None),
        P(AXES, None),
        P(None, learner),
    )
    return jax.shard_map(
        shards,
        mesh=fine,
        in_specs=in_specs,
        out_specs=P(None, learner, tensor),
        check_vma=False,
    )
```

```python
import itertools

import jax
import jax.numpy as jnp
from jax import lax
from jax.experimental import pallas as pl
from jax.experimental.pallas import tpu as pltpu
from jax.sharding import Mesh, PartitionSpec as P

AXES = ("zh", "y", "x", "zl", "c")
SIZES = (2, 4, 4, 2, 2)
adapter_scale = 0.5
WIDTH = 8192
HALF = WIDTH // 2
QUARTER = WIDTH // 4
UNITS = 224
TILE = 4096
STEPS = WIDTH // TILE
PARTS = TILE // 256
f32, bf16 = jnp.float32, jnp.bfloat16
CK = 1
SMALL = pl.CostEstimate(flops=1, bytes_accessed=1, transcendentals=0)


def index(zh, y, x, zl, c):
    return (((zh * 4 + y) * 4 + x) * 2 + zl) * 2 + c


def pairs(partner):
    out = []
    for zh, y, x, zl, c in itertools.product(*map(range, SIZES)):
        z, y2, x2, c2 = partner(zh * 2 + zl, y, x, c)
        out.append((index(zh, y, x, zl, c), index(z >> 1, y2, x2, z & 1, c2)))
    return out


CORE = pairs(lambda z, y, x, c: (z, y, x, 1 - c))
ALONG_Z = {k: pairs(lambda z, y, x, c: (z ^ k, y, x, c)) for k in (1, 2, 3)}
FIRST = {
    k: pairs(lambda z, y, x, c: (z, y ^ k, x, c) if c else (z, y, x ^ k, c))
    for k in (1, 2, 3)
}
SECOND = {
    k: pairs(lambda z, y, x, c: (z, y, x ^ k, c) if c else (z, y ^ k, x, c))
    for k in (1, 2, 3)
}


def send(value, route):
    return lax.ppermute(value, AXES, route)


def nt(a, b):
    return lax.dot_general(a, b, (((1,), (1,)), ((), ())), preferred_element_type=f32)


def tn(a, b):
    return lax.dot_general(a, b, (((0,), (0,)), ((), ())), preferred_element_type=f32)


def nn(a, b):
    return jnp.dot(a, b, preferred_element_type=f32)


def widen(a):
    return a.astype(f32)


def after(value, others):
    return lax.optimization_barrier((value, others))[0]


def project_kernel(n, *refs):
    rows, weights, out = refs[:n], refs[n:-1], refs[-1]
    for i in range(WIDTH // TILE):
        tile = slice(i * TILE, (i + 1) * TILE)
        x = jnp.concatenate([r[:, tile] for r in rows], axis=0)
        w = jnp.concatenate([r[:, tile] for r in weights], axis=0)
        if i == 0:
            out[...] = nt(w, x)
        else:
            out[...] += nt(w, x)


def shard_homes(place):
    out = []
    for other in range(2):
        along_x = (place[3] ^ other) == 0
        cols = [
            [pl.ds(pl.multiple_of(g * 512 + (zh ^ place[0]) * 256, 256), 256) for zh in (0, 1)]
            for g in range(6)
        ]
        rows_at = []
        for y in range(4):
            for x in range(4):
                dy, dx = y ^ place[1], x ^ place[2]
                row = jnp.where(along_x, dy * 64 + dx * 16, dx * 64 + dy * 16)
                rows_at.append(pl.ds(pl.multiple_of(row, 16), 16))
        rank = (place[3] ^ other) * 32
        to_at = [
            pl.ds(pl.multiple_of(rank + (k // 2) * 64 + (k % 2) * 16, 16), 16)
            for k in range(4)
        ]
        out.append((cols, rows_at, to_at))
    return out


def low_rows(rows, first, prepare=None):
    low = 0.0
    for i in range(STEPS):
        tile = slice(i * TILE, (i + 1) * TILE)
        if prepare is not None:
            prepare(i)
        x = jnp.concatenate([r[:, tile] for r in rows], axis=0)
        low += nt(first[:, tile], x)
    return low


def finish(acc, low, seconds, theirs, hidden):
    u = (adapter_scale * low).astype(bf16)
    hs, back = [], 0.0
    for half, (ref, c) in enumerate(((seconds, 0), (theirs, 3072))):
        b = [ref[64 * k : 64 * k + 64, c : c + UNITS] for k in range(3)]
        at = half * UNITS
        g = acc[at : at + UNITS] + tn(b[0], u[:64])
        at += 2 * UNITS
        v = acc[at : at + UNITS] + tn(b[1], u[64:])
        h = g / (1.0 + jnp.exp(-g)) * v
        back += nn(b[2], h.astype(bf16))
        hs.append(h)
    h = jnp.concatenate([*hs, adapter_scale * back], axis=0)
    hidden[...] = h.T.astype(bf16)


def first_down_kernel(
    place, rows1, rows3, acc, down_w, down_w2, seconds, theirs, factor,
    out1, out3, first, second, hidden,
):
    homes = shard_homes(place)

    def gather(i, to, groups, base):
        for learner in range(i * PARTS, (i + 1) * PARTS):
            for src, (cols, rows_at, to_at) in zip((factor, theirs), homes, strict=True):
                for k in range(groups):
                    piece = src[rows_at[learner % 16], cols[base + k][learner // 16]]
                    to[to_at[k], learner * 256 : learner * 256 + 256] = piece

    low = low_rows((rows1, rows3), first, lambda i: gather(i, first, 4, 0))
    finish(acc[:, :128], low, seconds, theirs, hidden)
    for i in range(STEPS):
        tile = slice(i * TILE, (i + 1) * TILE)
        gather(i, second, 2, 4)
        w = jnp.concatenate([r[:, tile] for r in (down_w, down_w2, second)], axis=0)
        result = nn(hidden[...], w)
        out1[:, tile] = result[:64].astype(bf16)
        out3[:, tile] = result[64:].astype(bf16)


def own_down_kernel(
    own, acc, down_w, down_w2, seconds, theirs, first, second, total, hidden
):
    finish(acc[:, 128:], low_rows((own,), first), seconds, theirs, hidden)
    for i in range(STEPS):
        tile = slice(i * TILE, (i + 1) * TILE)
        w = jnp.concatenate([r[:, tile] for r in (down_w, down_w2, second)], axis=0)
        total[:, tile] = nn(hidden[...], w)


def last_down_kernel(acc, down_w, down_w2, seconds, theirs, second, out2, hidden):
    finish(acc[: 4 * UNITS, :], acc[4 * UNITS :, :], seconds, theirs, hidden)
    for i in range(STEPS):
        tile = slice(i * TILE, (i + 1) * TILE)
        w = jnp.concatenate([r[:, tile] for r in (down_w, down_w2, second)], axis=0)
        out2[:, tile] = nn(hidden[...], w).astype(bf16)


VMEM = pl.BlockSpec(memory_space=pltpu.VMEM)
SMEM = pl.BlockSpec(memory_space=pltpu.SMEM)


def in_vmem(operands):
    return [pltpu.with_memory_space_constraint(a, pltpu.VMEM) for a in operands]


def price_of(us):
    return pl.CostEstimate(
        flops=int(us * 1.15e9), bytes_accessed=int(us * 3.6e6), transcendentals=0
    )


def project(rows, weights, price, *extra):
    n, more, heights = len(rows), len(extra), sum(w.shape[0] for w in weights)
    return pl.pallas_call(
        lambda *refs: project_kernel(n, *refs[more:]),
        in_specs=[VMEM] * (more + n + len(weights)),
        out_specs=VMEM,
        out_shape=jax.ShapeDtypeStruct((heights, sum(r.shape[0] for r in rows)), f32),
        compiler_params=pltpu.CompilerParams(vmem_limit_bytes=10 * 1024 * 1024),
        cost_estimate=price,
    )(*extra, *in_vmem([*rows, *weights]))


def down(body, m, shapes, operands, *lead):
    return pl.pallas_call(
        body,
        in_specs=[SMEM] * len(lead) + [VMEM] * len(operands),
        out_specs=[VMEM] * len(shapes),
        out_shape=[jax.ShapeDtypeStruct(s, kind) for s, kind in shapes],
        scratch_shapes=[pltpu.VMEM((m, 512), bf16)],
        compiler_params=pltpu.CompilerParams(vmem_limit_bytes=10 * 1024 * 1024),
        cost_estimate=SMALL,
    )(*lead, *in_vmem(operands))


def local(body, shapes, operands, place=None, price=SMALL, far=(), scratch=()):
    lead = [] if place is None else [place]
    return pl.pallas_call(
        body,
        in_specs=[SMEM] * len(lead)
        + [VMEM] * len(operands)
        + [pl.BlockSpec(memory_space=pltpu.HBM)] * len(far),
        out_specs=[VMEM] * len(shapes),
        out_shape=[jax.ShapeDtypeStruct(s, kind) for s, kind in shapes],
        scratch_shapes=list(scratch),
        compiler_params=pltpu.CompilerParams(vmem_limit_bytes=6 * 1024 * 1024),
        cost_estimate=price,
    )(*lead, *operands, *(pltpu.with_memory_space_constraint(a, pltpu.HBM) for a in far))


def half_kernel(place, gate, up, down, factor, ranks, sems):
    half = pl.ds(pl.multiple_of(place[3] * 32, 32), 32)
    copies = [
        pltpu.make_async_copy(r.at[half, :], ranks.at[k], sems.at[k])
        for k, r in enumerate((gate, up, down))
    ]
    for copy in copies:
        copy.start()
    for copy in copies:
        copy.wait()
    for i in range(6):
        col = slice(256 * i, 256 * i + 256)
        factor[:, col] = ranks[i // 2, (i % 2) * 16 : (i % 2) * 16 + 16, :]


def shape_kernel(place, own, other, factor, wide, message):
    c = place[3]
    wide[:, pl.ds(pl.multiple_of(c * QUARTER, QUARTER), QUARTER)] = own[...]
    wide[:, pl.ds(pl.multiple_of((1 - c) * QUARTER, QUARTER), QUARTER)] = other[...]
    rows = widen(wide[...])
    rows = jnp.concatenate([rows[:, :QUARTER], rows[:, QUARTER:]], axis=0)
    message[:, :QUARTER] = rows.astype(bf16)
    message[:, QUARTER:] = factor[...]


def pack_kernel(place, wide, z1, z2, message, far_message, out):
    zl = place[4]
    here = pl.ds(pl.multiple_of(zl * HALF, HALF), HALF)
    there = pl.ds(pl.multiple_of((1 - zl) * HALF, HALF), HALF)
    z3 = widen(far_message[:, :QUARTER])
    z3 = jnp.concatenate([z3[:8], z3[8:]], axis=1)
    pair = lambda a, b: jnp.concatenate([widen(a), widen(b)], 0).astype(bf16)
    out[:, here] = pair(wide[...], z2[...])
    out[:, there] = pair(z1[...], z3)
    for i in range(6):
        at, col = WIDTH + 512 * i, QUARTER + 256 * i
        out[:, at : at + 256] = message[:, col : col + 256]
        out[:, at + 256 : at + 512] = far_message[:, col : col + 256]


def unpack_kernel(own, got2, got1, got3, factor, packed):
    for k, g in enumerate((own, got1, got2, got3)):
        factor[16 * k : 16 * k + 16, :] = g[:, WIDTH:]
        packed[16 * k : 16 * k + 16, :] = g[...]


def halves_kernel(from3, from1, to1, to3):
    to1[...] = from3[:32, :WIDTH]
    to3[...] = from1[32:, :WIDTH]


def touch_kernel(gate_w, up_w, down_w, out):
    out[...] = jnp.zeros_like(out)


def seconds_kernel(gate, up, down, out):
    out[...] = jnp.zeros_like(out)
    for k, r in enumerate((gate, up, down)):
        out[64 * k : 64 * k + 64, :UNITS] = r[...]


def stack_kernel(f0, packed1, f2, packed3, seconds, out):
    at = 0
    for r in (f0, packed1, f2, packed3):
        out[at : at + r.shape[0], :3072] = r[:, -3072:]
        at += r.shape[0]
    out[:, 3072:] = seconds[...]


def add_kernel(own, b1, b3, out):
    out[...] = own[...] + widen(b1[...]) + widen(b3[...])


def sum_kernel(own, b, keep, s1, s2, s3):
    for k, out in enumerate((keep, s1, s2, s3)):
        part = slice(16 * k, 16 * k + 16)
        out[...] = (own[part, :] + widen(b[part, :])).astype(out.dtype)


def split_kernel(place, own, b2, b1, b3, keep, s1, s2, s3):
    zl = place[4]
    here = pl.ds(pl.multiple_of(zl * HALF, HALF), HALF)
    there = pl.ds(pl.multiple_of((1 - zl) * HALF, HALF), HALF)
    for cols, near, far in ((here, keep, s2), (there, s1, s3)):
        total = own[:, cols]
        for b in (b1, b2, b3):
            total += widen(b[:, cols])
        near[...] = total[:8].astype(near.dtype)
        far[...] = total[8:].astype(far.dtype)


def last_kernel(place, own, b2, b1, b3, keep, give):
    c = place[3]
    for at, out in ((c, keep), (1 - c, give)):
        cols = pl.ds(pl.multiple_of(at * QUARTER, QUARTER), QUARTER)
        total = own[:, cols] + widen(b1[:, cols])
        total += widen(b2[:, cols]) + widen(b3[:, cols])
        out[...] = total.astype(bf16)


def shards(
    inputs,
    frozen_gate_weight,
    frozen_up_weight,
    frozen_down_weight,
    adapter_first_gate,
    adapter_second_gate,
    adapter_first_up,
    adapter_second_up,
    adapter_first_down,
    adapter_second_down,
):
    zh, y, x, zl, c = (lax.axis_index(a) for a in AXES)
    place = jnp.stack([zh, y, x, c, zl]).astype(jnp.int32)

    own = jnp.where(c == 0, inputs[0], inputs[1])
    other = send(jnp.where(c == 0, inputs[1], inputs[0]), CORE)
    (factor,) = local(
        half_kernel,
        [((16, 1536), bf16)],
        (),
        place,
        far=(adapter_first_gate, adapter_first_up, adapter_second_down),
        scratch=[pltpu.VMEM((3, 32, 256), bf16), pltpu.SemaphoreType.DMA((3,))],
    )
    wide, message = local(
        shape_kernel,
        [((8, HALF), bf16), ((16, QUARTER + 1536), bf16)],
        (own, other, factor),
        place,
    )

    z1, z2, z3 = (
        send(v, ALONG_Z[k]) for k, v in ((1, wide), (2, wide), (3, message))
    )
    gate2 = send(after(frozen_gate_weight, wide), CORE)
    (packed,) = local(
        pack_kernel, [((16, WIDTH + 3072), bf16)], (wide, z1, z2, message, z3), place
    )

    packed = after(packed, gate2)
    got = {k: send(packed, FIRST[k]) for k in (1, 2, 3)}
    seconds = (adapter_second_gate, adapter_second_up, adapter_first_down)
    (seconds,) = local(
        seconds_kernel, [((256, 256), bf16)], [a.T for a in after(seconds, packed)]
    )
    factor, packed = local(
        unpack_kernel,
        [((64, 3072), bf16), ((64, WIDTH + 3072), bf16)],
        (packed, got[2], got[1], got[3]),
    )

    factor, packed = after((factor, packed), seconds)
    far = send(factor, SECOND[2])
    packed1, packed3 = send(packed, SECOND[1]), send(packed, SECOND[3])
    frozen = (frozen_gate_weight, frozen_up_weight, frozen_down_weight)
    owned = after(frozen, packed)
    up2, down2 = send(owned[1], CORE), send(owned[2], CORE)
    to1, to3 = local(halves_kernel, [((32, WIDTH), bf16)] * 2, (packed3, packed1))
    rows2 = (send(to1, SECOND[1]), send(to3, SECOND[3]))
    (touched,) = local(touch_kernel, [((8, 128), f32)], in_vmem(owned))
    weights = (owned[0], gate2, owned[1], up2)
    down_weights = (owned[2], down2)

    acc = project((packed1, packed3, packed), weights, price_of(CK), touched)
    (factor,) = local(
        stack_kernel,
        [((256, 3072 + 256), bf16)],
        (factor, packed1, after(far, acc), packed3, seconds),
    )
    factor2 = send(factor, CORE)
    part1, part3, first, second = down(
        first_down_kernel,
        128,
        [((64, WIDTH), bf16)] * 2 + [((128, WIDTH), bf16), ((64, WIDTH), bf16)],
        (packed1, packed3, acc, *down_weights, seconds, factor2, factor),
        place,
    )
    back1, back3 = send(part1, SECOND[1]), send(part3, SECOND[3])
    acc2 = project(after(rows2, part1), (*weights, first), SMALL)
    (part2,) = down(
        last_down_kernel,
        64,
        [((64, WIDTH), bf16)],
        (acc2, *down_weights, seconds, factor2, second),
    )
    back2 = send(part2, SECOND[2])
    (total,) = down(
        own_down_kernel,
        64,
        [((64, WIDTH), f32)],
        (packed, after(acc, part2), *down_weights, seconds, factor2, first, second),
    )
    (total,) = local(
        add_kernel,
        [((64, WIDTH), f32)],
        (total, back1, back3),
        price=price_of(4.5),
    )
    small = [((16, WIDTH), f32)] + [((16, WIDTH), bf16)] * 3
    mine, *parts = local(sum_kernel, small, (total, back2))
    b1, b2, b3 = (send(p, FIRST[k]) for k, p in zip((1, 2, 3), parts, strict=True))
    small = [((8, HALF), f32)] + [((8, HALF), bf16)] * 3
    done, *parts = local(split_kernel, small, (mine, b2, b1, b3), place)
    b1, b2, b3 = (send(p, ALONG_Z[k]) for k, p in zip((1, 2, 3), parts, strict=True))
    small = [((8, QUARTER), bf16)] * 2
    keep, give = local(last_kernel, small, (done, b2, b1, b3), place)
    got = send(give, CORE)
    return jnp.where(c == 0, jnp.stack([keep, got]), jnp.stack([got, keep]))


def solution(mesh):
    fine = Mesh(mesh.devices.reshape(SIZES), AXES)
    learner, tensor = ("zh", "y", "x"), ("zl", "c")
    in_specs = (
        P(None, learner, tensor),
        P(AXES, None),
        P(AXES, None),
        P(AXES, None),
        P(None, learner),
        P(AXES, None),
        P(None, learner),
        P(AXES, None),
        P(AXES, None),
        P(None, learner),
    )
    return jax.shard_map(
        shards,
        mesh=fine,
        in_specs=in_specs,
        out_specs=P(None, learner, tensor),
        check_vma=False,
    )
```

```python
import itertools

import jax
import jax.numpy as jnp
from jax import lax
from jax.experimental import pallas as pl
from jax.experimental.pallas import tpu as pltpu
from jax.sharding import Mesh, PartitionSpec as P

AXES = ("zh", "y", "x", "zl", "c")
SIZES = (2, 4, 4, 2, 2)
adapter_scale = 0.5
WIDTH = 8192
HALF = WIDTH // 2
QUARTER = WIDTH // 4
UNITS = 224
TILE = 4096
STEPS = WIDTH // TILE
PARTS = TILE // 256
f32, bf16 = jnp.float32, jnp.bfloat16
CK = 8
SMALL = pl.CostEstimate(flops=1, bytes_accessed=1, transcendentals=0)


def index(zh, y, x, zl, c):
    return (((zh * 4 + y) * 4 + x) * 2 + zl) * 2 + c


def pairs(partner):
    out = []
    for zh, y, x, zl, c in itertools.product(*map(range, SIZES)):
        z, y2, x2, c2 = partner(zh * 2 + zl, y, x, c)
        out.append((index(zh, y, x, zl, c), index(z >> 1, y2, x2, z & 1, c2)))
    return out


CORE = pairs(lambda z, y, x, c: (z, y, x, 1 - c))
ALONG_Z = {k: pairs(lambda z, y, x, c: (z ^ k, y, x, c)) for k in (1, 2, 3)}
FIRST = {
    k: pairs(lambda z, y, x, c: (z, y ^ k, x, c) if c else (z, y, x ^ k, c))
    for k in (1, 2, 3)
}
SECOND = {
    k: pairs(lambda z, y, x, c: (z, y, x ^ k, c) if c else (z, y ^ k, x, c))
    for k in (1, 2, 3)
}


def send(value, route):
    return lax.ppermute(value, AXES, route)


def nt(a, b):
    return lax.dot_general(a, b, (((1,), (1,)), ((), ())), preferred_element_type=f32)


def tn(a, b):
    return lax.dot_general(a, b, (((0,), (0,)), ((), ())), preferred_element_type=f32)


def nn(a, b):
    return jnp.dot(a, b, preferred_element_type=f32)


def widen(a):
    return a.astype(f32)


def after(value, others):
    return lax.optimization_barrier((value, others))[0]


def project_kernel(n, *refs):
    rows, weights, out = refs[:n], refs[n:-1], refs[-1]
    for i in range(WIDTH // TILE):
        tile = slice(i * TILE, (i + 1) * TILE)
        x = jnp.concatenate([r[:, tile] for r in rows], axis=0)
        w = jnp.concatenate([r[:, tile] for r in weights], axis=0)
        if i == 0:
            out[...] = nt(w, x)
        else:
            out[...] += nt(w, x)


def shard_homes(place):
    out = []
    for other in range(2):
        along_x = (place[3] ^ other) == 0
        cols = [
            [pl.ds(pl.multiple_of(g * 512 + (zh ^ place[0]) * 256, 256), 256) for zh in (0, 1)]
            for g in range(6)
        ]
        rows_at = []
        for y in range(4):
            for x in range(4):
                dy, dx = y ^ place[1], x ^ place[2]
                row = jnp.where(along_x, dy * 64 + dx * 16, dx * 64 + dy * 16)
                rows_at.append(pl.ds(pl.multiple_of(row, 16), 16))
        rank = (place[3] ^ other) * 32
        to_at = [
            pl.ds(pl.multiple_of(rank + (k // 2) * 64 + (k % 2) * 16, 16), 16)
            for k in range(4)
        ]
        out.append((cols, rows_at, to_at))
    return out


def low_rows(rows, first, prepare=None):
    low = 0.0
    for i in range(STEPS):
        tile = slice(i * TILE, (i + 1) * TILE)
        if prepare is not None:
            prepare(i)
        x = jnp.concatenate([r[:, tile] for r in rows], axis=0)
        low += nt(first[:, tile], x)
    return low


def finish(acc, low, seconds, theirs, hidden):
    u = (adapter_scale * low).astype(bf16)
    hs, back = [], 0.0
    for half, (ref, c) in enumerate(((seconds, 0), (theirs, 3072))):
        b = [ref[64 * k : 64 * k + 64, c : c + UNITS] for k in range(3)]
        at = half * UNITS
        g = acc[at : at + UNITS] + tn(b[0], u[:64])
        at += 2 * UNITS
        v = acc[at : at + UNITS] + tn(b[1], u[64:])
        h = g / (1.0 + jnp.exp(-g)) * v
        back += nn(b[2], h.astype(bf16))
        hs.append(h)
    h = jnp.concatenate([*hs, adapter_scale * back], axis=0)
    hidden[...] = h.T.astype(bf16)


def first_down_kernel(
    place, rows3, rows1, acc, down_w, down_w2, seconds, theirs, factor,
    out3, out1, first, second, hidden,
):
    homes = shard_homes(place)

    def gather(i, to, groups, base):
        for learner in range(i * PARTS, (i + 1) * PARTS):
            for src, (cols, rows_at, to_at) in zip((factor, theirs), homes, strict=True):
                for k in range(groups):
                    piece = src[rows_at[learner % 16], cols[base + k][learner // 16]]
                    to[to_at[k], learner * 256 : learner * 256 + 256] = piece

    low = low_rows((rows3, rows1), first, lambda i: gather(i, first, 4, 0))
    finish(acc[:, :128], low, seconds, theirs, hidden)
    for i in range(STEPS):
        tile = slice(i * TILE, (i + 1) * TILE)
        gather(i, second, 2, 4)
        w = jnp.concatenate([r[:, tile] for r in (down_w, down_w2, second)], axis=0)
        result = nn(hidden[...], w)
        out3[:, tile] = result[:64].astype(bf16)
        out1[:, tile] = result[64:].astype(bf16)


def own_down_kernel(
    own, acc, down_w, down_w2, seconds, theirs, first, second, total, hidden
):
    finish(acc[:, 128:], low_rows((own,), first), seconds, theirs, hidden)
    for i in range(STEPS):
        tile = slice(i * TILE, (i + 1) * TILE)
        w = jnp.concatenate([r[:, tile] for r in (down_w, down_w2, second)], axis=0)
        total[:, tile] = nn(hidden[...], w)


def last_down_kernel(acc, down_w, down_w2, seconds, theirs, second, out2, hidden):
    finish(acc[: 4 * UNITS, :], acc[4 * UNITS :, :], seconds, theirs, hidden)
    for i in range(STEPS):
        tile = slice(i * TILE, (i + 1) * TILE)
        w = jnp.concatenate([r[:, tile] for r in (down_w, down_w2, second)], axis=0)
        out2[:, tile] = nn(hidden[...], w).astype(bf16)


VMEM = pl.BlockSpec(memory_space=pltpu.VMEM)
SMEM = pl.BlockSpec(memory_space=pltpu.SMEM)


def in_vmem(operands):
    return [pltpu.with_memory_space_constraint(a, pltpu.VMEM) for a in operands]


def price_of(us):
    return pl.CostEstimate(
        flops=int(us * 1.15e9), bytes_accessed=int(us * 3.6e6), transcendentals=0
    )


def project(rows, weights, price, *extra):
    n, more, heights = len(rows), len(extra), sum(w.shape[0] for w in weights)
    return pl.pallas_call(
        lambda *refs: project_kernel(n, *refs[more:]),
        in_specs=[VMEM] * (more + n + len(weights)),
        out_specs=VMEM,
        out_shape=jax.ShapeDtypeStruct((heights, sum(r.shape[0] for r in rows)), f32),
        compiler_params=pltpu.CompilerParams(vmem_limit_bytes=10 * 1024 * 1024),
        cost_estimate=price,
    )(*extra, *in_vmem([*rows, *weights]))


def down(body, m, shapes, operands, *lead):
    return pl.pallas_call(
        body,
        in_specs=[SMEM] * len(lead) + [VMEM] * len(operands),
        out_specs=[VMEM] * len(shapes),
        out_shape=[jax.ShapeDtypeStruct(s, kind) for s, kind in shapes],
        scratch_shapes=[pltpu.VMEM((m, 512), bf16)],
        compiler_params=pltpu.CompilerParams(vmem_limit_bytes=10 * 1024 * 1024),
        cost_estimate=SMALL,
    )(*lead, *in_vmem(operands))


def local(body, shapes, operands, place=None, price=SMALL, far=(), scratch=()):
    lead = [] if place is None else [place]
    return pl.pallas_call(
        body,
        in_specs=[SMEM] * len(lead)
        + [VMEM] * len(operands)
        + [pl.BlockSpec(memory_space=pltpu.HBM)] * len(far),
        out_specs=[VMEM] * len(shapes),
        out_shape=[jax.ShapeDtypeStruct(s, kind) for s, kind in shapes],
        scratch_shapes=list(scratch),
        compiler_params=pltpu.CompilerParams(vmem_limit_bytes=6 * 1024 * 1024),
        cost_estimate=price,
    )(*lead, *operands, *(pltpu.with_memory_space_constraint(a, pltpu.HBM) for a in far))


def half_kernel(place, gate, up, down, factor, ranks, sems):
    half = pl.ds(pl.multiple_of(place[3] * 32, 32), 32)
    copies = [
        pltpu.make_async_copy(r.at[half, :], ranks.at[k], sems.at[k])
        for k, r in enumerate((gate, up, down))
    ]
    for copy in copies:
        copy.start()
    for copy in copies:
        copy.wait()
    for i in range(6):
        col = slice(256 * i, 256 * i + 256)
        factor[:, col] = ranks[i // 2, (i % 2) * 16 : (i % 2) * 16 + 16, :]


def shape_kernel(place, own, other, factor, wide, message):
    c = place[3]
    wide[:, pl.ds(pl.multiple_of(c * QUARTER, QUARTER), QUARTER)] = own[...]
    wide[:, pl.ds(pl.multiple_of((1 - c) * QUARTER, QUARTER), QUARTER)] = other[...]
    rows = widen(wide[...])
    rows = jnp.concatenate([rows[:, :QUARTER], rows[:, QUARTER:]], axis=0)
    message[:, :QUARTER] = rows.astype(bf16)
    message[:, QUARTER:] = factor[...]


def pack_kernel(place, wide, z1, z2, message, far_message, out):
    zl = place[4]
    here = pl.ds(pl.multiple_of(zl * HALF, HALF), HALF)
    there = pl.ds(pl.multiple_of((1 - zl) * HALF, HALF), HALF)
    z3 = widen(far_message[:, :QUARTER])
    z3 = jnp.concatenate([z3[:8], z3[8:]], axis=1)
    pair = lambda a, b: jnp.concatenate([widen(a), widen(b)], 0).astype(bf16)
    out[:, here] = pair(wide[...], z2[...])
    out[:, there] = pair(z1[...], z3)
    for i in range(6):
        at, col = WIDTH + 512 * i, QUARTER + 256 * i
        out[:, at : at + 256] = message[:, col : col + 256]
        out[:, at + 256 : at + 512] = far_message[:, col : col + 256]


def unpack_kernel(own, got2, got1, got3, factor, packed):
    for k, g in enumerate((own, got1, got2, got3)):
        factor[16 * k : 16 * k + 16, :] = g[:, WIDTH:]
        packed[16 * k : 16 * k + 16, :] = g[...]


def part_kernel(*refs):
    at, out = 0, refs[-1]
    for r in refs[:-1]:
        out[at : at + r.shape[0], :] = r[:, : out.shape[1]]
        at += r.shape[0]


def touch_kernel(gate_w, up_w, down_w, out):
    out[...] = jnp.zeros_like(out)


def seconds_kernel(gate, up, down, out):
    out[...] = jnp.zeros_like(out)
    for k, r in enumerate((gate, up, down)):
        out[64 * k : 64 * k + 64, :UNITS] = r[...]


def stack_kernel(f0, packed3, packed1, f2, seconds, out):
    at = 0
    for r in (f0, packed1, f2, packed3):
        out[at : at + r.shape[0], :3072] = r[:, -3072:]
        at += r.shape[0]
    out[:, 3072:] = seconds[...]


def add_kernel(own, b1, b3, out):
    out[...] = own[...] + widen(b1[...]) + widen(b3[...])


def sum_kernel(own, b, keep, s1, s2, s3):
    for k, out in enumerate((keep, s1, s2, s3)):
        part = slice(16 * k, 16 * k + 16)
        out[...] = (own[part, :] + widen(b[part, :])).astype(out.dtype)


def split_kernel(place, own, b2, b1, b3, keep, s1, s2, s3):
    zl = place[4]
    here = pl.ds(pl.multiple_of(zl * HALF, HALF), HALF)
    there = pl.ds(pl.multiple_of((1 - zl) * HALF, HALF), HALF)
    for cols, near, far in ((here, keep, s2), (there, s1, s3)):
        total = own[:, cols]
        for b in (b1, b2, b3):
            total += widen(b[:, cols])
        near[...] = total[:8].astype(near.dtype)
        far[...] = total[8:].astype(far.dtype)


def last_kernel(place, own, b2, b1, b3, keep, give):
    c = place[3]
    for at, out in ((c, keep), (1 - c, give)):
        cols = pl.ds(pl.multiple_of(at * QUARTER, QUARTER), QUARTER)
        total = own[:, cols] + widen(b1[:, cols])
        total += widen(b2[:, cols]) + widen(b3[:, cols])
        out[...] = total.astype(bf16)


def shards(
    inputs,
    frozen_gate_weight,
    frozen_up_weight,
    frozen_down_weight,
    adapter_first_gate,
    adapter_second_gate,
    adapter_first_up,
    adapter_second_up,
    adapter_first_down,
    adapter_second_down,
):
    zh, y, x, zl, c = (lax.axis_index(a) for a in AXES)
    place = jnp.stack([zh, y, x, c, zl]).astype(jnp.int32)

    own = jnp.where(c == 0, inputs[0], inputs[1])
    other = send(jnp.where(c == 0, inputs[1], inputs[0]), CORE)
    (factor,) = local(
        half_kernel,
        [((16, 1536), bf16)],
        (),
        place,
        far=(adapter_first_gate, adapter_first_up, adapter_second_down),
        scratch=[pltpu.VMEM((3, 32, 256), bf16), pltpu.SemaphoreType.DMA((3,))],
    )
    wide, message = local(
        shape_kernel,
        [((8, HALF), bf16), ((16, QUARTER + 1536), bf16)],
        (own, other, factor),
        place,
    )

    z1, z2, z3 = (
        send(v, ALONG_Z[k]) for k, v in ((1, wide), (2, wide), (3, message))
    )
    gate2 = send(after(frozen_gate_weight, wide), CORE)
    (packed,) = local(
        pack_kernel, [((16, WIDTH + 3072), bf16)], (wide, z1, z2, message, z3), place
    )

    packed = after(packed, gate2)
    got = {k: send(packed, FIRST[k]) for k in (1, 2, 3)}
    seconds = (adapter_second_gate, adapter_second_up, adapter_first_down)
    (seconds,) = local(
        seconds_kernel, [((256, 256), bf16)], [a.T for a in after(seconds, packed)]
    )
    factor, packed = local(
        unpack_kernel,
        [((64, 3072), bf16), ((64, WIDTH + 3072), bf16)],
        (packed, got[2], got[1], got[3]),
    )

    factor, packed = after((factor, packed), seconds)
    far = send(factor, SECOND[2])
    packed1, packed3 = send(packed, SECOND[1]), send(packed, SECOND[3])
    frozen = (frozen_gate_weight, frozen_up_weight, frozen_down_weight)
    owned = after(frozen, packed)
    up2, down2 = send(owned[1], CORE), send(owned[2], CORE)
    (far,) = local(part_kernel, [((64, 3072), bf16)], (far,), price=price_of(11))
    (factor,) = local(
        stack_kernel,
        [((256, 3072 + 256), bf16)],
        (factor, packed3, packed1, far, seconds),
    )
    factor2 = send(factor, CORE)
    (rows3,) = local(part_kernel, [((64, WIDTH), bf16)], (packed3,))
    rows2 = send(rows3, SECOND[1])
    (touched,) = local(touch_kernel, [((8, 128), f32)], in_vmem(owned))

    weights = (owned[0], gate2, owned[1], up2)
    down_weights = (owned[2], down2)

    acc = project((packed3, packed1, packed), weights, price_of(CK), touched)
    part3, part1, first, second = down(
        first_down_kernel,
        128,
        [((64, WIDTH), bf16)] * 2 + [((128, WIDTH), bf16), ((64, WIDTH), bf16)],
        (packed3, packed1, acc, *down_weights, seconds, factor2, factor),
        place,
    )
    back1, back3 = send(part1, SECOND[1]), send(part3, SECOND[3])
    acc2 = project((after(rows2, part1),), (*weights, first), SMALL)
    (part2,) = down(
        last_down_kernel,
        64,
        [((64, WIDTH), bf16)],
        (acc2, *down_weights, seconds, factor2, second),
    )
    back2 = send(part2, SECOND[2])
    (total,) = down(
        own_down_kernel,
        64,
        [((64, WIDTH), f32)],
        (packed, after(acc, part2), *down_weights, seconds, factor2, first, second),
    )
    (total,) = local(
        add_kernel,
        [((64, WIDTH), f32)],
        (total, back1, back3),
        price=price_of(4.5),
    )
    small = [((16, WIDTH), f32)] + [((16, WIDTH), bf16)] * 3
    mine, *parts = local(sum_kernel, small, (total, back2))
    b1, b2, b3 = (send(p, FIRST[k]) for k, p in zip((1, 2, 3), parts, strict=True))
    small = [((8, HALF), f32)] + [((8, HALF), bf16)] * 3
    done, *parts = local(split_kernel, small, (mine, b2, b1, b3), place)
    b1, b2, b3 = (send(p, ALONG_Z[k]) for k, p in zip((1, 2, 3), parts, strict=True))
    small = [((8, QUARTER), bf16)] * 2
    keep, give = local(last_kernel, small, (done, b2, b1, b3), place)
    got = send(give, CORE)
    return jnp.where(c == 0, jnp.stack([keep, got]), jnp.stack([got, keep]))


def solution(mesh):
    fine = Mesh(mesh.devices.reshape(SIZES), AXES)
    learner, tensor = ("zh", "y", "x"), ("zl", "c")
    in_specs = (
        P(None, learner, tensor),
        P(AXES, None),
        P(AXES, None),
        P(AXES, None),
        P(None, learner),
        P(AXES, None),
        P(None, learner),
        P(AXES, None),
        P(AXES, None),
        P(None, learner),
    )
    return jax.shard_map(
        shards,
        mesh=fine,
        in_specs=in_specs,
        out_specs=P(None, learner, tensor),
        check_vma=False,
    )
```

```python
import itertools

import jax
import jax.numpy as jnp
from jax import lax
from jax.experimental import pallas as pl
from jax.experimental.pallas import tpu as pltpu
from jax.sharding import Mesh, PartitionSpec as P

AXES = ("zh", "y", "x", "zl", "c")
SIZES = (2, 4, 4, 2, 2)
adapter_scale = 0.5
WIDTH = 8192
HALF = WIDTH // 2
QUARTER = WIDTH // 4
UNITS = 224
TILE = 4096
STEPS = WIDTH // TILE
PARTS = TILE // 256
f32, bf16 = jnp.float32, jnp.bfloat16
CK = 8
SMALL = pl.CostEstimate(flops=1, bytes_accessed=1, transcendentals=0)


def index(zh, y, x, zl, c):
    return (((zh * 4 + y) * 4 + x) * 2 + zl) * 2 + c


def pairs(partner):
    out = []
    for zh, y, x, zl, c in itertools.product(*map(range, SIZES)):
        z, y2, x2, c2 = partner(zh * 2 + zl, y, x, c)
        out.append((index(zh, y, x, zl, c), index(z >> 1, y2, x2, z & 1, c2)))
    return out


CORE = pairs(lambda z, y, x, c: (z, y, x, 1 - c))
ALONG_Z = {k: pairs(lambda z, y, x, c: (z ^ k, y, x, c)) for k in (1, 2, 3)}
FIRST = {
    k: pairs(lambda z, y, x, c: (z, y ^ k, x, c) if c else (z, y, x ^ k, c))
    for k in (1, 2, 3)
}
SECOND = {
    k: pairs(lambda z, y, x, c: (z, y, x ^ k, c) if c else (z, y ^ k, x, c))
    for k in (1, 2, 3)
}


def send(value, route):
    return lax.ppermute(value, AXES, route)


def nt(a, b):
    return lax.dot_general(a, b, (((1,), (1,)), ((), ())), preferred_element_type=f32)


def tn(a, b):
    return lax.dot_general(a, b, (((0,), (0,)), ((), ())), preferred_element_type=f32)


def nn(a, b):
    return jnp.dot(a, b, preferred_element_type=f32)


def widen(a):
    return a.astype(f32)


def after(value, others):
    return lax.optimization_barrier((value, others))[0]


def project_kernel(n, *refs):
    rows, weights, out = refs[:n], refs[n:-1], refs[-1]
    for i in range(WIDTH // TILE):
        tile = slice(i * TILE, (i + 1) * TILE)
        x = jnp.concatenate([r[:, tile] for r in rows], axis=0)
        w = jnp.concatenate([r[:, tile] for r in weights], axis=0)
        if i == 0:
            out[...] = nt(w, x)
        else:
            out[...] += nt(w, x)


def shard_homes(place):
    out = []
    for other in range(2):
        along_x = (place[3] ^ other) == 0
        cols = [
            [pl.ds(pl.multiple_of(g * 512 + (zh ^ place[0]) * 256, 256), 256) for zh in (0, 1)]
            for g in range(6)
        ]
        rows_at = []
        for y in range(4):
            for x in range(4):
                dy, dx = y ^ place[1], x ^ place[2]
                row = jnp.where(along_x, dy * 64 + dx * 16, dx * 64 + dy * 16)
                rows_at.append(pl.ds(pl.multiple_of(row, 16), 16))
        rank = (place[3] ^ other) * 32
        to_at = [
            pl.ds(pl.multiple_of(rank + (k // 2) * 64 + (k % 2) * 16, 16), 16)
            for k in range(4)
        ]
        out.append((cols, rows_at, to_at))
    return out


def low_rows(rows, first, prepare=None):
    low = 0.0
    for i in range(STEPS):
        tile = slice(i * TILE, (i + 1) * TILE)
        if prepare is not None:
            prepare(i)
        x = jnp.concatenate([r[:, tile] for r in rows], axis=0)
        low += nt(first[:, tile], x)
    return low


def finish(acc, low, seconds, theirs, hidden):
    u = (adapter_scale * low).astype(bf16)
    hs, back = [], 0.0
    for half, (ref, c) in enumerate(((seconds, 0), (theirs, 3072))):
        b = [ref[64 * k : 64 * k + 64, c : c + UNITS] for k in range(3)]
        at = half * UNITS
        g = acc[at : at + UNITS] + tn(b[0], u[:64])
        at += 2 * UNITS
        v = acc[at : at + UNITS] + tn(b[1], u[64:])
        h = g / (1.0 + jnp.exp(-g)) * v
        back += nn(b[2], h.astype(bf16))
        hs.append(h)
    h = jnp.concatenate([*hs, adapter_scale * back], axis=0)
    hidden[...] = h.T.astype(bf16)


def first_down_kernel(
    place, rows3, rows1, acc, down_w, down_w2, seconds, theirs, factor,
    out3, out1, first, second, hidden,
):
    homes = shard_homes(place)

    def gather(i, to, groups, base):
        for learner in range(i * PARTS, (i + 1) * PARTS):
            for src, (cols, rows_at, to_at) in zip((factor, theirs), homes, strict=True):
                for k in range(groups):
                    piece = src[rows_at[learner % 16], cols[base + k][learner // 16]]
                    to[to_at[k], learner * 256 : learner * 256 + 256] = piece

    low = low_rows((rows3, rows1), first, lambda i: gather(i, first, 4, 0))
    finish(acc[:, :128], low, seconds, theirs, hidden)
    for i in range(STEPS):
        tile = slice(i * TILE, (i + 1) * TILE)
        gather(i, second, 2, 4)
        w = jnp.concatenate([r[:, tile] for r in (down_w, down_w2, second)], axis=0)
        result = nn(hidden[...], w)
        out3[:, tile] = result[:64].astype(bf16)
        out1[:, tile] = result[64:].astype(bf16)


def own_down_kernel(
    own, acc, down_w, down_w2, seconds, theirs, first, second, total, hidden
):
    finish(acc[:, 128:], low_rows((own,), first), seconds, theirs, hidden)
    for i in range(STEPS):
        tile = slice(i * TILE, (i + 1) * TILE)
        w = jnp.concatenate([r[:, tile] for r in (down_w, down_w2, second)], axis=0)
        total[:, tile] = nn(hidden[...], w)


def last_down_kernel(acc, down_w, down_w2, seconds, theirs, second, out2, hidden):
    finish(acc[: 4 * UNITS, :], acc[4 * UNITS :, :], seconds, theirs, hidden)
    for i in range(STEPS):
        tile = slice(i * TILE, (i + 1) * TILE)
        w = jnp.concatenate([r[:, tile] for r in (down_w, down_w2, second)], axis=0)
        out2[:, tile] = nn(hidden[...], w).astype(bf16)


VMEM = pl.BlockSpec(memory_space=pltpu.VMEM)
SMEM = pl.BlockSpec(memory_space=pltpu.SMEM)


def in_vmem(operands):
    return [pltpu.with_memory_space_constraint(a, pltpu.VMEM) for a in operands]


def price_of(us):
    return pl.CostEstimate(
        flops=int(us * 1.15e9), bytes_accessed=int(us * 3.6e6), transcendentals=0
    )


def project(rows, weights, price, *extra):
    n, more, heights = len(rows), len(extra), sum(w.shape[0] for w in weights)
    return pl.pallas_call(
        lambda *refs: project_kernel(n, *refs[more:]),
        in_specs=[VMEM] * (more + n + len(weights)),
        out_specs=VMEM,
        out_shape=jax.ShapeDtypeStruct((heights, sum(r.shape[0] for r in rows)), f32),
        compiler_params=pltpu.CompilerParams(vmem_limit_bytes=10 * 1024 * 1024),
        cost_estimate=price,
    )(*extra, *in_vmem([*rows, *weights]))


def down(body, m, shapes, operands, *lead):
    return pl.pallas_call(
        body,
        in_specs=[SMEM] * len(lead) + [VMEM] * len(operands),
        out_specs=[VMEM] * len(shapes),
        out_shape=[jax.ShapeDtypeStruct(s, kind) for s, kind in shapes],
        scratch_shapes=[pltpu.VMEM((m, 512), bf16)],
        compiler_params=pltpu.CompilerParams(vmem_limit_bytes=10 * 1024 * 1024),
        cost_estimate=SMALL,
    )(*lead, *in_vmem(operands))


def local(body, shapes, operands, place=None, price=SMALL, far=(), scratch=()):
    lead = [] if place is None else [place]
    return pl.pallas_call(
        body,
        in_specs=[SMEM] * len(lead)
        + [VMEM] * len(operands)
        + [pl.BlockSpec(memory_space=pltpu.HBM)] * len(far),
        out_specs=[VMEM] * len(shapes),
        out_shape=[jax.ShapeDtypeStruct(s, kind) for s, kind in shapes],
        scratch_shapes=list(scratch),
        compiler_params=pltpu.CompilerParams(vmem_limit_bytes=6 * 1024 * 1024),
        cost_estimate=price,
    )(*lead, *operands, *(pltpu.with_memory_space_constraint(a, pltpu.HBM) for a in far))


def half_kernel(place, gate, up, down, factor, ranks, sems):
    half = pl.ds(pl.multiple_of(place[3] * 32, 32), 32)
    copies = [
        pltpu.make_async_copy(r.at[half, :], ranks.at[k], sems.at[k])
        for k, r in enumerate((gate, up, down))
    ]
    for copy in copies:
        copy.start()
    for copy in copies:
        copy.wait()
    for i in range(6):
        col = slice(256 * i, 256 * i + 256)
        factor[:, col] = ranks[i // 2, (i % 2) * 16 : (i % 2) * 16 + 16, :]


def shape_kernel(place, own, other, factor, wide, message):
    c = place[3]
    wide[:, pl.ds(pl.multiple_of(c * QUARTER, QUARTER), QUARTER)] = own[...]
    wide[:, pl.ds(pl.multiple_of((1 - c) * QUARTER, QUARTER), QUARTER)] = other[...]
    rows = widen(wide[...])
    rows = jnp.concatenate([rows[:, :QUARTER], rows[:, QUARTER:]], axis=0)
    message[:, :QUARTER] = rows.astype(bf16)
    message[:, QUARTER:] = factor[...]


def pack_kernel(place, wide, z1, z2, message, far_message, out):
    zl = place[4]
    here = pl.ds(pl.multiple_of(zl * HALF, HALF), HALF)
    there = pl.ds(pl.multiple_of((1 - zl) * HALF, HALF), HALF)
    z3 = widen(far_message[:, :QUARTER])
    z3 = jnp.concatenate([z3[:8], z3[8:]], axis=1)
    pair = lambda a, b: jnp.concatenate([widen(a), widen(b)], 0).astype(bf16)
    out[:, here] = pair(wide[...], z2[...])
    out[:, there] = pair(z1[...], z3)
    for i in range(6):
        at, col = WIDTH + 512 * i, QUARTER + 256 * i
        out[:, at : at + 256] = message[:, col : col + 256]
        out[:, at + 256 : at + 512] = far_message[:, col : col + 256]


def unpack_kernel(own, got2, got1, got3, factor, packed):
    for k, g in enumerate((own, got1, got2, got3)):
        factor[16 * k : 16 * k + 16, :] = g[:, WIDTH:]
        packed[16 * k : 16 * k + 16, :] = g[...]


def part_kernel(*refs):
    at, out = 0, refs[-1]
    for r in refs[:-1]:
        out[at : at + r.shape[0], :] = r[:, : out.shape[1]]
        at += r.shape[0]


def touch_kernel(gate_w, up_w, down_w, out):
    out[...] = jnp.zeros_like(out)


def seconds_kernel(gate, up, down, out):
    out[...] = jnp.zeros_like(out)
    for k, r in enumerate((gate, up, down)):
        out[64 * k : 64 * k + 64, :UNITS] = r[...]


def stack_kernel(f0, packed3, packed1, f2, seconds, out):
    at = 0
    for r in (f0, packed1, f2, packed3):
        out[at : at + r.shape[0], :3072] = r[:, -3072:]
        at += r.shape[0]
    out[:, 3072:] = seconds[...]


def add_kernel(own, b1, b3, out):
    out[...] = own[...] + widen(b1[...]) + widen(b3[...])


def sum_kernel(own, b, keep, s1, s2, s3):
    for k, out in enumerate((keep, s1, s2, s3)):
        part = slice(16 * k, 16 * k + 16)
        out[...] = (own[part, :] + widen(b[part, :])).astype(out.dtype)


def split_kernel(place, own, b2, b1, b3, keep, s1, s2, s3):
    zl = place[4]
    here = pl.ds(pl.multiple_of(zl * HALF, HALF), HALF)
    there = pl.ds(pl.multiple_of((1 - zl) * HALF, HALF), HALF)
    for cols, near, far in ((here, keep, s2), (there, s1, s3)):
        total = own[:, cols]
        for b in (b1, b2, b3):
            total += widen(b[:, cols])
        near[...] = total[:8].astype(near.dtype)
        far[...] = total[8:].astype(far.dtype)


def last_kernel(place, own, b2, b1, b3, keep, give):
    c = place[3]
    for at, out in ((c, keep), (1 - c, give)):
        cols = pl.ds(pl.multiple_of(at * QUARTER, QUARTER), QUARTER)
        total = own[:, cols] + widen(b1[:, cols])
        total += widen(b2[:, cols]) + widen(b3[:, cols])
        out[...] = total.astype(bf16)


def shards(
    inputs,
    frozen_gate_weight,
    frozen_up_weight,
    frozen_down_weight,
    adapter_first_gate,
    adapter_second_gate,
    adapter_first_up,
    adapter_second_up,
    adapter_first_down,
    adapter_second_down,
):
    zh, y, x, zl, c = (lax.axis_index(a) for a in AXES)
    place = jnp.stack([zh, y, x, c, zl]).astype(jnp.int32)

    own = jnp.where(c == 0, inputs[0], inputs[1])
    other = send(jnp.where(c == 0, inputs[1], inputs[0]), CORE)
    (factor,) = local(
        half_kernel,
        [((16, 1536), bf16)],
        (),
        place,
        far=(adapter_first_gate, adapter_first_up, adapter_second_down),
        scratch=[pltpu.VMEM((3, 32, 256), bf16), pltpu.SemaphoreType.DMA((3,))],
    )
    wide, message = local(
        shape_kernel,
        [((8, HALF), bf16), ((16, QUARTER + 1536), bf16)],
        (own, other, factor),
        place,
    )

    z1, z2, z3 = (
        send(v, ALONG_Z[k]) for k, v in ((1, wide), (2, wide), (3, message))
    )
    gate2 = send(after(frozen_gate_weight, wide), CORE)
    (packed,) = local(
        pack_kernel, [((16, WIDTH + 3072), bf16)], (wide, z1, z2, message, z3), place
    )

    packed = after(packed, gate2)
    got = {k: send(packed, FIRST[k]) for k in (1, 2, 3)}
    seconds = (adapter_second_gate, adapter_second_up, adapter_first_down)
    (seconds,) = local(
        seconds_kernel, [((256, 256), bf16)], [a.T for a in after(seconds, packed)]
    )
    factor, packed = local(
        unpack_kernel,
        [((64, 3072), bf16), ((64, WIDTH + 3072), bf16)],
        (packed, got[2], got[1], got[3]),
    )

    factor, packed = after((factor, packed), seconds)
    far = send(factor, SECOND[2])
    packed1, packed3 = send(packed, SECOND[1]), send(packed, SECOND[3])
    frozen = (frozen_gate_weight, frozen_up_weight, frozen_down_weight)
    owned = after(frozen, packed)
    up2, down2 = send(owned[1], CORE), send(owned[2], CORE)
    (far,) = local(part_kernel, [((64, 3072), bf16)], (far,), price=price_of(11))
    (factor,) = local(
        stack_kernel,
        [((256, 3072 + 256), bf16)],
        (factor, packed3, packed1, far, seconds),
    )
    factor2 = send(factor, CORE)
    (rows1,) = local(part_kernel, [((64, WIDTH), bf16)], (packed1,))
    rows2 = send(rows1, SECOND[3])
    (touched,) = local(touch_kernel, [((8, 128), f32)], in_vmem(owned))

    weights = (owned[0], gate2, owned[1], up2)
    down_weights = (owned[2], down2)

    acc = project((packed3, packed1, packed), weights, price_of(CK), touched)
    part3, part1, first, second = down(
        first_down_kernel,
        128,
        [((64, WIDTH), bf16)] * 2 + [((128, WIDTH), bf16), ((64, WIDTH), bf16)],
        (packed3, packed1, acc, *down_weights, seconds, factor2, factor),
        place,
    )
    back1, back3 = send(part1, SECOND[1]), send(part3, SECOND[3])
    acc2 = project((after(rows2, part1),), (*weights, first), SMALL)
    (part2,) = down(
        last_down_kernel,
        64,
        [((64, WIDTH), bf16)],
        (acc2, *down_weights, seconds, factor2, second),
    )
    back2 = send(part2, SECOND[2])
    (total,) = down(
        own_down_kernel,
        64,
        [((64, WIDTH), f32)],
        (packed, after(acc, part2), *down_weights, seconds, factor2, first, second),
    )
    (total,) = local(
        add_kernel,
        [((64, WIDTH), f32)],
        (total, back1, back3),
        price=price_of(4.5),
    )
    small = [((16, WIDTH), f32)] + [((16, WIDTH), bf16)] * 3
    mine, *parts = local(sum_kernel, small, (total, back2))
    b1, b2, b3 = (send(p, FIRST[k]) for k, p in zip((1, 2, 3), parts, strict=True))
    small = [((8, HALF), f32)] + [((8, HALF), bf16)] * 3
    done, *parts = local(split_kernel, small, (mine, b2, b1, b3), place)
    b1, b2, b3 = (send(p, ALONG_Z[k]) for k, p in zip((1, 2, 3), parts, strict=True))
    small = [((8, QUARTER), bf16)] * 2
    keep, give = local(last_kernel, small, (done, b2, b1, b3), place)
    got = send(give, CORE)
    return jnp.where(c == 0, jnp.stack([keep, got]), jnp.stack([got, keep]))


def solution(mesh):
    fine = Mesh(mesh.devices.reshape(SIZES), AXES)
    learner, tensor = ("zh", "y", "x"), ("zl", "c")
    in_specs = (
        P(None, learner, tensor),
        P(AXES, None),
        P(AXES, None),
        P(AXES, None),
        P(None, learner),
        P(AXES, None),
        P(None, learner),
        P(AXES, None),
        P(AXES, None),
        P(None, learner),
    )
    return jax.shard_map(
        shards,
        mesh=fine,
        in_specs=in_specs,
        out_specs=P(None, learner, tensor),
        check_vma=False,
    )
```
